32 devices in a mesh: rec: 8 (over z, y), tile: 4 (over x, core).
Axes of the slice: x: 2, y: 2, z: 4, core: 2. Of those that a mesh axis runs over, the one named last changes fastest.
Arguments:
- prior_flux: bfloat16 [240, 128, 512], P(None, 'rec', 'tile'), may hold values from -6 to 6
- flux_scale: bfloat16 [240, 128, 512], P(None, 'rec', 'tile'), may hold values from 0.5 to 2
- control: float32 [240, 128, 512], P(None, 'rec', 'tile'), may hold values from -6 to 6
- footprint: bfloat16 [1024, 8, 24, 128], P(('rec', 'tile')), may hold values from 0 to 0.019897461
- slot_count: int32 [1024], P(('rec', 'tile')), may hold values from 0 to 8, as said below
- start_hour: int32 [1024, 8], P(('rec', 'tile')), may hold values from 0 to 216
- grid_row: int32 [1024, 8], P(('rec', 'tile')), may hold values from 0 to 15
- receptor_slot: int32 [1024, 8], P(('rec', 'tile')), may hold values from 0 to 63
- observed: float32 [512], P('rec'), may hold values from -32 to 32
- obs_error: float32 [512], P('rec'), may hold values from 0.1 to 0.4
Outputs:
- model_co2: float32 [512], P('rec')
- flux_gradient: float32 [240, 128, 512], P(None, 'rec', 'tile')
The draws below stay inside these ranges and needn't reach their ends.
Inputs may be any that keep to these rules, and one draw needn't show every extreme that they name: `slot_count`: A source device sends at most 8 blocks to one flux owner; some source reaches it, and in every draw one owner receives 8 blocks from every source.
All inputs are finite; a program needn't handle non-finite values.
Results may differ from the reference program's by a relative error of at most 0.0003.
Values may be sent and summed in bfloat16 or wider, within the bound.
No kernel may reach another device: no remote copies, remote signals or barrier semaphores. Data moves between devices by JAX's collectives and lax.ppermute only.
A program may use at most 128 MiB of HBM per device.

```python
import math
import jax
import jax.numpy as jnp
from jax import lax

HOURS = 240
CY = 16
CX = 128
BH = 24
CAP = 8
REC_DEV = 64
RAD = 4
TAPS = 12
GY = 128
GX = 512
RECEPTORS = 512
N_REC = 8
N_TILE = 4
DEVICES = 32


def draw_slot_count(key, part):
    key = jax.random.fold_in(key, 1)
    key_ceiling, key_counts, key_target = jax.random.split(key, 3)
    ceiling = jax.random.randint(key_ceiling, (DEVICES,), 1, CAP + 1)
    lower = ceiling // 2
    raw_counts = jax.random.randint(key_counts, (DEVICES, DEVICES), 0, 1 << 20)
    counts = lower[None, :] + raw_counts % (ceiling - lower + 1)[None, :]
    target = jax.random.randint(key_target, (), 0, DEVICES)
    counts = jnp.where(jnp.arange(DEVICES)[None, :] == target, CAP, counts)
    return counts.reshape(-1).astype(jnp.int32)


def touch_ends(drawn, stream_key, least, high):
    spot = [jax.random.randint(jax.random.fold_in(stream_key, axis), (), 0, length) for axis, length in enumerate(drawn.shape)]
    main_axis = drawn.shape.index(max(drawn.shape))
    beside = spot[:main_axis] + [(spot[main_axis] + 1) % drawn.shape[main_axis]] + spot[main_axis + 1:]
    return drawn.at[tuple(spot)].set(least).at[tuple(beside)].set(high)


def steps_of(rng, dims, cuts, smallest, high):
    def one(dim, shards_of):
        heights = jax.random.uniform(jax.random.fold_in(jax.random.fold_in(rng, 6), dim), (shards_of,), jnp.float32, smallest / len(cuts), high / len(cuts))
        return jnp.repeat(jnp.exp(heights), dims[dim] // shards_of).reshape((-1,) + (1,) * (len(dims) - dim - 1))

    loudness = one(*cuts[0])
    for cut in cuts[1:]:
        loudness = loudness * one(*cut)
    return loudness


def scatter_about(rng, dims, deviation, limit, cuts=(), dtype=jnp.bfloat16):
    values = jax.random.normal(rng, dims, jnp.float32) * deviation
    if len(cuts) > 0:
        values = steps_of(rng, dims, cuts, -0.22, 0.18) * values
    return jnp.clip(values, min=-limit, max=limit).astype(dtype)


def setup_inputs(seed: int = 0) -> dict:
    arg_keys = jax.random.split(jax.random.key(seed), 11)
    return {
        "prior_flux": scatter_about(arg_keys[0], (HOURS, GY, GX), 1.0, 6.0, ((1, 8), (2, 4))),
        "flux_scale": jnp.clip(jnp.exp(math.log(2.0) - 1.3862944 * jax.random.uniform(arg_keys[1], (HOURS, GY, GX), jnp.float32) ** steps_of(arg_keys[1], (HOURS, GY, GX), ((1, 8), (2, 4)), -0.2, 0.2)), 0.5, 2.0).astype(jnp.bfloat16),
        "control": scatter_about(arg_keys[2], (HOURS, GY, GX), 1.0, 6.0, ((1, 8), (2, 4)), jnp.float32),
        "footprint": jnp.clip(0.019897461 * jax.random.uniform(arg_keys[3], (DEVICES * DEVICES, CAP, BH, CX), jnp.float32) ** steps_of(arg_keys[3], (DEVICES * DEVICES, CAP, BH, CX), ((0, 32),), -0.2, 0.2), 0.0, 0.019897461).astype(jnp.bfloat16),
        "slot_count": draw_slot_count(jax.random.fold_in(arg_keys[10], 71), 0),
        "start_hour": touch_ends(jax.random.randint(arg_keys[5], (DEVICES * DEVICES, CAP), 0, HOURS - BH + 1), jax.random.fold_in(arg_keys[5], 1), 0, HOURS - BH).astype(jnp.int32),
        "grid_row": touch_ends(jax.random.randint(arg_keys[6], (DEVICES * DEVICES, CAP), 0, CY), jax.random.fold_in(arg_keys[6], 1), 0, CY - 1).astype(jnp.int32),
        "receptor_slot": touch_ends(jax.random.randint(arg_keys[7], (DEVICES * DEVICES, CAP), 0, REC_DEV), jax.random.fold_in(arg_keys[7], 1), 0, REC_DEV - 1).astype(jnp.int32),
        "observed": scatter_about(arg_keys[8], (RECEPTORS,), 5.0, 32.0, ((0, 8),), jnp.float32),
        "obs_error": jnp.clip(jnp.exp(math.log(0.4) - 1.3862944 * jax.random.uniform(arg_keys[9], (RECEPTORS,), jnp.float32) ** steps_of(arg_keys[9], (RECEPTORS,), ((0, 8),), -0.2, 0.2)), 0.1, 0.4),
    }


def space_kernel():
    offsets = jnp.arange(-RAD, RAD + 1).astype(jnp.float32)
    values = jnp.exp(-2.0 * offsets * offsets / (RAD * RAD))
    return values / jnp.sqrt(jnp.sum(values * values))

def time_kernel():
    offsets = jnp.arange(-TAPS, TAPS + 1).astype(jnp.float32)
    values = jnp.exp(-2.0 * jnp.abs(offsets) / TAPS)
    return values / jnp.sqrt(jnp.sum(values * values))

def correlate(field):
    spatial = space_kernel()
    temporal = time_kernel()
    padded = jnp.pad(field, ((0, 0), (RAD, RAD), (RAD, RAD)))
    height = field.shape[1]
    breadth = field.shape[2]
    by_rows = spatial[0] * padded[:, 0:height, :]
    for offset in range(1, 2 * RAD + 1):
        by_rows = by_rows + spatial[offset] * padded[:, offset:offset + height, :]
    by_cols = spatial[0] * by_rows[:, :, 0:breadth]
    for offset in range(1, 2 * RAD + 1):
        by_cols = by_cols + spatial[offset] * by_rows[:, :, offset:offset + breadth]
    hours_pad = jnp.pad(by_cols, ((TAPS, TAPS), (0, 0), (0, 0)))
    result = temporal[0] * hours_pad[0:HOURS]
    for offset in range(1, 2 * TAPS + 1):
        result = result + temporal[offset] * hours_pad[offset:offset + HOURS]
    return result

def reference(prior_flux, flux_scale, control, footprint, slot_count, start_hour, grid_row, receptor_slot, observed, obs_error):
    n_dev = N_REC * N_TILE
    grid_rows = CY * N_REC
    grid_cols = CX * N_TILE
    flux_field = prior_flux.astype(jnp.float32) + flux_scale.astype(jnp.float32) * correlate(control)
    flux_rows = flux_field.reshape(HOURS * grid_rows, grid_cols)
    blocks = footprint.reshape(n_dev, n_dev, CAP, BH, CX)
    counts = slot_count.reshape(n_dev, n_dev)
    starts = start_hour.reshape(n_dev, n_dev, CAP)
    row_ids = grid_row.reshape(n_dev, n_dev, CAP)
    slots = receptor_slot.reshape(n_dev, n_dev, CAP)
    owners = jnp.arange(n_dev).astype(jnp.int32)
    owner_rec = owners // N_TILE
    owner_tile = owners % N_TILE
    hour_steps = jnp.arange(BH).astype(jnp.int32)
    columns = owner_tile[:, None] * CX + jnp.arange(CX).astype(jnp.int32)[None, :]
    sources = jnp.arange(n_dev).astype(jnp.int32)

    def locate(start_set, row_set):
        return ((start_set[:, :, None] + hour_steps[None, None, :]) * grid_rows + (owner_rec[:, None, None] * CY + row_set[:, :, None])).astype(jnp.int32)

    def forward(carry, items):
        block_set, count_set, start_set, row_set, slot_set, source = items
        flat_index = locate(start_set, row_set)
        windows = flux_rows[flat_index[..., None], columns[:, None, None, :]]
        valid = jnp.arange(CAP)[None, :] < count_set[:, None]
        block_value = jnp.where(valid, lax.optimization_barrier(jnp.sum(block_set.astype(jnp.float32) * windows, axis=(2, 3))), 0.0)
        receptor = (source // N_TILE * REC_DEV + slot_set).astype(jnp.int32)
        return (carry.at[receptor].add(block_value), None)
    model_co2, _ = lax.scan(forward, jnp.zeros((REC_DEV * N_REC,), jnp.float32), (blocks, counts, starts, row_ids, slots, sources))
    weight = (model_co2 - observed) / (obs_error * obs_error)

    def adjoint(carry, items):
        block_set, count_set, start_set, row_set, slot_set, source = items
        flat_index = locate(start_set, row_set)
        valid = jnp.arange(CAP)[None, :] < count_set[:, None]
        receptor = (source // N_TILE * REC_DEV + slot_set).astype(jnp.int32)
        block_weight = jnp.where(valid, weight[receptor], 0.0)
        contrib = block_set.astype(jnp.float32) * block_weight[:, :, None, None]
        return (carry.at[flat_index[..., None], columns[:, None, None, :]].add(contrib), None)
    adjoint_rows, _ = lax.scan(adjoint, jnp.zeros((HOURS * grid_rows, grid_cols), jnp.float32), (blocks, counts, starts, row_ids, slots, sources))
    adjoint_field = adjoint_rows.reshape(HOURS, grid_rows, grid_cols)
    flux_gradient = correlate(flux_scale.astype(jnp.float32) * adjoint_field)
    return (model_co2, flux_gradient)
```

```python
import numpy as np
import jax
import jax.numpy as jnp
from jax import lax
from jax.experimental import pallas as pl
from jax.experimental.pallas import tpu as pltpu
from jax.sharding import PartitionSpec as P

RAD = 4
TAPS = 12
AXES = ("rec", "tile")
LANES = 128
SUB = 8
VMEM_LIMIT = 56 * 1024 * 1024
F32 = jnp.float32
BF16 = jnp.bfloat16


def space_taps():
    offsets = np.arange(-RAD, RAD + 1).astype(np.float64)
    values = np.exp(-2.0 * offsets * offsets / (RAD * RAD))
    return values / np.sqrt(np.sum(values * values))


def time_taps():
    offsets = np.arange(-TAPS, TAPS + 1).astype(np.float64)
    values = np.exp(-2.0 * np.abs(offsets) / TAPS)
    return values / np.sqrt(np.sum(values * values))


def banded(distance, taps, reach):
    inside = np.abs(distance) <= reach
    return np.where(inside, taps[np.clip(distance, -reach, reach) + reach], 0.0)


def two_parts(matrix):
    high = matrix.astype(np.float32).astype(jnp.bfloat16)
    low = (matrix - high.astype(np.float64)).astype(np.float32).astype(jnp.bfloat16)
    return high, low


def constants(hours, rows, cols):
    space = space_taps()
    hour = np.arange(hours)
    time_high, time_low = two_parts(banded(hour[:, None] - hour[None, :], time_taps(), TAPS))
    col = np.arange(cols)
    col_high, col_low = two_parts(banded(col[:, None] - col[None, :], space, RAD))
    halo_col = np.concatenate([np.arange(-RAD, 0), np.arange(cols, cols + RAD)])
    edge = banded(halo_col[:, None] - col[None, :], space, RAD)
    edge_high, edge_low = two_parts(np.tile(edge, (rows, 1)))
    row_of, halo_of = [], []
    for side in range(2):
        for row in range(rows):
            row_of += [row] * RAD
            halo_of += [side * RAD + j for j in range(RAD)]
    for row_side in range(2):
        for side in range(2):
            for row in range(RAD):
                row_of += [row - RAD if row_side == 0 else rows + row] * RAD
                halo_of += [side * RAD + j for j in range(RAD)]
    row_of, halo_of = np.array(row_of), np.array(halo_of)
    target = np.arange(rows * 2 * RAD)
    gather = banded(row_of[:, None] - (target // (2 * RAD))[None, :], space, RAD)
    gather = np.where(halo_of[:, None] == (target % (2 * RAD))[None, :], gather, 0.0)
    return {
        "time": (time_high, time_low),
        "col": (col_high, col_low),
        "edge": (edge_high, edge_low),
        "gather": gather.astype(np.float32),
    }


def split(value):
    high = value.astype(BF16)
    low = (value - high.astype(F32)).astype(BF16)
    return high, low


def dot(a, b):
    return jnp.dot(a, b, preferred_element_type=F32)


def pack_strips(row_value, parity, rows, strips):
    cols = row_value(0).shape[1]
    lane = lax.broadcasted_iota(jnp.int32, (2 * RAD, cols), 1)
    which = lax.broadcasted_iota(jnp.int32, (2 * RAD, cols), 0)
    first = which < RAD
    j = jnp.where(first, which, which - RAD)
    high_end = jnp.logical_xor(first, parity == 1)
    pick = jnp.where(lane == jnp.where(high_end, cols - RAD + j, j), 1.0, 0.0).astype(BF16)
    pick = jnp.concatenate([pick, pick], axis=1)
    for row in range(rows):
        high, low = split(row_value(row))
        both = jnp.concatenate([high, low], axis=1)
        strips[row] = lax.dot_general(
            pick, both, (((1,), (1,)), ((), ())), preferred_element_type=F32
        )


def write_halos(par_ref, row_value, rows, strips, rows_e, rows_o, cols_e, cols_o, corners):
    rec_parity, tile_parity = par_ref[0], par_ref[1]
    pack_strips(row_value, tile_parity, rows, strips)
    for row in range(rows):
        cols_e[row] = strips[row, 0:RAD, :]
        cols_o[row] = strips[row, RAD : 2 * RAD, :]
    top = rows - RAD

    def send(even_ref, odd_ref, first, last):
        for row in range(RAD):
            rows_e[row] = row_value(first + row)
            rows_o[row] = row_value(last + row)
            for which, source in ((0, first), (1, last)):
                corners[2 * which][row] = strips[source + row, 0:RAD, :]
                corners[2 * which + 1][row] = strips[source + row, RAD : 2 * RAD, :]

    @pl.when(rec_parity == 0)
    def _():
        send(rows_e, rows_o, top, 0)

    @pl.when(rec_parity == 1)
    def _():
        send(rows_e, rows_o, 0, top)


def pack_kernel(par_ref, field_ref, rows_e, rows_o, cols_e, cols_o, c0, c1, c2, c3, strips):
    rows = field_ref.shape[1]
    write_halos(
        par_ref, lambda r: field_ref[:, r, :], rows, strips, rows_e, rows_o, cols_e, cols_o, (c0, c1, c2, c3)
    )


def halo_shapes(hours, rows, cols):
    block = jax.ShapeDtypeStruct((RAD, hours, cols), F32)
    strip = jax.ShapeDtypeStruct((rows, RAD, hours), F32)
    corner = jax.ShapeDtypeStruct((RAD, RAD, hours), F32)
    return [block, block, strip, strip, corner, corner, corner, corner]


def column_halo(par_ref, cols_e, cols_o, corners, gather_ref, strips):
    rec_parity, tile_parity = par_ref[0], par_ref[1]
    rows, _, hours = cols_e.shape
    strips[...] = jnp.zeros_like(strips)
    for row in range(rows):
        even, odd = cols_e[row], cols_o[row]
        strips[row * RAD : (row + 1) * RAD, 0:hours] = jnp.where(tile_parity == 0, odd, even)
        base = (rows + row) * RAD
        strips[base : base + RAD, 0:hours] = jnp.where(tile_parity == 0, even, odd)
    for row in range(RAD):
        by_tile = []
        for a in range(2):
            even, odd = corners[2 * a][row], corners[2 * a + 1][row]
            by_tile.append(
                (jnp.where(tile_parity == 0, odd, even), jnp.where(tile_parity == 0, even, odd))
            )
        for side in range(2):
            prev_rec = jnp.where(rec_parity == 0, by_tile[1][side], by_tile[0][side])
            next_rec = jnp.where(rec_parity == 0, by_tile[0][side], by_tile[1][side])
            base = (2 * rows + side * RAD + row) * RAD
            strips[base : base + RAD, 0:hours] = prev_rec
            base = (2 * rows + (2 + side) * RAD + row) * RAD
            strips[base : base + RAD, 0:hours] = next_rec
    turned = jnp.transpose(strips[...])[0:hours, 0 : gather_ref.shape[0]]
    return jnp.dot(turned, gather_ref[...], precision=lax.Precision.HIGHEST, preferred_element_type=F32)


def edge_weights(row, edge_ref):
    group = lax.broadcasted_iota(jnp.int32, edge_ref.shape, 0) // (2 * RAD)
    return jnp.where(group == row, edge_ref[...].astype(F32), 0.0).astype(BF16)


def column_sums(value, halo_parts, row, col_high, col_low, edge_high, edge_low):
    high, low = split(value)
    out = dot(high, col_high) + dot(low, col_high) + dot(high, col_low)
    if halo_parts is not None:
        halo_high, halo_low = halo_parts
        weights_high, weights_low = edge_weights(row, edge_high), edge_weights(row, edge_low)
        out = out + (dot(halo_high, weights_high) + dot(halo_low, weights_high) + dot(halo_high, weights_low))
    return out


def time_sums(value, time_high, time_low):
    high, low = split(value)
    return dot(time_high, high) + dot(time_high, low) + dot(time_low, high)


def row_sums(get, row, low, high, taps):
    total = None
    for distance in range(RAD + 1):
        here = [get(r) for r in sorted({row - distance, row + distance}) if low <= r < high]
        if not here:
            continue
        part = here[0] if len(here) == 1 else here[0] + here[1]
        part = float(taps[RAD + distance]) * part
        total = part if total is None else total + part
    return total


def flux_kernel(
    par_ref, control_ref, prior_ref, scale_ref, rows_e, rows_o, cols_e, cols_o, c0, c1, c2, c3,
    gather_ref, time_high, time_low, col_high, col_low, edge_high, edge_low,
    flux_ref, scale_out, padded, strips, wide,
):
    hours, rows, cols = control_ref.shape
    taps = space_taps()
    rec_parity = par_ref[0]
    for row in range(RAD):
        even, odd = rows_e[row], rows_o[row]
        padded[row] = jnp.where(rec_parity == 0, odd, even)
        padded[RAD + rows + row] = jnp.where(rec_parity == 0, even, odd)
    for row in range(rows):
        padded[RAD + row] = control_ref[:, row, :]
    halo = split(column_halo(par_ref, cols_e, cols_o, (c0, c1, c2, c3), gather_ref, strips))
    wide[...] = scale_ref[...].astype(F32)
    for row in range(rows):
        scale_out[row] = wide[:, row, :].astype(BF16)
    wide[...] = prior_ref[...].astype(F32)
    for row in range(0, rows, 2):
        pair = []
        for r in (row, row + 1):
            summed = row_sums(lambda i: padded[i], RAD + r, 0, rows + 2 * RAD, taps)
            pair.append(
                column_sums(summed, halo, r, col_high[...], col_low[...], edge_high, edge_low)
            )
        both = time_sums(jnp.concatenate(pair, axis=1), time_high[...], time_low[...])
        for k, r in enumerate((row, row + 1)):
            part = both[:, k * cols : (k + 1) * cols]
            flux_ref[r] = wide[:, r, :] + scale_out[r].astype(F32) * part


def forward_kernel(me_ref, offset_ref, receptor_ref, foot_ref, flux_ref, own_ref, out_ref, sums, *, shift):
    sources, slots, heights, cols = foot_ref.shape
    me = me_ref[0]

    def body(j, carry):
        source = jnp.bitwise_xor(me, j)
        parts = []
        for c in range(slots):
            offset = offset_ref[j * slots + c]
            row = lax.shift_right_logical(offset, shift)
            start = jnp.bitwise_and(offset, (1 << shift) - 1)
            window = flux_ref[row, pl.ds(start, heights), :]
            product = foot_ref[source, c].astype(F32) * window
            parts.append(jnp.sum(product, axis=0, keepdims=True))
        sums[pl.ds(pl.multiple_of(j * slots, slots), slots), :] = jnp.concatenate(parts, axis=0)
        return carry

    lax.fori_loop(0, sources, body, 0)
    value = jnp.sum(sums[...], axis=1, keepdims=True)
    receptor = receptor_ref[...]
    lane = lax.broadcasted_iota(jnp.int32, (sources * slots, LANES), 1)
    groups = out_ref.shape[1] - 1
    for q in range(groups):
        hit = receptor == lane + q * LANES
        total = jnp.sum(jnp.where(hit, value, 0.0), axis=0, keepdims=True)
        out_ref[:, q : q + 1, :] = jnp.broadcast_to(total[None], (sources, 1, LANES))
    out_ref[:, groups : groups + 1, :] = jnp.broadcast_to(own_ref[...][None], (sources, 1, LANES))


def adjoint_kernel(
    me_ref, par_ref, offset_ref, receptor_ref, got_ref, foot_ref, scale_ref,
    model_ref, field_ref, rows_e, rows_o, cols_e, cols_o, c0, c1, c2, c3,
    weight_vmem, weight_smem, strips, sem, *, shift, tiles, per,
):
    sources, slots, heights, cols = foot_ref.shape
    groups = model_ref.shape[0]
    rows = field_ref.shape[0]
    me = me_ref[0]
    model = jnp.sum(got_ref[:, 0:groups, :], axis=0)
    model_ref[...] = model
    packed = LANES // per
    lane = lax.broadcasted_iota(jnp.int32, (1, LANES), 1)
    weight_vmem[...] = jnp.zeros_like(weight_vmem)
    for q in range(groups):
        observed, error = jnp.zeros((1, LANES), F32), jnp.ones((1, LANES), F32)
        for k in range(packed):
            line = got_ref[(q * packed + k) * tiles, groups : groups + 1, :]
            here = (lane >= k * per) & (lane < (k + 1) * per)
            observed = jnp.where(here, line if k == 0 else pltpu.roll(line, k * per, 1), observed)
            turn = (k * per - per) % LANES
            error = jnp.where(here, line if turn == 0 else pltpu.roll(line, turn, 1), error)
        weight_vmem[q : q + 1, :] = (model[q : q + 1, :] - observed) / (error * error)
    copy = pltpu.make_async_copy(weight_vmem, weight_smem, sem)
    copy.start()
    field_ref[...] = jnp.zeros_like(field_ref)
    copy.wait()

    def body(j, carry):
        source = jnp.bitwise_xor(me, j)
        for c in range(slots):
            offset = offset_ref[j * slots + c]
            receptor = receptor_ref[j * slots + c]
            row = lax.shift_right_logical(offset, shift)
            start = jnp.bitwise_and(offset, (1 << shift) - 1)
            weight = weight_smem[lax.shift_right_logical(receptor, 7), jnp.bitwise_and(receptor, LANES - 1)]
            field_ref[row, pl.ds(start, heights), :] += foot_ref[source, c].astype(F32) * weight
        return carry

    lax.fori_loop(0, sources, body, 0)
    for row in range(rows):
        field_ref[row] = field_ref[row] * scale_ref[row].astype(F32)
    write_halos(
        par_ref, lambda r: field_ref[r], rows, strips, rows_e, rows_o, cols_e, cols_o, (c0, c1, c2, c3)
    )


def local_kernel(
    par_ref, field_ref, cols_e, cols_o, c0, c1, c2, c3,
    gather_ref, time_high, time_low, col_high, col_low, edge_high, edge_low, out_ref, strips,
):
    rows, hours, cols = field_ref.shape
    taps = space_taps()
    halo = split(column_halo(par_ref, cols_e, cols_o, (c0, c1, c2, c3), gather_ref, strips))
    for row in range(0, rows, 2):
        pair = []
        for r in (row, row + 1):
            summed = row_sums(lambda i: field_ref[i], r, 0, rows, taps)
            pair.append(
                column_sums(summed, halo, r, col_high[...], col_low[...], edge_high, edge_low)
            )
        both = time_sums(jnp.concatenate(pair, axis=1), time_high[...], time_low[...])
        for k, r in enumerate((row, row + 1)):
            out_ref[r] = both[:, k * cols : (k + 1) * cols]


def finish_kernel(
    par_ref, local_ref, rows_e, rows_o, time_high, time_low, col_high, col_low, out_ref, halo,
):
    rows, hours, cols = local_ref.shape
    taps = space_taps()
    rec_parity = par_ref[0]
    for row in range(RAD):
        even, odd = rows_e[row], rows_o[row]
        halo[row] = jnp.where(rec_parity == 0, odd, even)
        halo[RAD + row] = jnp.where(rec_parity == 0, even, odd)
    edge = list(range(RAD)) + list(range(rows - RAD, rows))
    for row in range(RAD, rows - RAD):
        out_ref[:, row, :] = local_ref[row]
    for first in range(0, 2 * RAD, 2):
        pair = []
        for r in edge[first : first + 2]:
            if r < RAD:
                summed = row_sums(lambda i: halo[i + RAD], r, -RAD, 0, taps)
            else:
                summed = row_sums(lambda i: halo[RAD + i - rows], r, rows, rows + RAD, taps)
            pair.append(column_sums(summed, None, r, col_high[...], col_low[...], None, None))
        both = time_sums(jnp.concatenate(pair, axis=1), time_high[...], time_low[...])
        for k, r in enumerate(edge[first : first + 2]):
            out_ref[:, r, :] = local_ref[r] + both[:, k * cols : (k + 1) * cols]


def swap_pairs(count, odd):
    pairs = []
    for i in range(1 if odd else 0, count - 1, 2):
        pairs += [(i, i + 1), (i + 1, i)]
    return pairs


def swap_halos(parts, n_rec, n_tile):
    rows_e, rows_o, cols_e, cols_o, c0, c1, c2, c3 = parts
    out = [
        lax.ppermute(rows_e, "rec", swap_pairs(n_rec, False)),
        lax.ppermute(rows_o, "rec", swap_pairs(n_rec, True)),
        lax.ppermute(cols_e, "tile", swap_pairs(n_tile, False)),
        lax.ppermute(cols_o, "tile", swap_pairs(n_tile, True)),
    ]
    corner = (c0, c1, c2, c3)
    for a in range(2):
        for b in range(2):
            pairs = [
                (r0 * n_tile + t0, r1 * n_tile + t1)
                for r0, r1 in swap_pairs(n_rec, a == 1)
                for t0, t1 in swap_pairs(n_tile, b == 1)
            ]
            out.append(lax.ppermute(corner[2 * a + b], AXES, pairs))
    return out


def call(kernel, out_shape, in_specs, scratch, name):
    return pl.pallas_call(
        kernel,
        out_shape=out_shape,
        in_specs=in_specs,
        out_specs=jax.tree.map(lambda _: VM, out_shape),
        scratch_shapes=scratch,
        compiler_params=pltpu.CompilerParams(vmem_limit_bytes=VMEM_LIMIT),
        name=name,
    )


SM = pl.BlockSpec(memory_space=pltpu.SMEM)
VM = pl.BlockSpec(memory_space=pltpu.VMEM)


def per_device(
    prior_flux,
    flux_scale,
    control,
    footprint,
    slot_count,
    start_hour,
    grid_row,
    receptor_slot,
    observed,
    obs_error,
):
    hours, rows, cols = control.shape
    n_rec, n_tile = lax.axis_size("rec"), lax.axis_size("tile")
    devices = n_rec * n_tile
    slots = footprint.shape[1]
    per = observed.shape[0]
    receptors = per * n_rec
    groups = receptors // LANES
    shift = (hours - 1).bit_length()
    rec, tile = lax.axis_index("rec"), lax.axis_index("tile")
    me = (rec * n_tile + tile).astype(jnp.int32)
    me_arr = me[None]
    par = jnp.stack([rec % 2, tile % 2]).astype(jnp.int32)
    const = constants(hours, rows, cols)
    time_parts = [jnp.asarray(c) for c in const["time"]]
    col_parts = [jnp.asarray(c) for c in const["col"]]
    edge_parts = [jnp.asarray(c) for c in const["edge"]]
    gather = jnp.asarray(const["gather"])
    n_strips = gather.shape[0]
    strip_scratch = pltpu.VMEM((rows, 2 * RAD, hours), F32)
    turn_scratch = pltpu.VMEM((-(-n_strips // LANES) * LANES, -(-hours // LANES) * LANES), F32)

    foot = lax.all_to_all(footprint, AXES, split_axis=0, concat_axis=0, tiled=True)

    halos = call(
        pack_kernel, halo_shapes(hours, rows, cols), [SM, VM], [strip_scratch], "pack_control"
    )(par, control)
    got = swap_halos(halos, n_rec, n_tile)

    valid = jnp.arange(slots)[None, :] < slot_count[:, None]
    receptor = jnp.where(valid, rec * per + receptor_slot, receptors).astype(jnp.int32)
    offset = (grid_row << shift) + start_hour
    info = jnp.concatenate([offset, receptor], axis=1)[None]
    step = 1
    while step < devices:
        other = lax.ppermute(info, AXES, [(i, i ^ step) for i in range(devices)])
        info = jnp.concatenate([info, other], axis=0)
        step *= 2
    info = lax.dynamic_index_in_dim(info, me, axis=1, keepdims=False)
    offset = info[:, :slots].reshape(-1)
    receptor = info[:, slots:].reshape(-1)

    flux, scale = call(
        flux_kernel,
        [jax.ShapeDtypeStruct((rows, hours, cols), F32), jax.ShapeDtypeStruct((rows, hours, cols), BF16)],
        [SM] + [VM] * 18,
        [pltpu.VMEM((rows + 2 * RAD, hours, cols), F32), turn_scratch, pltpu.VMEM((hours, rows, cols), F32)],
        "flux_field",
    )(par, control, prior_flux, flux_scale, *got, gather, *time_parts, *col_parts, *edge_parts)

    own = jnp.concatenate(
        [observed, obs_error, jnp.zeros((LANES - 2 * per,), F32)]
    )[None]

    def forward(*args):
        return forward_kernel(*args, shift=shift)

    partial = call(
        forward,
        jax.ShapeDtypeStruct((devices, groups + 1, LANES), F32),
        [SM, SM, VM, VM, VM, VM],
        [pltpu.VMEM((devices * slots, LANES), F32)],
        "block_values",
    )(me_arr, offset, receptor[:, None], foot, flux, own)
    everyone = lax.all_to_all(partial, AXES, split_axis=0, concat_axis=0, tiled=True)

    def adjoint(*args):
        return adjoint_kernel(*args, shift=shift, tiles=n_tile, per=per)

    weight_rows = -(-(groups + 1) // SUB) * SUB
    model, field, *halos = call(
        adjoint,
        [jax.ShapeDtypeStruct((groups, LANES), F32), jax.ShapeDtypeStruct((rows, hours, cols), F32)]
        + halo_shapes(hours, rows, cols),
        [SM, SM, SM, SM, VM, VM, VM],
        [
            pltpu.VMEM((weight_rows, LANES), F32),
            pltpu.SMEM((weight_rows, LANES), F32),
            strip_scratch,
            pltpu.SemaphoreType.DMA,
        ],
        "adjoint_field",
    )(me_arr, par, offset, receptor, everyone, foot, scale)
    got = swap_halos(halos, n_rec, n_tile)
    model_co2 = lax.dynamic_slice_in_dim(model.reshape(-1), rec * per, per)

    local = call(
        local_kernel,
        jax.ShapeDtypeStruct((rows, hours, cols), F32),
        [SM] + [VM] * 14,
        [turn_scratch],
        "correlate_local",
    )(par, field, *got[2:], gather, *time_parts, *col_parts, *edge_parts)
    gradient = call(
        finish_kernel,
        jax.ShapeDtypeStruct((hours, rows, cols), F32),
        [SM] + [VM] * 7,
        [pltpu.VMEM((2 * RAD, hours, cols), F32)],
        "correlate_edges",
    )(par, local, got[0], got[1], *time_parts, *col_parts)
    return (model_co2, gradient)


def solution(mesh):
    return jax.shard_map(
        per_device,
        mesh=mesh,
        in_specs=(
            P(None, "rec", "tile"),
            P(None, "rec", "tile"),
            P(None, "rec", "tile"),
            P(("rec", "tile"), None, None, None),
            P(("rec", "tile")),
            P(("rec", "tile"), None),
            P(("rec", "tile"), None),
            P(("rec", "tile"), None),
            P("rec"),
            P("rec"),
        ),
        out_specs=(P("rec"), P(None, "rec", "tile")),
        check_vma=False,
    )
```

```python
import numpy as np
import jax
import jax.numpy as jnp
from jax import lax
from jax.experimental import pallas as pl
from jax.experimental.pallas import tpu as pltpu
from jax.sharding import PartitionSpec as P

RAD = 4
TAPS = 12
AXES = ("rec", "tile")
LANES = 128
SUB = 8
FOOT_MAX = 0.02
SCALE_MAX = 2.0
HALF_TOP = 32768.0
F16 = jnp.float16
VMEM_LIMIT = 12 * 1024 * 1024
F32 = jnp.float32
BF16 = jnp.bfloat16


def space_taps():
    offsets = np.arange(-RAD, RAD + 1).astype(np.float64)
    values = np.exp(-2.0 * offsets * offsets / (RAD * RAD))
    return values / np.sqrt(np.sum(values * values))


def time_taps():
    offsets = np.arange(-TAPS, TAPS + 1).astype(np.float64)
    values = np.exp(-2.0 * np.abs(offsets) / TAPS)
    return values / np.sqrt(np.sum(values * values))


def banded(distance, taps, reach):
    inside = np.abs(distance) <= reach
    return np.where(inside, taps[np.clip(distance, -reach, reach) + reach], 0.0)


def two_parts(matrix):
    high = matrix.astype(np.float32).astype(jnp.bfloat16)
    low = (matrix - high.astype(np.float64)).astype(np.float32).astype(jnp.bfloat16)
    return high, low


def constants(hours, rows, cols):
    space = space_taps()
    hour = np.arange(hours)
    time_high, time_low = two_parts(banded(hour[:, None] - hour[None, :], time_taps(), TAPS))
    col = np.arange(cols)
    col_high, col_low = two_parts(banded(col[:, None] - col[None, :], space, RAD))
    col_both = np.block([[col_high, col_low], [col_high, np.zeros_like(col_high)]])
    halo_col = np.concatenate([np.arange(-RAD, 0), np.arange(cols, cols + RAD)])
    edge = banded(halo_col[:, None] - col[None, :], space, RAD)

    def strips(row_of, halo_of, targets):
        by_row = banded(np.array(row_of)[:, None] - np.array(targets)[None, :], space, RAD)
        both = by_row[:, :, None] * edge[np.array(halo_of)][:, None, :]
        return two_parts(both.reshape(len(row_of), -1))

    own = [(row, side * RAD + j) for side in range(2) for row in range(rows) for j in range(RAD)]
    corner = [
        (row, side * RAD + j)
        for first in (-RAD, rows)
        for side in range(2)
        for row in range(first, first + RAD)
        for j in range(RAD)
    ]
    corner += [(-100, 0)] * (LANES - len(corner))
    edge_rows = list(range(RAD)) + list(range(rows - RAD, rows))
    own_parts = strips(*zip(*own), np.arange(rows))
    corner_parts = strips(*zip(*corner), np.array(edge_rows))
    return (time_high, time_low, col_both), own_parts, corner_parts


def split(value):
    high = value.astype(BF16)
    low = (value - high.astype(F32)).astype(BF16)
    return high, low


def dot(a, b):
    return jnp.dot(a, b, preferred_element_type=F32)


def lane_ids(shape):
    return lax.broadcasted_iota(jnp.int32, shape, 1)


def choose(flag, yes, no):
    return jnp.where(flag, yes, no)


def pack_strips(row_value, parity, rows):
    cols = row_value(0).shape[1]
    half = rows * RAD
    source = lax.broadcasted_iota(jnp.int32, (cols, 2 * half), 0)
    lane = lax.broadcasted_iota(jnp.int32, (cols, 2 * half), 1)
    first = lane < half
    j = lane & (RAD - 1)
    high_end = jnp.logical_xor(first, parity == 1)
    wanted = jnp.where(high_end, cols - RAD + j, j)
    lane_row = jnp.where(first, lane, lane - half) // RAD
    total = None
    for row in range(rows):
        high, low = split(row_value(row))
        pick = jnp.where((source == wanted) & (lane_row == row), 1.0, 0.0).astype(BF16)
        part = dot(jnp.concatenate([high, low], axis=1), jnp.concatenate([pick, pick], axis=0))
        total = part if total is None else total + part
    return total


def fold_hours(value, hours, strip_e, strip_o):
    fold = strip_e.shape[0]
    half = LANES // 2
    early = value[0:fold]
    late = jnp.concatenate([value[fold:hours], jnp.zeros((2 * fold - hours, LANES), F32)], axis=0)
    left = lane_ids((fold, LANES)) < half
    strip_e[...] = choose(left, early, pltpu.roll(late, half, 1))
    strip_o[...] = choose(left, pltpu.roll(early, half, 1), late)


def write_rows(parity, row_value, rows, rows_e, rows_o):
    top = rows - RAD

    def send(first, last):
        for row in range(RAD):
            rows_e[row] = row_value(first + row)
            rows_o[row] = row_value(last + row)

    @pl.when(parity == 0)
    def _():
        send(top, 0)

    @pl.when(parity == 1)
    def _():
        send(0, top)


def pack_kernel(par_ref, control_ref, field_ref, rows_e, rows_o, strip_e, strip_o):
    hours, rows, _ = control_ref.shape
    for row in range(rows):
        field_ref[row] = control_ref[:, row, :]
    write_rows(par_ref[0], lambda r: field_ref[r], rows, rows_e, rows_o)
    fold_hours(pack_strips(lambda r: field_ref[r], par_ref[1], rows), hours, strip_e, strip_o)


def corner_kernel(par_ref, strip_e, strip_o, halo_ref, corner_e, corner_o):
    fold = strip_e.shape[0]
    quarter = corner_e.shape[0]
    half = LANES // 2
    part = RAD * RAD
    even, odd = strip_e[...], strip_o[...]
    is_even = par_ref[1] == 0
    prev, following = choose(is_even, odd, even), choose(is_even, even, odd)
    left = lane_ids((fold, LANES)) < half
    halo_ref[0:fold] = choose(left, prev, pltpu.roll(following, half, 1))
    halo_ref[fold : 2 * fold] = choose(left, pltpu.roll(prev, half, 1), following)
    lane = lane_ids((quarter, LANES))
    low = high = jnp.zeros((quarter, LANES), F32)
    for q in range(LANES // (2 * part)):
        piece = halo_ref[q * quarter : (q + 1) * quarter]
        base = q * 2 * part
        for side in range(2):
            here = (lane >= base + side * part) & (lane < base + (side + 1) * part)
            to = base + side * part
            low = choose(here, pltpu.roll(piece, (to - side * half) % LANES, 1), low)
            high = choose(here, pltpu.roll(piece, (to - side * half - (half - part)) % LANES, 1), high)
    rec_even = par_ref[0] == 0
    corner_e[...] = choose(rec_even, high, low)
    corner_o[...] = choose(rec_even, low, high)


def corner_strips(is_even, corner_e, corner_o):
    part = 2 * RAD * RAD
    prev = choose(is_even, corner_o[...], corner_e[...])
    following = choose(is_even, corner_e[...], corner_o[...])
    lane = lane_ids(prev.shape)
    pieces = []
    for q in range(LANES // part):
        a = prev if q == 0 else pltpu.roll(prev, LANES - q * part, 1)
        turn = (part - q * part) % LANES
        b = following if turn == 0 else pltpu.roll(following, turn, 1)
        pieces.append(choose(lane < part, a, choose(lane < 2 * part, b, 0.0)))
    return jnp.concatenate(pieces, axis=0)


def halo_sums(parts, high_ref, low_ref, first, width):
    high, both = parts
    weights = high_ref[:, first : first + width]
    return dot(both, jnp.concatenate([weights, weights], axis=0)) + dot(high, low_ref[:, first : first + width])


def halo_parts(value):
    high, low = split(value)
    return high, jnp.concatenate([high, low], axis=1)


def column_sums(value, col_both):
    cols = value.shape[1]
    high, low = split(value)
    out = dot(jnp.concatenate([high, low], axis=1), col_both)
    return out[:, :cols] + out[:, cols:]


def time_sums(value, time_high, time_low):
    high, low = split(value)
    return dot(time_high, high) + dot(time_high, low) + dot(time_low, high)


def row_sums(get, row, low, high, taps):
    total = None
    for distance in range(RAD + 1):
        here = [get(r) for r in sorted({row - distance, row + distance}) if low <= r < high]
        if not here:
            continue
        part = here[0] if len(here) == 1 else here[0] + here[1]
        part = float(taps[RAD + distance]) * part
        total = part if total is None else total + part
    return total


def local_kernel(field_ref, halo_ref, time_high, time_low, col_both, own_high, own_low, out_ref, *, by_hour):
    rows, hours, cols = field_ref.shape
    taps = space_taps()
    halo = halo_parts(halo_ref[0:hours, :])
    for row in range(0, rows, 2):
        pair = [
            column_sums(row_sums(lambda i: field_ref[i], r, 0, rows, taps), col_both[...])
            for r in (row, row + 1)
        ]
        value = jnp.concatenate(pair, axis=1) + halo_sums(halo, own_high, own_low, row * cols, 2 * cols)
        both = time_sums(value, time_high[...], time_low[...])
        for k, r in enumerate((row, row + 1)):
            part = both[:, k * cols : (k + 1) * cols]
            if by_hour:
                out_ref[:, r, :] = part
            else:
                out_ref[r] = part


def edge_parts(is_even, rows, got_e, got_o, corner_e, corner_o, consts, halo, factor):
    time_high, time_low, col_both, corner_high, corner_low = consts
    hours, cols = halo.shape[1:]
    taps = space_taps()
    for row in range(RAD):
        even, odd = got_e[row].astype(F32), got_o[row].astype(F32)
        if factor is not None:
            even, odd = even * factor, odd * factor
        halo[row] = choose(is_even, odd, even)
        halo[RAD + row] = choose(is_even, even, odd)
    corner = halo_parts(corner_strips(is_even, corner_e, corner_o)[0:hours])
    edge = list(range(RAD)) + list(range(rows - RAD, rows))
    for first in range(0, 2 * RAD, 2):
        pair = []
        for r in edge[first : first + 2]:
            if r < RAD:
                summed = row_sums(lambda i: halo[i + RAD], r, -RAD, 0, taps)
            else:
                summed = row_sums(lambda i: halo[RAD + i - rows], r, rows, rows + RAD, taps)
            pair.append(column_sums(summed, col_both[...]))
        value = jnp.concatenate(pair, axis=1)
        value = value + halo_sums(corner, corner_high, corner_low, first * cols, 2 * cols)
        both = time_sums(value, time_high[...], time_low[...])
        for k, r in enumerate(edge[first : first + 2]):
            yield r, both[:, k * cols : (k + 1) * cols]


def flux_kernel(
    par_ref, local_ref, prior_ref, scale_ref, got_e, got_o, corner_e, corner_o,
    time_high, time_low, col_both, corner_high, corner_low, flux_ref, scale_out, halo, wide,
):
    rows, hours, cols = local_ref.shape
    consts = (time_high, time_low, col_both, corner_high, corner_low)
    wide[...] = scale_ref[...].astype(F32)
    for row in range(rows):
        scale_out[row] = wide[:, row, :]
    wide[...] = prior_ref[...].astype(F32)
    for row in range(RAD, rows - RAD):
        flux_ref[row] = wide[:, row, :] + scale_out[row] * local_ref[row]
    parts = edge_parts(par_ref[0] == 0, rows, got_e, got_o, corner_e, corner_o, consts, halo, None)
    for row, part in parts:
        flux_ref[row] = wide[:, row, :] + scale_out[row] * (local_ref[row] + part)


def finish_kernel(
    par_ref, local_ref, factor_ref, got_e, got_o, corner_e, corner_o,
    time_high, time_low, col_both, corner_high, corner_low, out_ref, halo,
):
    hours, rows, cols = local_ref.shape
    consts = (time_high, time_low, col_both, corner_high, corner_low)
    out_ref[...] = local_ref[...]
    factor = factor_ref[1:2, :]
    parts = edge_parts(par_ref[0] == 0, rows, got_e, got_o, corner_e, corner_o, consts, halo, factor)
    for row, part in parts:
        out_ref[:, row, :] = out_ref[:, row, :] + part


def blocks_of(foot_ref, source, heights, slots):
    for c in range(0, slots, 2):
        both = foot_ref[source, c * heights : (c + 2) * heights, :].astype(F32)
        yield c, both[0:heights]
        yield c + 1, both[heights : 2 * heights]


def forward_kernel(
    foot_ref, flux_ref, own_ref, out_ref, table_ref, sums, table_smem, sem,
    *, shift, slots, heights, tiles, per,
):
    sources = foot_ref.shape[0]
    groups = out_ref.shape[1] - 1
    base = slots * heights
    lane = lane_ids((sources, LANES))
    notes = foot_ref[:, base : base + SUB, :].astype(F32)[:, 0, :].astype(jnp.int32)
    start = notes * 16 + pltpu.roll(notes, LANES - slots, 1)
    offset = start + pltpu.roll(notes, LANES - 2 * slots, 1) * (1 << shift)
    source_rec = lax.broadcasted_iota(jnp.int32, (sources, LANES), 0) // tiles
    receptor = jnp.where(notes < per, source_rec * per + notes, groups * LANES)
    table = jnp.where(lane < slots, offset, receptor)
    table_ref[...] = table
    copy = pltpu.make_async_copy(table_ref, table_smem, sem)
    copy.start()
    copy.wait()

    def body(source, carry):
        for c, block in blocks_of(foot_ref, source, heights, slots):
            offset = table_smem[source, c]
            row = lax.shift_right_logical(offset, shift)
            begin = jnp.bitwise_and(offset, (1 << shift) - 1)
            product = flux_ref[row, pl.ds(begin, heights), :] * block
            sums[c, pl.ds(source, 1), :] = jnp.sum(product, axis=0, keepdims=True)
        return carry

    lax.fori_loop(0, sources, body, 0)
    totals = [jnp.zeros((sources, LANES), F32) for _ in range(groups)]
    for c in range(slots):
        value = jnp.sum(sums[c], axis=1, keepdims=True)
        which = table[:, 3 * slots + c : 3 * slots + c + 1]
        for q in range(groups):
            totals[q] = totals[q] + jnp.where(which == lane + q * LANES, value, 0.0)
    for q in range(groups):
        total = jnp.sum(totals[q], axis=0, keepdims=True)
        out_ref[:, q : q + 1, :] = jnp.broadcast_to(total[None], (sources, 1, LANES))
    out_ref[:, groups : groups + 1, :] = jnp.broadcast_to(own_ref[...][None], (sources, 1, LANES))


def adjoint_kernel(
    par_ref, table_ref, got_ref, foot_ref, scale_ref,
    model_ref, factor_ref, field_ref, rows_e, rows_o, strip_e, strip_o,
    weight_vmem, weight_smem, sem, *, shift, slots, heights, tiles, per,
):
    sources = foot_ref.shape[0]
    groups = model_ref.shape[0]
    rows, hours, _ = field_ref.shape
    model = jnp.sum(got_ref[:, 0:groups, :], axis=0)
    model_ref[...] = model
    packed = LANES // per
    lane = lane_ids((1, LANES))
    weight_vmem[...] = jnp.zeros_like(weight_vmem)
    for q in range(groups):
        observed, error = jnp.zeros((1, LANES), F32), jnp.ones((1, LANES), F32)
        for k in range(packed):
            line = got_ref[(q * packed + k) * tiles, groups : groups + 1, :]
            here = (lane >= k * per) & (lane < (k + 1) * per)
            observed = jnp.where(here, line if k == 0 else pltpu.roll(line, k * per, 1), observed)
            turn = (k * per - per) % LANES
            error = jnp.where(here, line if turn == 0 else pltpu.roll(line, turn, 1), error)
        weight_vmem[q : q + 1, :] = (model[q : q + 1, :] - observed) / (error * error)
    copy = pltpu.make_async_copy(weight_vmem, weight_smem, sem)
    copy.start()
    field_ref[...] = jnp.zeros_like(field_ref)
    top = jnp.max(jnp.abs(weight_vmem[...]), keepdims=True) * (FOOT_MAX * SCALE_MAX * sources * slots)
    top = jnp.maximum(top, 1e-25)
    factor_ref[0:1, :] = jnp.broadcast_to(HALF_TOP / top, (1, LANES))
    factor_ref[1:2, :] = jnp.broadcast_to(top * (1.0 / HALF_TOP), (1, LANES))
    copy.wait()

    def body(source, carry):
        for c, block in blocks_of(foot_ref, source, heights, slots):
            offset = table_ref[source, c]
            receptor = table_ref[source, 3 * slots + c]
            row = lax.shift_right_logical(offset, shift)
            begin = jnp.bitwise_and(offset, (1 << shift) - 1)
            weight = weight_smem[lax.shift_right_logical(receptor, 7), jnp.bitwise_and(receptor, LANES - 1)]
            field_ref[row, pl.ds(begin, heights), :] += block * weight
        return carry

    lax.fori_loop(0, sources, body, 0)
    for row in range(rows):
        field_ref[row] = field_ref[row] * scale_ref[row]
    factor = factor_ref[0:1, :]
    write_rows(par_ref[0], lambda r: field_ref[r] * factor, rows, rows_e, rows_o)
    fold_hours(pack_strips(lambda r: field_ref[r], par_ref[1], rows), hours, strip_e, strip_o)


def swap_pairs(count, odd):
    pairs = []
    for i in range(1 if odd else 0, count - 1, 2):
        pairs += [(i, i + 1), (i + 1, i)]
    return pairs


def swap(axis, even, odd):
    count = lax.axis_size(axis)
    return (
        lax.ppermute(even, axis, swap_pairs(count, False)),
        lax.ppermute(odd, axis, swap_pairs(count, True)),
    )


SM = pl.BlockSpec(memory_space=pltpu.SMEM)
VM = pl.BlockSpec(memory_space=pltpu.VMEM)


def call(kernel, out_shape, in_specs, scratch, name):
    return pl.pallas_call(
        kernel,
        out_shape=out_shape,
        in_specs=in_specs,
        out_specs=jax.tree.map(lambda _: VM, out_shape),
        scratch_shapes=scratch,
        compiler_params=pltpu.CompilerParams(vmem_limit_bytes=VMEM_LIMIT),
        name=name,
    )


def array(*shape):
    return jax.ShapeDtypeStruct(shape, F32)


def per_device(
    prior_flux,
    flux_scale,
    control,
    footprint,
    slot_count,
    start_hour,
    grid_row,
    receptor_slot,
    observed,
    obs_error,
):
    hours, rows, cols = control.shape
    n_rec, n_tile = lax.axis_size("rec"), lax.axis_size("tile")
    devices = n_rec * n_tile
    slots, heights = footprint.shape[1], footprint.shape[2]
    per = observed.shape[0]
    groups = per * n_rec // LANES
    shift = (hours - 1).bit_length()
    rec, tile = lax.axis_index("rec"), lax.axis_index("tile")
    par = jnp.stack([rec % 2, tile % 2]).astype(jnp.int32)
    base, own_parts, corner_parts = constants(hours, rows, cols)
    base = [jnp.asarray(c) for c in base]
    own_parts = [jnp.asarray(c) for c in own_parts]
    corner_parts = [jnp.asarray(c) for c in corner_parts]
    fold = -(-hours // (2 * 64)) * 64
    strip, corner = array(fold, LANES), array(fold // 2, LANES)
    block = array(RAD, hours, cols)
    field_shape = array(rows, hours, cols)
    halo_scratch = pltpu.VMEM((2 * RAD, hours, cols), F32)

    valid = jnp.arange(slots)[None, :] < slot_count[:, None]
    notes = jnp.concatenate(
        [start_hour >> 4, start_hour & 15, grid_row, jnp.where(valid, receptor_slot, per)], axis=1
    ).astype(BF16)
    notes = jnp.pad(notes, ((0, 0), (0, LANES - 4 * slots)))[:, None, :]
    notes = jnp.pad(notes, ((0, 0), (0, SUB - 1), (0, 0)))
    sent = jnp.concatenate([footprint.reshape(devices, slots * heights, cols), notes], axis=1)
    foot = lax.all_to_all(sent, AXES, split_axis=0, concat_axis=0, tiled=True)

    field, rows_e, rows_o, strip_e, strip_o = call(
        pack_kernel, [field_shape, block, block, strip, strip], [SM, VM], [], "pack_control"
    )(par, control)

    def neighbours(rows_e, rows_o, strip_e, strip_o):
        got_rows = swap("rec", rows_e, rows_o)
        got_strips = swap("tile", strip_e, strip_o)
        halo, corner_e, corner_o = call(
            corner_kernel, [array(2 * fold, LANES), corner, corner], [SM, VM, VM], [], "corners"
        )(par, *got_strips)
        return got_rows, halo, swap("rec", corner_e, corner_o)

    def local_sums(field, halo, by_hour, name):
        def kernel(*refs):
            local_kernel(*refs, by_hour=by_hour)

        shape = array(hours, rows, cols) if by_hour else field_shape
        return call(kernel, shape, [VM] * 7, [], name)(field, halo, *base, *own_parts)

    got_rows, halo, got_corners = neighbours(rows_e, rows_o, strip_e, strip_o)
    local = local_sums(field, halo, False, "control_local")
    flux, scale = call(
        flux_kernel,
        [field_shape, field_shape],
        [SM] + [VM] * 12,
        [halo_scratch, pltpu.VMEM((hours, rows, cols), F32)],
        "flux_field",
    )(par, local, prior_flux, flux_scale, *got_rows, *got_corners, *base, *corner_parts)

    own = jnp.concatenate([observed, obs_error, jnp.zeros((LANES - 2 * per,), F32)])[None]
    sizes = dict(shift=shift, slots=slots, heights=heights, tiles=n_tile, per=per)

    def forward(*refs):
        forward_kernel(*refs, **sizes)

    partial, table = call(
        forward,
        [array(devices, groups + 1, LANES), jax.ShapeDtypeStruct((devices, LANES), jnp.int32)],
        [VM, VM, VM],
        [
            pltpu.VMEM((slots, devices, LANES), F32),
            pltpu.SMEM((devices, LANES), jnp.int32),
            pltpu.SemaphoreType.DMA,
        ],
        "block_values",
    )(foot, flux, own)
    everyone = lax.all_to_all(partial, AXES, split_axis=0, concat_axis=0, tiled=True)

    def adjoint(*refs):
        adjoint_kernel(*refs, **sizes)

    weight_rows = -(-(groups + 1) // SUB) * SUB
    model, factor, field, rows_e, rows_o, strip_e, strip_o = call(
        adjoint,
        [array(groups, LANES), array(2, LANES), field_shape, block, block, strip, strip],
        [SM, SM, VM, VM, VM],
        [
            pltpu.VMEM((weight_rows, LANES), F32),
            pltpu.SMEM((weight_rows, LANES), F32),
            pltpu.SemaphoreType.DMA,
        ],
        "adjoint_field",
    )(par, table, everyone, foot, scale)
    got_rows, halo, got_corners = neighbours(rows_e.astype(F16), rows_o.astype(F16), strip_e, strip_o)
    got_rows = [r.astype(F32) for r in got_rows]
    local = local_sums(field, halo, True, "gradient_local")
    gradient = call(
        finish_kernel, array(hours, rows, cols), [SM] + [VM] * 11, [halo_scratch], "gradient"
    )(par, local, factor, *got_rows, *got_corners, *base, *corner_parts)
    model_co2 = lax.dynamic_slice_in_dim(model.reshape(-1), rec * per, per)
    return (model_co2, gradient)


def solution(mesh):
    return jax.shard_map(
        per_device,
        mesh=mesh,
        in_specs=(
            P(None, "rec", "tile"),
            P(None, "rec", "tile"),
            P(None, "rec", "tile"),
            P(("rec", "tile"), None, None, None),
            P(("rec", "tile")),
            P(("rec", "tile"), None),
            P(("rec", "tile"), None),
            P(("rec", "tile"), None),
            P("rec"),
            P("rec"),
        ),
        out_specs=(P("rec"), P(None, "rec", "tile")),
        check_vma=False,
    )
```

```python
import numpy as np
import jax
import jax.numpy as jnp
from jax import lax
from jax.experimental import pallas as pl
from jax.experimental.pallas import tpu as pltpu
from jax.sharding import PartitionSpec as P

RAD = 4
TAPS = 12
AXES = ("rec", "tile")
LANES = 128
SUB = 8
FOOT_MAX = 0.02
PIECES = 3
SCALE_MAX = 2.0
HALF_TOP = 32768.0
CONTROL_FACTOR = 4096.0
F16 = jnp.float16
VMEM_LIMIT = 12 * 1024 * 1024
F32 = jnp.float32
BF16 = jnp.bfloat16


def space_taps():
    offsets = np.arange(-RAD, RAD + 1).astype(np.float64)
    values = np.exp(-2.0 * offsets * offsets / (RAD * RAD))
    return values / np.sqrt(np.sum(values * values))


def time_taps():
    offsets = np.arange(-TAPS, TAPS + 1).astype(np.float64)
    values = np.exp(-2.0 * np.abs(offsets) / TAPS)
    return values / np.sqrt(np.sum(values * values))


def banded(distance, taps, reach):
    inside = np.abs(distance) <= reach
    return np.where(inside, taps[np.clip(distance, -reach, reach) + reach], 0.0)


def two_parts(matrix):
    high = matrix.astype(np.float32).astype(jnp.bfloat16)
    low = (matrix - high.astype(np.float64)).astype(np.float32).astype(jnp.bfloat16)
    return high, low


def constants(hours, rows, cols):
    space = space_taps()
    hour = np.arange(hours)
    time_high, time_low = two_parts(banded(hour[:, None] - hour[None, :], time_taps(), TAPS))
    col = np.arange(cols)
    col_high, col_low = two_parts(banded(col[:, None] - col[None, :], space, RAD))
    col_both = np.block([[col_high, col_low], [col_high, np.zeros_like(col_high)]])
    halo_col = np.concatenate([np.arange(-RAD, 0), np.arange(cols, cols + RAD)])
    edge = banded(halo_col[:, None] - col[None, :], space, RAD)

    def strips(row_of, halo_of, targets):
        by_row = banded(np.array(row_of)[:, None] - np.array(targets)[None, :], space, RAD)
        both = by_row[:, :, None] * edge[np.array(halo_of)][:, None, :]
        return two_parts(both.reshape(len(row_of), -1))

    own = [(row, side * RAD + j) for side in range(2) for row in range(rows) for j in range(RAD)]
    corner = [
        (row, side * RAD + j)
        for first in (-RAD, rows)
        for side in range(2)
        for row in range(first, first + RAD)
        for j in range(RAD)
    ]
    corner += [(-100, 0)] * (LANES - len(corner))
    edge_rows = list(range(RAD)) + list(range(rows - RAD, rows))
    own_parts = strips(*zip(*own), np.arange(rows))
    corner_parts = strips(*zip(*corner), np.array(edge_rows))
    return (time_high, time_low, col_both), own_parts, corner_parts


def split(value):
    high = value.astype(BF16)
    low = (value - high.astype(F32)).astype(BF16)
    return high, low


def dot(a, b):
    return jnp.dot(a, b, preferred_element_type=F32)


def lane_ids(shape):
    return lax.broadcasted_iota(jnp.int32, shape, 1)


def choose(flag, yes, no):
    return jnp.where(flag, yes, no)


def pack_strips(row_value, parity, rows):
    cols = row_value(0).shape[1]
    half = rows * RAD
    source = lax.broadcasted_iota(jnp.int32, (cols, 2 * half), 0)
    lane = lax.broadcasted_iota(jnp.int32, (cols, 2 * half), 1)
    first = lane < half
    j = lane & (RAD - 1)
    high_end = jnp.logical_xor(first, parity == 1)
    wanted = jnp.where(high_end, cols - RAD + j, j)
    lane_row = jnp.where(first, lane, lane - half) // RAD
    total = None
    for row in range(rows):
        high, low = split(row_value(row))
        pick = jnp.where((source == wanted) & (lane_row == row), 1.0, 0.0).astype(BF16)
        part = dot(jnp.concatenate([high, low], axis=1), jnp.concatenate([pick, pick], axis=0))
        total = part if total is None else total + part
    return total


def fold_hours(value, hours, strip_e, strip_o):
    fold = strip_e.shape[0]
    half = LANES // 2
    early = value[0:fold]
    late = jnp.concatenate([value[fold:hours], jnp.zeros((2 * fold - hours, LANES), F32)], axis=0)
    left = lane_ids((fold, LANES)) < half
    strip_e[...] = choose(left, early, pltpu.roll(late, half, 1))
    strip_o[...] = choose(left, pltpu.roll(early, half, 1), late)


def write_rows(parity, row_value, rows, rows_e, rows_o):
    top = rows - RAD

    def send(first, last):
        for row in range(RAD):
            rows_e[row] = row_value(first + row)
            rows_o[row] = row_value(last + row)

    @pl.when(parity == 0)
    def _():
        send(top, 0)

    @pl.when(parity == 1)
    def _():
        send(0, top)


def pack_kernel(par_ref, control_ref, field_ref, rows_e, rows_o, strip_e, strip_o):
    hours, rows, _ = control_ref.shape
    for row in range(rows):
        field_ref[row] = control_ref[:, row, :]
    write_rows(par_ref[0], lambda r: field_ref[r] * CONTROL_FACTOR, rows, rows_e, rows_o)
    fold_hours(pack_strips(lambda r: field_ref[r], par_ref[1], rows), hours, strip_e, strip_o)


def strip_kernel(par_ref, field_ref, strip_e, strip_o):
    rows, hours, _ = field_ref.shape
    fold_hours(pack_strips(lambda r: field_ref[r], par_ref[1], rows), hours, strip_e, strip_o)


def prepare_kernel(
    foot_ref, start_ref, row_ref, slot_ref, count_ref, out_ref,
    start_vmem, row_vmem, slot_vmem, count_vmem, notes, sems, *, per,
):
    owners, lines, _ = foot_ref.shape
    slots = start_ref.shape[0]
    blocks = pltpu.make_async_copy(foot_ref, out_ref.at[:, 0:lines, :], sems.at[0])
    blocks.start()
    pairs = ((start_ref, start_vmem), (row_ref, row_vmem), (slot_ref, slot_vmem), (count_ref, count_vmem))
    small = [pltpu.make_async_copy(a, b, sems.at[1 + i]) for i, (a, b) in enumerate(pairs)]
    for copy in small:
        copy.start()
    for copy in small:
        copy.wait()
    start = start_vmem[...]
    valid = lax.broadcasted_iota(jnp.int32, start.shape, 0) < count_vmem[...]
    lanes = jnp.concatenate(
        [start >> 4, start & 15, row_vmem[...], jnp.where(valid, slot_vmem[...], per)], axis=0
    ).astype(F32)
    wide = jnp.pad(lanes, ((0, LANES - 4 * slots), (0, LANES - owners)))
    turned = jnp.transpose(wide)[0:owners]
    notes[...] = jnp.broadcast_to(turned[:, None, :], notes.shape).astype(BF16)
    copy = pltpu.make_async_copy(notes, out_ref.at[:, lines : lines + SUB, :], sems.at[5])
    copy.start()
    copy.wait()
    blocks.wait()


def corner_kernel(par_ref, strip_e, strip_o, halo_ref, corner_e, corner_o):
    fold = strip_e.shape[0]
    quarter = corner_e.shape[0]
    half = LANES // 2
    part = RAD * RAD
    even, odd = strip_e[...], strip_o[...]
    is_even = par_ref[1] == 0
    prev, following = choose(is_even, odd, even), choose(is_even, even, odd)
    left = lane_ids((fold, LANES)) < half
    halo_ref[0:fold] = choose(left, prev, pltpu.roll(following, half, 1))
    halo_ref[fold : 2 * fold] = choose(left, pltpu.roll(prev, half, 1), following)
    lane = lane_ids((quarter, LANES))
    low = high = jnp.zeros((quarter, LANES), F32)
    for q in range(LANES // (2 * part)):
        piece = halo_ref[q * quarter : (q + 1) * quarter]
        base = q * 2 * part
        for side in range(2):
            here = (lane >= base + side * part) & (lane < base + (side + 1) * part)
            to = base + side * part
            low = choose(here, pltpu.roll(piece, (to - side * half) % LANES, 1), low)
            high = choose(here, pltpu.roll(piece, (to - side * half - (half - part)) % LANES, 1), high)
    rec_even = par_ref[0] == 0
    corner_e[...] = choose(rec_even, high, low)
    corner_o[...] = choose(rec_even, low, high)


def corner_strips(is_even, corner_e, corner_o):
    part = 2 * RAD * RAD
    prev = choose(is_even, corner_o[...], corner_e[...])
    following = choose(is_even, corner_e[...], corner_o[...])
    lane = lane_ids(prev.shape)
    pieces = []
    for q in range(LANES // part):
        a = prev if q == 0 else pltpu.roll(prev, LANES - q * part, 1)
        turn = (part - q * part) % LANES
        b = following if turn == 0 else pltpu.roll(following, turn, 1)
        pieces.append(choose(lane < part, a, choose(lane < 2 * part, b, 0.0)))
    return jnp.concatenate(pieces, axis=0)


def halo_sums(parts, high_ref, low_ref, first, width):
    high, both = parts
    weights = high_ref[:, first : first + width]
    return dot(both, jnp.concatenate([weights, weights], axis=0)) + dot(high, low_ref[:, first : first + width])


def halo_parts(value):
    high, low = split(value)
    return high, jnp.concatenate([high, low], axis=1)


def column_sums(value, col_both):
    cols = value.shape[1]
    high, low = split(value)
    out = dot(jnp.concatenate([high, low], axis=1), col_both)
    return out[:, :cols] + out[:, cols:]


def time_sums(value, time_high, time_low):
    high, low = split(value)
    return dot(time_high, high) + dot(time_high, low) + dot(time_low, high)


def row_sums(get, row, low, high, taps):
    total = None
    for distance in range(RAD + 1):
        here = [get(r) for r in sorted({row - distance, row + distance}) if low <= r < high]
        if not here:
            continue
        part = here[0] if len(here) == 1 else here[0] + here[1]
        part = float(taps[RAD + distance]) * part
        total = part if total is None else total + part
    return total


def local_kernel(field_ref, time_high, time_low, col_both, out_ref, *, by_hour):
    rows, hours, cols = field_ref.shape
    taps = space_taps()
    for row in range(0, rows, 2):
        pair = [
            column_sums(row_sums(lambda i: field_ref[i], r, 0, rows, taps), col_both[...])
            for r in (row, row + 1)
        ]
        both = time_sums(jnp.concatenate(pair, axis=1), time_high[...], time_low[...])
        for k, r in enumerate((row, row + 1)):
            part = both[:, k * cols : (k + 1) * cols]
            if by_hour:
                out_ref[:, r, :] = part
            else:
                out_ref[r] = part


def strips_kernel(local_ref, halo_ref, time_high, time_low, own_high, own_low, out_ref, *, by_hour):
    if by_hour:
        hours, rows, cols = local_ref.shape
    else:
        rows, hours, cols = local_ref.shape
    halo = halo_parts(time_sums(halo_ref[0:hours, :], time_high[...], time_low[...]))
    for row in range(0, rows, 2):
        both = halo_sums(halo, own_high, own_low, row * cols, 2 * cols)
        for k, r in enumerate((row, row + 1)):
            part = both[:, k * cols : (k + 1) * cols]
            if by_hour:
                out_ref[:, r, :] = local_ref[:, r, :] + part
            else:
                out_ref[r] = local_ref[r] + part


def edge_parts(is_even, rows, got_e, got_o, corner_e, corner_o, consts, halo, factor):
    time_high, time_low, col_both, corner_high, corner_low = consts
    hours, cols = halo.shape[1:]
    taps = space_taps()
    for row in range(RAD):
        even, odd = got_e[row], got_o[row]
        halo[row] = choose(is_even, odd, even) * factor
        halo[RAD + row] = choose(is_even, even, odd) * factor
    corner = halo_parts(corner_strips(is_even, corner_e, corner_o)[0:hours])
    edge = list(range(RAD)) + list(range(rows - RAD, rows))
    for first in range(0, 2 * RAD, 2):
        pair = []
        for r in edge[first : first + 2]:
            if r < RAD:
                summed = row_sums(lambda i: halo[i + RAD], r, -RAD, 0, taps)
            else:
                summed = row_sums(lambda i: halo[RAD + i - rows], r, rows, rows + RAD, taps)
            pair.append(column_sums(summed, col_both[...]))
        value = jnp.concatenate(pair, axis=1)
        value = value + halo_sums(corner, corner_high, corner_low, first * cols, 2 * cols)
        both = time_sums(value, time_high[...], time_low[...])
        for k, r in enumerate(edge[first : first + 2]):
            yield r, both[:, k * cols : (k + 1) * cols]


def flux_kernel(
    par_ref, local_ref, prior_ref, scale_ref, got_e, got_o, corner_e, corner_o,
    time_high, time_low, col_both, corner_high, corner_low, flux_ref, scale_out, halo, wide,
):
    rows, hours, cols = local_ref.shape
    consts = (time_high, time_low, col_both, corner_high, corner_low)
    wide[...] = scale_ref[...].astype(F32)
    for row in range(rows):
        scale_out[row] = wide[:, row, :]
    wide[...] = prior_ref[...].astype(F32)
    for row in range(RAD, rows - RAD):
        flux_ref[row] = wide[:, row, :] + scale_out[row] * local_ref[row]
    parts = edge_parts(par_ref[0] == 0, rows, got_e, got_o, corner_e, corner_o, consts, halo, 1.0 / CONTROL_FACTOR)
    for row, part in parts:
        flux_ref[row] = wide[:, row, :] + scale_out[row] * (local_ref[row] + part)


def finish_kernel(
    par_ref, local_ref, factor_ref, got_e, got_o, corner_e, corner_o,
    time_high, time_low, col_both, corner_high, corner_low, out_ref, halo, edges, total, sems,
):
    hours, rows, cols = local_ref.shape
    consts = (time_high, time_low, col_both, corner_high, corner_low)
    factor = factor_ref[1:2, :]
    parts = edge_parts(par_ref[0] == 0, rows, got_e, got_o, corner_e, corner_o, consts, halo, factor)
    order = []
    for k, (row, part) in enumerate(parts):
        edges[k] = part
        order.append(row)
    chunk = hours // PIECES
    copies = []
    for piece in range(PIECES):
        here = slice(piece * chunk, (piece + 1) * chunk)
        total[here] = local_ref[here]
        for k, row in enumerate(order):
            total[here, row, :] = total[here, row, :] + edges[k, here, :]
        copies.append(pltpu.make_async_copy(total.at[here], out_ref.at[here], sems.at[piece]))
        copies[-1].start()
    for copy in copies:
        copy.wait()


def blocks_of(foot_ref, source, heights, slots):
    for c in range(0, slots, 2):
        both = foot_ref[source, c * heights : (c + 2) * heights, :].astype(F32)
        yield c, both[0:heights]
        yield c + 1, both[heights : 2 * heights]


def forward_kernel(
    foot_ref, flux_hbm, own_ref, out_ref, table_ref, flux_ref, sums, table_smem, sems,
    *, shift, slots, heights, tiles, per,
):
    sources = foot_ref.shape[0]
    load = pltpu.make_async_copy(flux_hbm, flux_ref, sems.at[0])
    load.start()
    groups = out_ref.shape[1] - 1
    base = slots * heights
    lane = lane_ids((sources, LANES))
    notes = foot_ref[:, base : base + SUB, :].astype(F32)[:, 0, :].astype(jnp.int32)
    start = notes * 16 + pltpu.roll(notes, LANES - slots, 1)
    offset = start + pltpu.roll(notes, LANES - 2 * slots, 1) * (1 << shift)
    source_rec = lax.broadcasted_iota(jnp.int32, (sources, LANES), 0) // tiles
    receptor = jnp.where(notes < per, source_rec * per + notes, groups * LANES)
    table = jnp.where(lane < slots, offset, receptor)
    table_ref[...] = table
    copy = pltpu.make_async_copy(table_ref, table_smem, sems.at[1])
    copy.start()
    copy.wait()
    load.wait()

    def body(source, carry):
        for c, block in blocks_of(foot_ref, source, heights, slots):
            offset = table_smem[source, c]
            row = lax.shift_right_logical(offset, shift)
            begin = jnp.bitwise_and(offset, (1 << shift) - 1)
            product = flux_ref[row, pl.ds(begin, heights), :] * block
            sums[c, pl.ds(source, 1), :] = jnp.sum(product, axis=0, keepdims=True)
        return carry

    lax.fori_loop(0, sources, body, 0)
    totals = [jnp.zeros((sources, LANES), F32) for _ in range(groups)]
    for c in range(slots):
        value = jnp.sum(sums[c], axis=1, keepdims=True)
        which = table[:, 3 * slots + c : 3 * slots + c + 1]
        for q in range(groups):
            totals[q] = totals[q] + jnp.where(which == lane + q * LANES, value, 0.0)
    for q in range(groups):
        total = jnp.sum(totals[q], axis=0, keepdims=True)
        out_ref[:, q : q + 1, :] = jnp.broadcast_to(total[None], (sources, 1, LANES))
    out_ref[:, groups : groups + 1, :] = jnp.broadcast_to(own_ref[...][None], (sources, 1, LANES))


def adjoint_kernel(
    par_ref, table_ref, got_ref, foot_ref, scale_ref,
    model_ref, factor_ref, field_ref, rows_e, rows_o,
    weight_vmem, weight_smem, sem, *, shift, slots, heights, tiles, per,
):
    sources = foot_ref.shape[0]
    groups = got_ref.shape[1] - 1
    rows, hours, _ = field_ref.shape
    model = jnp.sum(got_ref[:, 0:groups, :], axis=0)
    packed = LANES // per
    lane = lane_ids((1, LANES))
    own = jnp.zeros((1, LANES), F32)
    for q in range(groups):
        for k in range(packed):
            line = model[q : q + 1, :]
            line = line if k == 0 else pltpu.roll(line, LANES - k * per, 1)
            own = choose(par_ref[2] == q * packed + k, line, own)
    model_ref[...] = own[:, 0:per]
    weight_vmem[...] = jnp.zeros_like(weight_vmem)
    for q in range(groups):
        observed, error = jnp.zeros((1, LANES), F32), jnp.ones((1, LANES), F32)
        for k in range(packed):
            line = got_ref[(q * packed + k) * tiles, groups : groups + 1, :]
            here = (lane >= k * per) & (lane < (k + 1) * per)
            observed = jnp.where(here, line if k == 0 else pltpu.roll(line, k * per, 1), observed)
            turn = (k * per - per) % LANES
            error = jnp.where(here, line if turn == 0 else pltpu.roll(line, turn, 1), error)
        weight_vmem[q : q + 1, :] = (model[q : q + 1, :] - observed) / (error * error)
    copy = pltpu.make_async_copy(weight_vmem, weight_smem, sem)
    copy.start()
    field_ref[...] = jnp.zeros_like(field_ref)
    top = jnp.max(jnp.abs(weight_vmem[...]), keepdims=True) * (FOOT_MAX * SCALE_MAX * sources * slots)
    top = jnp.maximum(top, 1e-25)
    factor_ref[0:1, :] = jnp.broadcast_to(HALF_TOP / top, (1, LANES))
    factor_ref[1:2, :] = jnp.broadcast_to(top * (1.0 / HALF_TOP), (1, LANES))
    copy.wait()

    def body(source, carry):
        for c, block in blocks_of(foot_ref, source, heights, slots):
            offset = table_ref[source, c]
            receptor = table_ref[source, 3 * slots + c]
            row = lax.shift_right_logical(offset, shift)
            begin = jnp.bitwise_and(offset, (1 << shift) - 1)
            weight = weight_smem[lax.shift_right_logical(receptor, 7), jnp.bitwise_and(receptor, LANES - 1)]
            field_ref[row, pl.ds(begin, heights), :] += block * weight
        return carry

    lax.fori_loop(0, sources, body, 0)
    for row in range(rows):
        field_ref[row] = field_ref[row] * scale_ref[row]
    factor = factor_ref[0:1, :]
    write_rows(par_ref[0], lambda r: field_ref[r] * factor, rows, rows_e, rows_o)


def swap_pairs(count, odd):
    pairs = []
    for i in range(1 if odd else 0, count - 1, 2):
        pairs += [(i, i + 1), (i + 1, i)]
    return pairs


def swap(axis, even, odd):
    count = lax.axis_size(axis)
    return (
        lax.ppermute(even, axis, swap_pairs(count, False)),
        lax.ppermute(odd, axis, swap_pairs(count, True)),
    )


SM = pl.BlockSpec(memory_space=pltpu.SMEM)
VM = pl.BlockSpec(memory_space=pltpu.VMEM)
HB = pl.BlockSpec(memory_space=pltpu.HBM)


def call(kernel, out_shape, in_specs, scratch, name, out_specs=None, alias=None):
    return pl.pallas_call(
        kernel,
        out_shape=out_shape,
        in_specs=in_specs,
        out_specs=jax.tree.map(lambda _: VM, out_shape) if out_specs is None else out_specs,
        scratch_shapes=scratch,
        input_output_aliases={} if alias is None else alias,
        compiler_params=pltpu.CompilerParams(vmem_limit_bytes=VMEM_LIMIT),
        name=name,
    )


def array(*shape):
    return jax.ShapeDtypeStruct(shape, F32)


def per_device(
    prior_flux,
    flux_scale,
    control,
    footprint,
    slot_count,
    start_hour,
    grid_row,
    receptor_slot,
    observed,
    obs_error,
):
    hours, rows, cols = control.shape
    n_rec, n_tile = lax.axis_size("rec"), lax.axis_size("tile")
    devices = n_rec * n_tile
    slots, heights = footprint.shape[1], footprint.shape[2]
    per = observed.shape[0]
    groups = per * n_rec // LANES
    shift = (hours - 1).bit_length()
    rec, tile = lax.axis_index("rec"), lax.axis_index("tile")
    par = jnp.stack([rec % 2, tile % 2, rec]).astype(jnp.int32)
    base, own_parts, corner_parts = constants(hours, rows, cols)
    base = [jnp.asarray(c) for c in base]
    own_parts = [jnp.asarray(c) for c in own_parts]
    corner_parts = [jnp.asarray(c) for c in corner_parts]
    fold = -(-hours // (2 * 64)) * 64
    strip, corner = array(fold, LANES), array(fold // 2, LANES)
    block = array(RAD, hours, cols)
    field_shape = array(rows, hours, cols)
    halo_scratch = pltpu.VMEM((2 * RAD, hours, cols), F32)

    def prepare(*refs):
        prepare_kernel(*refs, per=per)

    numbers = pltpu.VMEM((slots, devices), jnp.int32)
    sent = call(
        prepare,
        jax.ShapeDtypeStruct((devices, slots * heights + SUB, cols), BF16),
        [HB] * 5,
        [
            numbers, numbers, numbers, pltpu.VMEM((1, devices), jnp.int32),
            pltpu.VMEM((devices, SUB, LANES), BF16), pltpu.SemaphoreType.DMA((6,)),
        ],
        "prepare_blocks",
        out_specs=HB,
    )(*[
        pltpu.with_memory_space_constraint(x, pltpu.HBM)
        for x in (
            footprint.reshape(devices, slots * heights, cols),
            start_hour.T, grid_row.T, receptor_slot.T, slot_count[None],
        )
    ])
    foot = lax.all_to_all(sent, AXES, split_axis=0, concat_axis=0, tiled=True)

    field, rows_e, rows_o, strip_e, strip_o = call(
        pack_kernel, [field_shape, block, block, strip, strip], [SM, VM], [], "pack_control"
    )(par, control)

    def neighbours(rows_e, rows_o):
        return [r.astype(F32) for r in swap("rec", rows_e.astype(F16), rows_o.astype(F16))]

    def sides(strip_e, strip_o):
        got_strips = swap("tile", strip_e, strip_o)
        halo, corner_e, corner_o = call(
            corner_kernel, [array(2 * fold, LANES), corner, corner], [SM, VM, VM], [], "corners"
        )(par, *got_strips)
        return halo, swap("rec", corner_e, corner_o)

    def inner_sums(field, halo, by_hour, name):
        def first(*refs):
            local_kernel(*refs, by_hour=by_hour)

        def second(*refs):
            strips_kernel(*refs, by_hour=by_hour)

        shape = array(hours, rows, cols) if by_hour else field_shape
        local = call(first, shape, [VM] * 4, [], name + "_local")(field, *base)
        return call(second, shape, [VM] * 6, [], name + "_strips", alias={0: 0})(
            local, halo, *base[:2], *own_parts
        )

    got_rows = neighbours(rows_e, rows_o)
    halo, got_corners = sides(strip_e, strip_o)
    local = inner_sums(field, halo, False, "control")
    flux, scale = call(
        flux_kernel,
        [field_shape, field_shape],
        [SM] + [VM] * 12,
        [halo_scratch, pltpu.VMEM((hours, rows, cols), F32)],
        "flux_field",
    )(par, local, prior_flux, flux_scale, *got_rows, *got_corners, *base, *corner_parts)

    own = jnp.concatenate([observed, obs_error, jnp.zeros((LANES - 2 * per,), F32)])[None]
    sizes = dict(shift=shift, slots=slots, heights=heights, tiles=n_tile, per=per)

    def forward(*refs):
        forward_kernel(*refs, **sizes)

    partial, table = call(
        forward,
        [array(devices, groups + 1, LANES), jax.ShapeDtypeStruct((devices, LANES), jnp.int32)],
        [VM, HB, VM],
        [
            pltpu.VMEM((rows, hours, cols), F32),
            pltpu.VMEM((slots, devices, LANES), F32),
            pltpu.SMEM((devices, LANES), jnp.int32),
            pltpu.SemaphoreType.DMA((2,)),
        ],
        "block_values",
    )(foot, flux, own)
    everyone = lax.all_to_all(partial, AXES, split_axis=0, concat_axis=0, tiled=True)

    def adjoint(*refs):
        adjoint_kernel(*refs, **sizes)

    weight_rows = -(-(groups + 1) // SUB) * SUB
    model_co2, factor, field, rows_e, rows_o = call(
        adjoint,
        [array(1, per), array(2, LANES), field_shape, block, block],
        [SM, SM, VM, VM, VM],
        [
            pltpu.VMEM((weight_rows, LANES), F32),
            pltpu.SMEM((weight_rows, LANES), F32),
            pltpu.SemaphoreType.DMA,
        ],
        "adjoint_field",
    )(par, table, everyone, foot, scale)
    got_rows = neighbours(rows_e, rows_o)
    strips = call(strip_kernel, [strip, strip], [SM, VM], [], "pack_strips")(par, field)
    halo, got_corners = sides(*strips)
    local = inner_sums(field, halo, True, "gradient")
    gradient = call(
        finish_kernel,
        array(hours, rows, cols),
        [SM] + [VM] * 11,
        [
            halo_scratch,
            halo_scratch,
            pltpu.VMEM((hours, rows, cols), F32),
            pltpu.SemaphoreType.DMA((PIECES,)),
        ],
        "gradient",
        out_specs=HB,
    )(par, local, factor, *got_rows, *got_corners, *base, *corner_parts)
    return (model_co2.reshape(-1), gradient)


def solution(mesh):
    return jax.shard_map(
        per_device,
        mesh=mesh,
        in_specs=(
            P(None, "rec", "tile"),
            P(None, "rec", "tile"),
            P(None, "rec", "tile"),
            P(("rec", "tile"), None, None, None),
            P(("rec", "tile")),
            P(("rec", "tile"), None),
            P(("rec", "tile"), None),
            P(("rec", "tile"), None),
            P("rec"),
            P("rec"),
        ),
        out_specs=(P("rec"), P(None, "rec", "tile")),
        check_vma=False,
    )
```

```python
import numpy as np
import jax
import jax.numpy as jnp
from jax import lax
from jax.experimental import pallas as pl
from jax.experimental.pallas import tpu as pltpu
from jax.sharding import PartitionSpec as P

RAD = 4
TAPS = 12
AXES = ("rec", "tile")
LANES = 128
SUB = 8
FOOT_MAX = 0.02
PIECES = 3
SCALE_MAX = 2.0
HALF_TOP = 32768.0
CONTROL_FACTOR = 4096.0
F16 = jnp.float16
VMEM_LIMIT = 12 * 1024 * 1024
F32 = jnp.float32
BF16 = jnp.bfloat16


def space_taps():
    offsets = np.arange(-RAD, RAD + 1).astype(np.float64)
    values = np.exp(-2.0 * offsets * offsets / (RAD * RAD))
    return values / np.sqrt(np.sum(values * values))


def time_taps():
    offsets = np.arange(-TAPS, TAPS + 1).astype(np.float64)
    values = np.exp(-2.0 * np.abs(offsets) / TAPS)
    return values / np.sqrt(np.sum(values * values))


def banded(distance, taps, reach):
    inside = np.abs(distance) <= reach
    return np.where(inside, taps[np.clip(distance, -reach, reach) + reach], 0.0)


def two_parts(matrix):
    high = matrix.astype(np.float32).astype(jnp.bfloat16)
    low = (matrix - high.astype(np.float64)).astype(np.float32).astype(jnp.bfloat16)
    return high, low


def constants(hours, rows, cols):
    space = space_taps()
    hour = np.arange(hours)
    time_high, time_low = two_parts(banded(hour[:, None] - hour[None, :], time_taps(), TAPS))
    col = np.arange(cols)
    col_high, col_low = two_parts(banded(col[:, None] - col[None, :], space, RAD))
    col_both = np.block([[col_high, col_low], [col_high, np.zeros_like(col_high)]])
    halo_col = np.concatenate([np.arange(-RAD, 0), np.arange(cols, cols + RAD)])
    edge = banded(halo_col[:, None] - col[None, :], space, RAD)

    def strips(row_of, halo_of, targets):
        by_row = banded(np.array(row_of)[:, None] - np.array(targets)[None, :], space, RAD)
        both = by_row[:, :, None] * edge[np.array(halo_of)][:, None, :]
        return two_parts(both.reshape(len(row_of), -1))

    own = [(row, side * RAD + j) for side in range(2) for row in range(rows) for j in range(RAD)]
    corner = [
        (row, side * RAD + j)
        for first in (-RAD, rows)
        for side in range(2)
        for row in range(first, first + RAD)
        for j in range(RAD)
    ]
    corner += [(-100, 0)] * (LANES - len(corner))
    edge_rows = list(range(RAD)) + list(range(rows - RAD, rows))
    own_parts = strips(*zip(*own), np.arange(rows))
    corner_parts = strips(*zip(*corner), np.array(edge_rows))
    return (time_high, time_low, col_both), own_parts, corner_parts


def split(value):
    high = value.astype(BF16)
    low = (value - high.astype(F32)).astype(BF16)
    return high, low


def dot(a, b):
    return jnp.dot(a, b, preferred_element_type=F32)


def lane_ids(shape):
    return lax.broadcasted_iota(jnp.int32, shape, 1)


def choose(flag, yes, no):
    return jnp.where(flag, yes, no)


def pack_strips(row_value, parity, rows):
    cols = row_value(0).shape[1]
    half = rows * RAD
    source = lax.broadcasted_iota(jnp.int32, (cols, 2 * half), 0)
    lane = lax.broadcasted_iota(jnp.int32, (cols, 2 * half), 1)
    first = lane < half
    j = lane & (RAD - 1)
    high_end = jnp.logical_xor(first, parity == 1)
    wanted = jnp.where(high_end, cols - RAD + j, j)
    lane_row = jnp.where(first, lane, lane - half) // RAD
    total = None
    for row in range(rows):
        high, low = split(row_value(row))
        pick = jnp.where((source == wanted) & (lane_row == row), 1.0, 0.0).astype(BF16)
        part = dot(jnp.concatenate([high, low], axis=1), jnp.concatenate([pick, pick], axis=0))
        total = part if total is None else total + part
    return total


def fold_hours(value, hours, strip_e, strip_o):
    fold = strip_e.shape[0]
    half = LANES // 2
    early = value[0:fold]
    late = jnp.concatenate([value[fold:hours], jnp.zeros((2 * fold - hours, LANES), F32)], axis=0)
    left = lane_ids((fold, LANES)) < half
    strip_e[...] = choose(left, early, pltpu.roll(late, half, 1))
    strip_o[...] = choose(left, pltpu.roll(early, half, 1), late)


def write_rows(parity, row_value, rows, rows_e, rows_o):
    top = rows - RAD

    def send(first, last):
        for row in range(RAD):
            rows_e[row] = row_value(first + row)
            rows_o[row] = row_value(last + row)

    @pl.when(parity == 0)
    def _():
        send(top, 0)

    @pl.when(parity == 1)
    def _():
        send(0, top)


def pack_kernel(par_ref, control_ref, rows_e, rows_o):
    rows = control_ref.shape[1]
    write_rows(par_ref[0], lambda r: control_ref[:, r, :] * CONTROL_FACTOR, rows, rows_e, rows_o)


def turn_kernel(par_ref, after, control_ref, field_ref, strip_e, strip_o):
    hours, rows, _ = control_ref.shape
    for row in range(rows):
        field_ref[row] = control_ref[:, row, :]
    fold_hours(pack_strips(lambda r: field_ref[r], par_ref[1], rows), hours, strip_e, strip_o)


def strip_kernel(par_ref, field_ref, strip_e, strip_o):
    rows, hours, _ = field_ref.shape
    fold_hours(pack_strips(lambda r: field_ref[r], par_ref[1], rows), hours, strip_e, strip_o)


def prepare_kernel(
    after_e, after_o, foot_ref, start_ref, row_ref, slot_ref, count_ref, out_ref, notes, sems, *, per,
):
    owners, lines, _ = foot_ref.shape
    slots = start_ref.shape[0]
    blocks = pltpu.make_async_copy(foot_ref, out_ref.at[:, 0:lines, :], sems.at[0])
    blocks.start()
    start = start_ref[...]
    valid = lax.broadcasted_iota(jnp.int32, start.shape, 0) < count_ref[...]
    lanes = jnp.concatenate(
        [start >> 4, start & 15, row_ref[...], jnp.where(valid, slot_ref[...], per)], axis=0
    ).astype(F32)
    wide = jnp.pad(lanes, ((0, LANES - 4 * slots), (0, LANES - owners)))
    turned = jnp.transpose(wide)[0:owners]
    notes[...] = jnp.broadcast_to(turned[:, None, :], notes.shape).astype(BF16)
    copy = pltpu.make_async_copy(notes, out_ref.at[:, lines : lines + SUB, :], sems.at[1])
    copy.start()
    copy.wait()
    blocks.wait()


def corner_kernel(par_ref, after, strip_e, strip_o, halo_ref, corner_e, corner_o):
    fold = strip_e.shape[0]
    quarter = corner_e.shape[0]
    half = LANES // 2
    part = RAD * RAD
    even, odd = strip_e[...], strip_o[...]
    is_even = par_ref[1] == 0
    prev, following = choose(is_even, odd, even), choose(is_even, even, odd)
    left = lane_ids((fold, LANES)) < half
    halo_ref[0:fold] = choose(left, prev, pltpu.roll(following, half, 1))
    halo_ref[fold : 2 * fold] = choose(left, pltpu.roll(prev, half, 1), following)
    lane = lane_ids((quarter, LANES))
    low = high = jnp.zeros((quarter, LANES), F32)
    for q in range(LANES // (2 * part)):
        piece = halo_ref[q * quarter : (q + 1) * quarter]
        base = q * 2 * part
        for side in range(2):
            here = (lane >= base + side * part) & (lane < base + (side + 1) * part)
            to = base + side * part
            low = choose(here, pltpu.roll(piece, (to - side * half) % LANES, 1), low)
            high = choose(here, pltpu.roll(piece, (to - side * half - (half - part)) % LANES, 1), high)
    rec_even = par_ref[0] == 0
    corner_e[...] = choose(rec_even, high, low)
    corner_o[...] = choose(rec_even, low, high)


def corner_strips(is_even, corner_e, corner_o):
    part = 2 * RAD * RAD
    prev = choose(is_even, corner_o[...], corner_e[...])
    following = choose(is_even, corner_e[...], corner_o[...])
    lane = lane_ids(prev.shape)
    pieces = []
    for q in range(LANES // part):
        a = prev if q == 0 else pltpu.roll(prev, LANES - q * part, 1)
        turn = (part - q * part) % LANES
        b = following if turn == 0 else pltpu.roll(following, turn, 1)
        pieces.append(choose(lane < part, a, choose(lane < 2 * part, b, 0.0)))
    return jnp.concatenate(pieces, axis=0)


def halo_sums(parts, high_ref, low_ref, first, width):
    high, both = parts
    weights = high_ref[:, first : first + width]
    return dot(both, jnp.concatenate([weights, weights], axis=0)) + dot(high, low_ref[:, first : first + width])


def halo_parts(value):
    high, low = split(value)
    return high, jnp.concatenate([high, low], axis=1)


def column_sums(value, col_both):
    cols = value.shape[1]
    high, low = split(value)
    out = dot(jnp.concatenate([high, low], axis=1), col_both)
    return out[:, :cols] + out[:, cols:]


def time_sums(value, time_high, time_low):
    high, low = split(value)
    return dot(time_high, high) + dot(time_high, low) + dot(time_low, high)


def row_sums(get, row, low, high, taps):
    total = None
    for distance in range(RAD + 1):
        here = [get(r) for r in sorted({row - distance, row + distance}) if low <= r < high]
        if not here:
            continue
        part = here[0] if len(here) == 1 else here[0] + here[1]
        part = float(taps[RAD + distance]) * part
        total = part if total is None else total + part
    return total


def local_kernel(after, field_ref, time_high, time_low, col_both, out_ref):
    rows, hours, cols = field_ref.shape
    taps = space_taps()
    for row in range(0, rows, 2):
        pair = [
            column_sums(row_sums(lambda i: field_ref[i], r, 0, rows, taps), col_both[...])
            for r in (row, row + 1)
        ]
        both = time_sums(jnp.concatenate(pair, axis=1), time_high[...], time_low[...])
        for k, r in enumerate((row, row + 1)):
            out_ref[r] = both[:, k * cols : (k + 1) * cols]


def strips_kernel(local_ref, halo_ref, time_high, time_low, own_high, own_low, out_ref, *, by_hour):
    rows, hours, cols = local_ref.shape
    halo = halo_parts(time_sums(halo_ref[0:hours, :], time_high[...], time_low[...]))
    for row in range(0, rows, 2):
        both = halo_sums(halo, own_high, own_low, row * cols, 2 * cols)
        for k, r in enumerate((row, row + 1)):
            part = local_ref[r] + both[:, k * cols : (k + 1) * cols]
            if by_hour:
                out_ref[:, r, :] = part
            else:
                out_ref[r] = part


def edge_parts(is_even, rows, got_e, got_o, corner_e, corner_o, consts, halo, factor):
    time_high, time_low, col_both, corner_high, corner_low = consts
    hours, cols = halo.shape[1:]
    taps = space_taps()
    for row in range(RAD):
        even, odd = got_e[row], got_o[row]
        halo[row] = choose(is_even, odd, even) * factor
        halo[RAD + row] = choose(is_even, even, odd) * factor
    corner = halo_parts(corner_strips(is_even, corner_e, corner_o)[0:hours])
    edge = list(range(RAD)) + list(range(rows - RAD, rows))
    for first in range(0, 2 * RAD, 2):
        pair = []
        for r in edge[first : first + 2]:
            if r < RAD:
                summed = row_sums(lambda i: halo[i + RAD], r, -RAD, 0, taps)
            else:
                summed = row_sums(lambda i: halo[RAD + i - rows], r, rows, rows + RAD, taps)
            pair.append(column_sums(summed, col_both[...]))
        value = jnp.concatenate(pair, axis=1)
        value = value + halo_sums(corner, corner_high, corner_low, first * cols, 2 * cols)
        both = time_sums(value, time_high[...], time_low[...])
        for k, r in enumerate(edge[first : first + 2]):
            yield r, both[:, k * cols : (k + 1) * cols]


def flux_kernel(local_ref, prior_ref, scale_ref, flux_ref, scale_out, wide):
    rows = local_ref.shape[0]
    wide[...] = scale_ref[...].astype(F32)
    for row in range(rows):
        scale_out[row] = wide[:, row, :]
    wide[...] = prior_ref[...].astype(F32)
    for row in range(rows):
        flux_ref[row] = wide[:, row, :] + scale_out[row] * local_ref[row]


def finish_kernel(
    par_ref, local_ref, factor_ref, got_e, got_o, corner_e, corner_o,
    time_high, time_low, col_both, corner_high, corner_low, out_ref, halo, edges, total, sems,
):
    hours, rows, cols = local_ref.shape
    consts = (time_high, time_low, col_both, corner_high, corner_low)
    factor = factor_ref[1:2, :]
    parts = edge_parts(par_ref[0] == 0, rows, got_e, got_o, corner_e, corner_o, consts, halo, factor)
    for k, (_, part) in enumerate(parts):
        edges[:, k, :] = part
    chunk = hours // PIECES
    first = lax.broadcasted_iota(jnp.int32, (chunk, 2 * RAD, cols), 1) < RAD
    copies = []
    for piece in range(PIECES):
        here = slice(piece * chunk, (piece + 1) * chunk)
        part = edges[here]
        low, high = slice(0, 2 * RAD), slice(rows - 2 * RAD, rows)
        total[here, low, :] = local_ref[here, low, :] + jnp.where(first, part, 0.0)
        total[here, high, :] = local_ref[here, high, :] + jnp.where(first, 0.0, part)
        copies.append(pltpu.make_async_copy(total.at[here], out_ref.at[here], sems.at[piece]))
        copies[-1].start()
    for copy in copies:
        copy.wait()


def blocks_of(foot_ref, source, heights, slots):
    for c in range(0, slots, 2):
        both = foot_ref[source, c * heights : (c + 2) * heights, :].astype(F32)
        yield c, both[0:heights]
        yield c + 1, both[heights : 2 * heights]


def forward_kernel(
    par_ref, foot_ref, own_ref, flux_hbm, scale_hbm, *refs, shift, slots, heights, tiles, per,
):
    far, near = refs[0:9], refs[11:20]
    out_ref, table_ref = refs[9:11]
    flux_ref, scale_ref, halo, sums, table_smem, sems = refs[20:]
    got_e, got_o, corner_e, corner_o = near[0:4]
    sources = foot_ref.shape[0]
    rows = flux_ref.shape[0]
    pairs = list(zip(far, near)) + [
        (scale_hbm.at[0:RAD], scale_ref.at[0:RAD]),
        (scale_hbm.at[rows - RAD : rows], scale_ref.at[RAD : 2 * RAD]),
        (flux_hbm, flux_ref),
    ]
    loads = [pltpu.make_async_copy(a, b, sems.at[i]) for i, (a, b) in enumerate(pairs)]
    for load in loads:
        load.start()
    groups = out_ref.shape[1] - 1
    base = slots * heights
    lane = lane_ids((sources, LANES))
    notes = foot_ref[:, base : base + SUB, :].astype(F32)[:, 0, :].astype(jnp.int32)
    start = notes * 16 + pltpu.roll(notes, LANES - slots, 1)
    offset = start + pltpu.roll(notes, LANES - 2 * slots, 1) * (1 << shift)
    source_rec = lax.broadcasted_iota(jnp.int32, (sources, LANES), 0) // tiles
    receptor = jnp.where(notes < per, source_rec * per + notes, groups * LANES)
    table = jnp.where(lane < slots, offset, receptor)
    table_ref[...] = table
    copy = pltpu.make_async_copy(table_ref, table_smem, sems.at[len(loads)])
    copy.start()
    for load in loads:
        load.wait()
    parts = edge_parts(
        par_ref[0] == 0, rows, got_e, got_o, corner_e, corner_o, near[4:], halo, 1.0 / CONTROL_FACTOR
    )
    for k, (row, part) in enumerate(parts):
        flux_ref[row] = flux_ref[row] + scale_ref[k] * part
    copy.wait()

    def body(source, carry):
        for c, block in blocks_of(foot_ref, source, heights, slots):
            offset = table_smem[source, c]
            row = lax.shift_right_logical(offset, shift)
            begin = jnp.bitwise_and(offset, (1 << shift) - 1)
            product = flux_ref[row, pl.ds(begin, heights), :] * block
            sums[c, pl.ds(source, 1), :] = jnp.sum(product, axis=0, keepdims=True)
        return carry

    lax.fori_loop(0, sources, body, 0)
    totals = [jnp.zeros((sources, LANES), F32) for _ in range(groups)]
    for c in range(slots):
        value = jnp.sum(sums[c], axis=1, keepdims=True)
        which = table[:, 3 * slots + c : 3 * slots + c + 1]
        for q in range(groups):
            totals[q] = totals[q] + jnp.where(which == lane + q * LANES, value, 0.0)
    for q in range(groups):
        total = jnp.sum(totals[q], axis=0, keepdims=True)
        out_ref[:, q : q + 1, :] = jnp.broadcast_to(total[None], (sources, 1, LANES))
    out_ref[:, groups : groups + 1, :] = jnp.broadcast_to(own_ref[...][None], (sources, 1, LANES))


def adjoint_kernel(
    par_ref, table_ref, got_ref, foot_ref, scale_ref,
    model_ref, factor_ref, field_ref, rows_e, rows_o,
    weight_vmem, weight_smem, sem, *, shift, slots, heights, tiles, per,
):
    sources = foot_ref.shape[0]
    groups = got_ref.shape[1] - 1
    rows, hours, _ = field_ref.shape
    model = jnp.sum(got_ref[:, 0:groups, :], axis=0)
    packed = LANES // per
    lane = lane_ids((1, LANES))
    own = jnp.zeros((1, LANES), F32)
    for q in range(groups):
        for k in range(packed):
            line = model[q : q + 1, :]
            line = line if k == 0 else pltpu.roll(line, LANES - k * per, 1)
            own = choose(par_ref[2] == q * packed + k, line, own)
    model_ref[...] = own[:, 0:per]
    weight_vmem[...] = jnp.zeros_like(weight_vmem)
    for q in range(groups):
        observed, error = jnp.zeros((1, LANES), F32), jnp.ones((1, LANES), F32)
        for k in range(packed):
            line = got_ref[(q * packed + k) * tiles, groups : groups + 1, :]
            here = (lane >= k * per) & (lane < (k + 1) * per)
            observed = jnp.where(here, line if k == 0 else pltpu.roll(line, k * per, 1), observed)
            turn = (k * per - per) % LANES
            error = jnp.where(here, line if turn == 0 else pltpu.roll(line, turn, 1), error)
        weight_vmem[q : q + 1, :] = (model[q : q + 1, :] - observed) / (error * error)
    copy = pltpu.make_async_copy(weight_vmem, weight_smem, sem)
    copy.start()
    field_ref[...] = jnp.zeros_like(field_ref)
    top = jnp.max(jnp.abs(weight_vmem[...]), keepdims=True) * (FOOT_MAX * SCALE_MAX * sources * slots)
    top = jnp.maximum(top, 1e-25)
    factor_ref[0:1, :] = jnp.broadcast_to(HALF_TOP / top, (1, LANES))
    factor_ref[1:2, :] = jnp.broadcast_to(top * (1.0 / HALF_TOP), (1, LANES))
    copy.wait()

    def body(source, carry):
        for c, block in blocks_of(foot_ref, source, heights, slots):
            offset = table_ref[source, c]
            receptor = table_ref[source, 3 * slots + c]
            row = lax.shift_right_logical(offset, shift)
            begin = jnp.bitwise_and(offset, (1 << shift) - 1)
            weight = weight_smem[lax.shift_right_logical(receptor, 7), jnp.bitwise_and(receptor, LANES - 1)]
            field_ref[row, pl.ds(begin, heights), :] += block * weight
        return carry

    lax.fori_loop(0, sources, body, 0)
    for row in range(rows):
        field_ref[row] = field_ref[row] * scale_ref[row]
    factor = factor_ref[0:1, :]
    write_rows(par_ref[0], lambda r: field_ref[r] * factor, rows, rows_e, rows_o)


def swap_pairs(count, odd):
    pairs = []
    for i in range(1 if odd else 0, count - 1, 2):
        pairs += [(i, i + 1), (i + 1, i)]
    return pairs


def swap(axis, even, odd):
    count = lax.axis_size(axis)
    return (
        lax.ppermute(even, axis, swap_pairs(count, False)),
        lax.ppermute(odd, axis, swap_pairs(count, True)),
    )


SM = pl.BlockSpec(memory_space=pltpu.SMEM)
VM = pl.BlockSpec(memory_space=pltpu.VMEM)
HB = pl.BlockSpec(memory_space=pltpu.HBM)


def call(kernel, out_shape, in_specs, scratch, name, out_specs=None):
    return pl.pallas_call(
        kernel,
        out_shape=out_shape,
        in_specs=in_specs,
        out_specs=jax.tree.map(lambda _: VM, out_shape) if out_specs is None else out_specs,
        scratch_shapes=scratch,
        compiler_params=pltpu.CompilerParams(vmem_limit_bytes=VMEM_LIMIT),
        name=name,
    )


def array(*shape):
    return jax.ShapeDtypeStruct(shape, F32)


def per_device(
    prior_flux,
    flux_scale,
    control,
    footprint,
    slot_count,
    start_hour,
    grid_row,
    receptor_slot,
    observed,
    obs_error,
):
    hours, rows, cols = control.shape
    n_rec, n_tile = lax.axis_size("rec"), lax.axis_size("tile")
    devices = n_rec * n_tile
    slots, heights = footprint.shape[1], footprint.shape[2]
    per = observed.shape[0]
    groups = per * n_rec // LANES
    shift = (hours - 1).bit_length()
    rec, tile = lax.axis_index("rec"), lax.axis_index("tile")
    par = jnp.stack([rec % 2, tile % 2, rec]).astype(jnp.int32)
    base, own_parts, corner_parts = constants(hours, rows, cols)
    base = [jnp.asarray(c) for c in base]
    own_parts = [jnp.asarray(c) for c in own_parts]
    corner_parts = [jnp.asarray(c) for c in corner_parts]
    fold = -(-hours // (2 * 64)) * 64
    strip, corner = array(fold, LANES), array(fold // 2, LANES)
    block = array(RAD, hours, cols)
    field_shape = array(rows, hours, cols)
    halo_scratch = pltpu.VMEM((2 * RAD, hours, cols), F32)

    def half(rows_e, rows_o):
        return rows_e.astype(F16), rows_o.astype(F16)

    def rows_of(rows_e, rows_o):
        return [r.astype(F32) for r in swap("rec", rows_e, rows_o)]

    def sides(after, strip_e, strip_o):
        got_strips = swap("tile", strip_e, strip_o)
        halo, corner_e, corner_o = call(
            corner_kernel, [array(2 * fold, LANES), corner, corner], [SM, VM, VM, VM], [], "corners"
        )(par, after, *got_strips)
        return halo, swap("rec", corner_e, corner_o)

    def inner_sums(field, strip_e, strip_o, by_hour, name):
        def second(*refs):
            strips_kernel(*refs, by_hour=by_hour)

        local = call(local_kernel, field_shape, [VM] * 5, [], name + "_local")(strip_e, field, *base)
        halo, got_corners = sides(local, strip_e, strip_o)
        shape = array(hours, rows, cols) if by_hour else field_shape
        local = call(second, shape, [VM] * 6, [], name + "_strips")(local, halo, *base[:2], *own_parts)
        return local, got_corners

    def prepare(*refs):
        prepare_kernel(*refs, per=per)

    rows_e, rows_o = call(pack_kernel, [block, block], [SM, VM], [], "pack_control")(par, control)
    sent = call(
        prepare,
        jax.ShapeDtypeStruct((devices, slots * heights + SUB, cols), BF16),
        [VM] * 7,
        [pltpu.VMEM((devices, SUB, LANES), BF16), pltpu.SemaphoreType.DMA((2,))],
        "prepare_blocks",
        out_specs=HB,
    )(
        rows_e, rows_o, footprint.reshape(devices, slots * heights, cols),
        start_hour.T, grid_row.T, receptor_slot.T, slot_count[None],
    )
    foot = lax.all_to_all(sent, AXES, split_axis=0, concat_axis=0, tiled=True)
    got_rows = rows_of(*half(rows_e, rows_o))
    field, *strips = call(
        turn_kernel, [field_shape, strip, strip], [SM, HB, VM], [], "turn_control"
    )(par, sent, control)
    local, got_corners = inner_sums(field, *strips, False, "control")
    flux, scale = call(
        flux_kernel, [field_shape, field_shape], [VM] * 3, [pltpu.VMEM((hours, rows, cols), F32)], "flux_inner"
    )(local, prior_flux, flux_scale)

    own = jnp.concatenate([observed, obs_error, jnp.zeros((LANES - 2 * per,), F32)])[None]
    sizes = dict(shift=shift, slots=slots, heights=heights, tiles=n_tile, per=per)

    def forward(*refs):
        forward_kernel(*refs, **sizes)

    needed = [*got_rows, *got_corners, *base, *corner_parts]
    partial, table = call(
        forward,
        [array(devices, groups + 1, LANES), jax.ShapeDtypeStruct((devices, LANES), jnp.int32)],
        [SM, VM, VM] + [HB] * 11,
        [pltpu.VMEM(x.shape, x.dtype) for x in needed]
        + [pltpu.VMEM((rows, hours, cols), F32), halo_scratch, halo_scratch]
        + [
            pltpu.VMEM((slots, devices, LANES), F32),
            pltpu.SMEM((devices, LANES), jnp.int32),
            pltpu.SemaphoreType.DMA((len(needed) + 4,)),
        ],
        "block_values",
    )(par, foot, own, *[pltpu.with_memory_space_constraint(x, pltpu.HBM) for x in (flux, scale, *needed)])
    everyone = lax.all_to_all(partial, AXES, split_axis=0, concat_axis=0, tiled=True)

    def adjoint(*refs):
        adjoint_kernel(*refs, **sizes)

    weight_rows = -(-(groups + 1) // SUB) * SUB
    model_co2, factor, field, rows_e, rows_o = call(
        adjoint,
        [array(1, per), array(2, LANES), field_shape, block, block],
        [SM, SM, VM, VM, VM],
        [
            pltpu.VMEM((weight_rows, LANES), F32),
            pltpu.SMEM((weight_rows, LANES), F32),
            pltpu.SemaphoreType.DMA,
        ],
        "adjoint_field",
    )(par, table, everyone, foot, scale)
    got_rows = rows_of(*half(rows_e, rows_o))
    strips = call(strip_kernel, [strip, strip], [SM, VM], [], "pack_strips")(par, field)
    local, got_corners = inner_sums(field, *strips, True, "gradient")
    gradient = call(
        finish_kernel,
        array(hours, rows, cols),
        [SM] + [VM] * 11,
        [
            halo_scratch,
            pltpu.VMEM((hours, 2 * RAD, cols), F32),
            pltpu.VMEM((hours, rows, cols), F32),
            pltpu.SemaphoreType.DMA((PIECES,)),
        ],
        "gradient",
        out_specs=HB,
    )(par, local, factor, *got_rows, *got_corners, *base, *corner_parts)
    return (model_co2.reshape(-1), gradient)


def solution(mesh):
    return jax.shard_map(
        per_device,
        mesh=mesh,
        in_specs=(
            P(None, "rec", "tile"),
            P(None, "rec", "tile"),
            P(None, "rec", "tile"),
            P(("rec", "tile"), None, None, None),
            P(("rec", "tile")),
            P(("rec", "tile"), None),
            P(("rec", "tile"), None),
            P(("rec", "tile"), None),
            P("rec"),
            P("rec"),
        ),
        out_specs=(P("rec"), P(None, "rec", "tile")),
        check_vma=False,
    )
```

```python
import numpy as np
import jax
import jax.numpy as jnp
from jax import lax
from jax.experimental import pallas as pl
from jax.experimental.pallas import tpu as pltpu
from jax.sharding import PartitionSpec as P

RAD = 4
TAPS = 12
AXES = ("rec", "tile")
LANES = 128
SUB = 8
FOOT_MAX = 0.02
PARTS = 4
SCALE_MAX = 2.0
HALF_TOP = 32768.0
CONTROL_FACTOR = 4096.0
F16 = jnp.float16
VMEM_LIMIT = 14 * 1024 * 1024
F32 = jnp.float32
BF16 = jnp.bfloat16


def space_taps():
    offsets = np.arange(-RAD, RAD + 1).astype(np.float64)
    values = np.exp(-2.0 * offsets * offsets / (RAD * RAD))
    return values / np.sqrt(np.sum(values * values))


def time_taps():
    offsets = np.arange(-TAPS, TAPS + 1).astype(np.float64)
    values = np.exp(-2.0 * np.abs(offsets) / TAPS)
    return values / np.sqrt(np.sum(values * values))


def banded(distance, taps, reach):
    inside = np.abs(distance) <= reach
    return np.where(inside, taps[np.clip(distance, -reach, reach) + reach], 0.0)


def two_parts(matrix):
    high = matrix.astype(np.float32).astype(jnp.bfloat16)
    low = (matrix - high.astype(np.float64)).astype(np.float32).astype(jnp.bfloat16)
    return high, low


def constants(hours, rows, cols):
    space = space_taps()
    hour = np.arange(hours)
    time_high, time_low = two_parts(banded(hour[:, None] - hour[None, :], time_taps(), TAPS))
    col = np.arange(cols)
    col_high, col_low = two_parts(banded(col[:, None] - col[None, :], space, RAD))
    col_both = np.block([[col_high, col_low], [col_high, np.zeros_like(col_high)]])
    halo_col = np.concatenate([np.arange(-RAD, 0), np.arange(cols, cols + RAD)])
    edge = banded(halo_col[:, None] - col[None, :], space, RAD)

    def strips(row_of, halo_of, targets):
        by_row = banded(np.array(row_of)[:, None] - np.array(targets)[None, :], space, RAD)
        both = by_row[:, :, None] * edge[np.array(halo_of)][:, None, :]
        return two_parts(both.reshape(len(row_of), -1))

    unused = [(-100, 0)] * (LANES - RAD * rows)
    own = []
    for side in range(2):
        own += [(row, side * RAD + j) for row in range(rows) for j in range(RAD)] + unused
    corner = [], []
    for first, targets in ((rows, rows - 1 - np.arange(RAD)), (-RAD, np.arange(RAD))):
        lanes = [
            (row, side * RAD + j) for side in range(2) for row in range(first, first + RAD) for j in range(RAD)
        ]
        lanes += [(-100, 0)] * (LANES - len(lanes))
        for part, value in zip(corner, strips(*zip(*lanes), targets)):
            part.append(value)
    return (time_high, time_low, col_both), strips(*zip(*own), np.arange(rows)), [np.stack(c) for c in corner]


def split(value):
    high = value.astype(BF16)
    low = (value - high.astype(F32)).astype(BF16)
    return high, low


def dot(a, b):
    return jnp.dot(a, b, preferred_element_type=F32)


def lane_ids(shape):
    return lax.broadcasted_iota(jnp.int32, shape, 1)


def choose(flag, yes, no):
    return jnp.where(flag, yes, no)


def pack_strips(row_value, odd, rows):
    cols = row_value(0).shape[1]
    half = rows * RAD
    source = lax.broadcasted_iota(jnp.int32, (cols, 2 * half), 0)
    lane = lane_ids((cols, 2 * half))
    first = lane < half
    j = lane & (RAD - 1)
    at_first, at_second = choose(odd, j, cols - RAD + j), choose(odd, cols - RAD + j, j)
    wanted = jnp.where(first, at_first, at_second)
    lane_row = jnp.where(first, lane, lane - half) // RAD
    total = None
    for row in range(rows):
        high, low = split(row_value(row))
        pick = jnp.where((source == wanted) & (lane_row == row), 1.0, 0.0).astype(BF16)
        part = dot(jnp.concatenate([high, low], axis=1), jnp.concatenate([pick, pick], axis=0))
        total = part if total is None else total + part
    return total


def fold_corners(odd, strips, corner_e, corner_o):
    quarter = corner_e.shape[0]
    half, part = LANES // 2, RAD * RAD
    lane = lane_ids((quarter, LANES))
    spare = jnp.zeros((4 * quarter - strips.shape[0], LANES), F32)
    whole = jnp.concatenate([strips, spare], axis=0)
    low = high = jnp.zeros((quarter, LANES), F32)
    for q in range(LANES // (2 * part)):
        piece = whole[q * quarter : (q + 1) * quarter]
        for side in range(2):
            to = q * 2 * part + side * part
            here = (lane >= to) & (lane < to + part)
            low = choose(here, pltpu.roll(piece, (to - side * half) % LANES, 1), low)
            high = choose(here, pltpu.roll(piece, (to - side * half - (half - part)) % LANES, 1), high)
    corner_e[...] = choose(odd, low, high)
    corner_o[...] = choose(odd, high, low)


def unfold_corners(value):
    part = 2 * RAD * RAD
    pieces = [value] + [pltpu.roll(value, LANES - q * part, 1) for q in range(1, LANES // part)]
    return jnp.concatenate(pieces, axis=0)


def is_odd(par_ref, axis):
    return par_ref[axis : axis + 1, :] == 1


def write_rows(odd, row_value, rows, rows_e, rows_o):
    for row in range(RAD):
        first, last = row_value(row), row_value(rows - 1 - row)
        rows_e[row] = choose(odd, first, last)
        rows_o[row] = choose(odd, last, first)


def turn_kernel(par_ref, after, control_ref, field_ref, strip_e, strip_o):
    rows = control_ref.shape[1]
    for row in range(rows):
        field_ref[row] = control_ref[:, row, :]
    write_strips(is_odd(par_ref, 1), field_ref, strip_e, strip_o)


def strip_kernel(par_ref, after_e, after_o, field_ref, strip_e, strip_o):
    write_strips(is_odd(par_ref, 1), field_ref, strip_e, strip_o)


def write_strips(odd, field_ref, strip_e, strip_o):
    strips = pack_strips(lambda r: field_ref[r], odd, field_ref.shape[0])
    half = LANES // 2
    left = lane_ids(strips.shape) < half
    strip_e[...] = jnp.where(left, strips, 0.0)
    strip_o[...] = jnp.where(left, pltpu.roll(strips, half, 1), 0.0)


def far_corner_kernel(par_ref, after, strip_e, strip_o, corner_e, corner_o):
    odd = is_odd(par_ref, 1)
    even_swap, odd_swap = strip_e[...], strip_o[...]
    before, after = choose(odd, even_swap, odd_swap), choose(odd, odd_swap, even_swap)
    half = LANES // 2
    both = jnp.where(lane_ids(before.shape) < half, before, pltpu.roll(after, half, 1))
    fold_corners(is_odd(par_ref, 0), both, corner_e, corner_o)


def rows_kernel(par_ref, factor_ref, field_ref, rows_e, rows_o):
    factor = factor_ref[0:1, :]
    write_rows(is_odd(par_ref, 0), lambda r: field_ref[r] * factor, field_ref.shape[0], rows_e, rows_o)


def prepare_kernel(
    foot_ref, start_ref, row_ref, slot_ref, count_ref, out_ref,
    wide_ref, start_vmem, row_vmem, slot_vmem, count_vmem, sems, *, per,
):
    owners, lines, _ = foot_ref.shape
    slots = start_ref.shape[0]
    pairs = ((start_ref, start_vmem), (row_ref, row_vmem), (slot_ref, slot_vmem), (count_ref, count_vmem))
    small = [pltpu.make_async_copy(a, b, sems.at[i]) for i, (a, b) in enumerate(pairs)]
    chunk = owners // PARTS
    parts = [slice(i * chunk, (i + 1) * chunk) for i in range(PARTS)]
    loads = [
        pltpu.make_async_copy(foot_ref.at[here], wide_ref.at[here, 0:lines, :], sems.at[4 + i])
        for i, here in enumerate(parts)
    ]
    for copy in small + loads:
        copy.start()
    for copy in small:
        copy.wait()
    start = start_vmem[...]
    valid = lax.broadcasted_iota(jnp.int32, start.shape, 0) < count_vmem[...]
    lanes = jnp.concatenate(
        [start >> 4, start & 15, row_vmem[...], jnp.where(valid, slot_vmem[...], per)], axis=0
    ).astype(F32)
    wide = jnp.pad(lanes, ((0, LANES - 4 * slots), (0, LANES - owners)))
    turned = jnp.transpose(wide)[0:owners]
    notes = jnp.broadcast_to(turned[:, None, :], (owners, SUB, LANES)).astype(BF16)
    wide_ref[:, lines : lines + SUB, :] = notes
    stores = []
    for i, here in enumerate(parts):
        loads[i].wait()
        stores.append(pltpu.make_async_copy(wide_ref.at[here], out_ref.at[here], sems.at[4 + PARTS + i]))
        stores[-1].start()
    for copy in stores:
        copy.wait()


def halo_sums(parts, high_ref, low_ref, first, width):
    high, low = parts
    weights = high_ref[:, first : first + width]
    return dot(high, weights) + dot(low, weights) + dot(high, low_ref[:, first : first + width])


def column_sums(value, col_both):
    cols = value.shape[1]
    high, low = split(value)
    out = dot(jnp.concatenate([high, low], axis=1), col_both)
    return out[:, :cols] + out[:, cols:]


def time_sums(value, time_high, time_low):
    high, low = split(value)
    return dot(time_high, high) + dot(time_high, low) + dot(time_low, high)


def row_sums(get, row, low, high, taps):
    total = None
    for distance in range(RAD + 1):
        here = [get(r) for r in sorted({row - distance, row + distance}) if low <= r < high]
        if not here:
            continue
        part = here[0] if len(here) == 1 else here[0] + here[1]
        part = float(taps[RAD + distance]) * part
        total = part if total is None else total + part
    return total


def local_kernel(after, field_ref, time_high, time_low, col_both, out_ref):
    rows, hours, cols = field_ref.shape
    taps = space_taps()
    for row in range(0, rows, 2):
        pair = [
            column_sums(row_sums(lambda i: field_ref[i], r, 0, rows, taps), col_both[...])
            for r in (row, row + 1)
        ]
        both = time_sums(jnp.concatenate(pair, axis=1), time_high[...], time_low[...])
        for k, r in enumerate((row, row + 1)):
            out_ref[r] = both[:, k * cols : (k + 1) * cols]


def strips_kernel(par_ref, local_ref, strip_e, strip_o, time_high, time_low, own_high, own_low, out_ref, *, by_hour):
    rows, hours, cols = local_ref.shape
    odd = is_odd(par_ref, 1)
    even_swap, odd_swap = strip_e[...], strip_o[...]
    halo = jnp.concatenate([choose(odd, even_swap, odd_swap), choose(odd, odd_swap, even_swap)], axis=1)
    halo = split(time_sums(halo, time_high[...], time_low[...]))
    for row in range(0, rows, 2):
        both = halo_sums(halo, own_high, own_low, row * cols, 2 * cols)
        for k, r in enumerate((row, row + 1)):
            part = local_ref[r] + both[:, k * cols : (k + 1) * cols]
            if by_hour:
                out_ref[:, r, :] = part
            else:
                out_ref[r] = part


def edge_parts(odd, rows, first, got_e, got_o, consts, halo, factor, corner=None):
    time_high, time_low, col_both = consts
    taps = space_taps()
    for row in range(RAD):
        even, other = got_e[row], got_o[row]
        halo[row] = (choose(odd, even, other) if first else choose(odd, other, even)) * factor
    parts = []
    for k in range(0, RAD, 2):
        pair = []
        for i in (k, k + 1):
            if first:
                summed = row_sums(lambda r: halo[r + RAD], i, -RAD, 0, taps)
            else:
                summed = row_sums(lambda r: halo[r - RAD], i, RAD, 2 * RAD, taps)
            pair.append(column_sums(summed, col_both[...]))
        value = jnp.concatenate(pair, axis=1)
        width = value.shape[1]
        if corner is not None:
            parts_of, high, low = corner
            at = (k if first else RAD + k) * (width // 2)
            value = value + halo_sums(parts_of, high, low, at, width)
        both = time_sums(value, time_high[...], time_low[...])
        half = width // 2
        parts += [both[:, :half], both[:, half:]]
    return parts


def edge_parts(halo, corner, corner_high, corner_low, consts):
    time_high, time_low, col_both = consts
    hours, cols = halo.shape[1:]
    taps = space_taps()
    corner = split(unfold_corners(corner)[0:hours])
    parts = []
    for k in range(0, RAD, 2):
        pair = []
        for i in (k, k + 1):
            summed = None
            for j in range(RAD - i):
                part = float(taps[RAD + i + j + 1]) * halo[j]
                summed = part if summed is None else summed + part
            pair.append(column_sums(summed, col_both[...]))
        value = jnp.concatenate(pair, axis=1) + halo_sums(corner, corner_high, corner_low, k * cols, 2 * cols)
        both = time_sums(value, time_high[...], time_low[...])
        parts += [both[:, :cols], both[:, cols:]]
    return parts


def flux_kernel(
    par_ref, local_ref, prior_ref, scale_ref, got_ref, corner_ref,
    time_high, time_low, col_both, corner_high, corner_low, flux_ref, scale_out, wide, halo,
):
    rows = local_ref.shape[0]
    odd = par_ref[0, 0]
    wide[...] = scale_ref[...].astype(F32)
    for row in range(rows):
        scale_out[row] = wide[:, row, :]
    wide[...] = prior_ref[...].astype(F32)
    for row in range(rows):
        flux_ref[row] = wide[:, row, :] + scale_out[row] * local_ref[row]
    halo[...] = got_ref[...] * (1.0 / CONTROL_FACTOR)
    consts = (time_high, time_low, col_both)
    parts = edge_parts(halo, corner_ref[...], corner_high.at[odd], corner_low.at[odd], consts)
    for k, part in enumerate(parts):
        row = jnp.where(odd == 1, k, rows - 1 - k)
        flux_ref[row] = flux_ref[row] + scale_out[row] * part


def finish_kernel(
    par_ref, local_ref, factor_ref, got_e, got_o, corner_e, corner_o,
    time_high, time_low, col_both, corner_high, corner_low, out_ref, halo, edges, total, sems,
):
    hours, rows, cols = local_ref.shape
    odd = is_odd(par_ref, 0)
    factor = factor_ref[1:2, :]
    consts = (time_high, time_low, col_both)
    inside = lax.broadcasted_iota(jnp.int32, (hours, 2 * RAD, cols), 1)
    copies = []
    for side in range(2):
        before = side == 0
        for k in range(RAD):
            even, other = got_e[k], got_o[k]
            halo[side, k] = (choose(odd, even, other) if before else choose(odd, other, even)) * factor
        even, other = corner_e[...], corner_o[...]
        corner = choose(odd, even, other) if before else choose(odd, other, even)
        which = 1 - side
        parts = edge_parts(halo.at[side], corner, corner_high.at[which], corner_low.at[which], consts)
        for k, part in enumerate(parts):
            edges[:, k if before else 2 * RAD - 1 - k, :] = part
        here = slice(0, 2 * RAD) if before else slice(rows - 2 * RAD, rows)
        mine = inside < RAD if before else inside >= RAD
        total[:, here, :] = local_ref[:, here, :] + jnp.where(mine, edges[...], 0.0)
        copies.append(pltpu.make_async_copy(total.at[:, here, :], out_ref.at[:, here, :], sems.at[side]))
        copies[-1].start()
    for copy in copies:
        copy.wait()


def blocks_of(foot_ref, source, heights, slots):
    for c in range(0, slots, 2):
        both = foot_ref[source, c * heights : (c + 2) * heights, :].astype(F32)
        yield c, both[0:heights]
        yield c + 1, both[heights : 2 * heights]


def forward_kernel(
    par_ref, foot_ref, own_ref, got_ref, flux_hbm, scale_hbm, *refs, shift, slots, heights, tiles, per,
):
    distant, near = refs[0:6], refs[8:14]
    out_ref, table_ref = refs[6:8]
    flux_ref, scale_ref, halo, edges, sums, table_smem, sems = refs[14:]
    corner_ref, *consts, corner_high, corner_low = near
    odd = par_ref[0, 0]
    sources = foot_ref.shape[0]
    rows = flux_ref.shape[0]
    first = (rows - RAD) * odd
    pairs = list(zip(distant, near)) + [(scale_hbm.at[pl.ds(first, RAD)], scale_ref), (flux_hbm, flux_ref)]
    loads = [pltpu.make_async_copy(a, b, sems.at[i]) for i, (a, b) in enumerate(pairs)]
    for load in loads:
        load.start()
    groups = out_ref.shape[1] - 1
    base = slots * heights
    lane = lane_ids((sources, LANES))
    notes = foot_ref[:, base : base + SUB, :].astype(F32)[:, 0, :].astype(jnp.int32)
    start = notes * 16 + pltpu.roll(notes, LANES - slots, 1)
    offset = start + pltpu.roll(notes, LANES - 2 * slots, 1) * (1 << shift)
    source_rec = lax.broadcasted_iota(jnp.int32, (sources, LANES), 0) // tiles
    receptor = jnp.where(notes < per, source_rec * per + notes, groups * LANES)
    table = jnp.where(lane < slots, offset, receptor)
    table_ref[...] = table
    copy = pltpu.make_async_copy(table_ref, table_smem, sems.at[len(loads)])
    copy.start()
    for load in loads[:-2]:
        load.wait()
    halo[...] = got_ref[...] * (1.0 / CONTROL_FACTOR)
    parts = edge_parts(halo, corner_ref[...], corner_high.at[1 - odd], corner_low.at[1 - odd], consts)
    for k, part in enumerate(parts):
        edges[k] = part
    for load in loads[-2:]:
        load.wait()
    for k in range(RAD):
        line = jnp.where(odd == 1, RAD - 1 - k, k)
        flux_ref[first + line] = flux_ref[first + line] + scale_ref[line] * edges[k]
    copy.wait()

    def body(source, carry):
        for c, block in blocks_of(foot_ref, source, heights, slots):
            offset = table_smem[source, c]
            row = lax.shift_right_logical(offset, shift)
            begin = jnp.bitwise_and(offset, (1 << shift) - 1)
            product = flux_ref[row, pl.ds(begin, heights), :] * block
            sums[c, pl.ds(source, 1), :] = jnp.sum(product, axis=0, keepdims=True)
        return carry

    lax.fori_loop(0, sources, body, 0)
    totals = [jnp.zeros((sources, LANES), F32) for _ in range(groups)]
    for c in range(slots):
        value = jnp.sum(sums[c], axis=1, keepdims=True)
        which = table[:, 3 * slots + c : 3 * slots + c + 1]
        for q in range(groups):
            totals[q] = totals[q] + jnp.where(which == lane + q * LANES, value, 0.0)
    for q in range(groups):
        total = jnp.sum(totals[q], axis=0, keepdims=True)
        out_ref[:, q : q + 1, :] = jnp.broadcast_to(total[None], (sources, 1, LANES))
    out_ref[:, groups : groups + 1, :] = jnp.broadcast_to(own_ref[...][None], (sources, 1, LANES))


def adjoint_kernel(
    par_ref, table_vmem, got_ref, foot_ref, scale_ref,
    model_ref, factor_ref, field_ref,
    weight_vmem, weight_smem, table_ref, sems, *, shift, slots, heights, tiles, per,
):
    load = pltpu.make_async_copy(table_vmem, table_ref, sems.at[1])
    load.start()
    sources = foot_ref.shape[0]
    groups = got_ref.shape[1] - 1
    rows, hours, _ = field_ref.shape
    model = jnp.sum(got_ref[:, 0:groups, :], axis=0)
    packed = LANES // per
    lane = lane_ids((1, LANES))
    own = jnp.zeros((1, LANES), F32)
    for q in range(groups):
        for k in range(packed):
            line = model[q : q + 1, :]
            line = line if k == 0 else pltpu.roll(line, LANES - k * per, 1)
            own = choose(par_ref[2:3, :] == q * packed + k, line, own)
    model_ref[...] = own[:, 0:per]
    weight_vmem[...] = jnp.zeros_like(weight_vmem)
    for q in range(groups):
        observed, error = jnp.zeros((1, LANES), F32), jnp.ones((1, LANES), F32)
        for k in range(packed):
            line = got_ref[(q * packed + k) * tiles, groups : groups + 1, :]
            here = (lane >= k * per) & (lane < (k + 1) * per)
            observed = jnp.where(here, line if k == 0 else pltpu.roll(line, k * per, 1), observed)
            turn = (k * per - per) % LANES
            error = jnp.where(here, line if turn == 0 else pltpu.roll(line, turn, 1), error)
        weight_vmem[q : q + 1, :] = (model[q : q + 1, :] - observed) / (error * error)
    copy = pltpu.make_async_copy(weight_vmem, weight_smem, sems.at[0])
    copy.start()
    field_ref[...] = jnp.zeros_like(field_ref)
    top = jnp.max(jnp.abs(weight_vmem[...]), keepdims=True) * (FOOT_MAX * SCALE_MAX * sources * slots)
    top = jnp.maximum(top, 1e-25)
    factor_ref[0:1, :] = jnp.broadcast_to(HALF_TOP / top, (1, LANES))
    factor_ref[1:2, :] = jnp.broadcast_to(top * (1.0 / HALF_TOP), (1, LANES))
    load.wait()
    copy.wait()

    def body(source, carry):
        for c, block in blocks_of(foot_ref, source, heights, slots):
            offset = table_ref[source, c]
            receptor = table_ref[source, 3 * slots + c]
            row = lax.shift_right_logical(offset, shift)
            begin = jnp.bitwise_and(offset, (1 << shift) - 1)
            weight = weight_smem[lax.shift_right_logical(receptor, 7), jnp.bitwise_and(receptor, LANES - 1)]
            field_ref[row, pl.ds(begin, heights), :] += block * weight
        return carry

    lax.fori_loop(0, sources, body, 0)
    for row in range(rows):
        field_ref[row] = field_ref[row] * scale_ref[row]


def swap_pairs(count, odd):
    pairs = []
    for i in range(1 if odd else 0, count - 1, 2):
        pairs += [(i, i + 1), (i + 1, i)]
    return pairs


def swap(axis, even, odd):
    count = lax.axis_size(axis)
    return (
        lax.ppermute(even, axis, swap_pairs(count, False)),
        lax.ppermute(odd, axis, swap_pairs(count, True)),
    )


VM = pl.BlockSpec(memory_space=pltpu.VMEM)
HB = pl.BlockSpec(memory_space=pltpu.HBM)


def call(kernel, out_shape, in_specs, scratch, name, out_specs=None):
    return pl.pallas_call(
        kernel,
        out_shape=out_shape,
        in_specs=in_specs,
        out_specs=jax.tree.map(lambda _: VM, out_shape) if out_specs is None else out_specs,
        scratch_shapes=scratch,
        compiler_params=pltpu.CompilerParams(vmem_limit_bytes=VMEM_LIMIT),
        name=name,
    )


def far(x):
    return pltpu.with_memory_space_constraint(x, pltpu.HBM)


def array(*shape):
    return jax.ShapeDtypeStruct(shape, F32)


def per_device(
    prior_flux,
    flux_scale,
    control,
    footprint,
    slot_count,
    start_hour,
    grid_row,
    receptor_slot,
    observed,
    obs_error,
):
    hours, rows, cols = control.shape
    n_rec, n_tile = lax.axis_size("rec"), lax.axis_size("tile")
    devices = n_rec * n_tile
    slots, heights = footprint.shape[1], footprint.shape[2]
    per = observed.shape[0]
    groups = per * n_rec // LANES
    shift = (hours - 1).bit_length()
    rec, tile = lax.axis_index("rec"), lax.axis_index("tile")
    par = jnp.stack([rec % 2, tile % 2, rec] + [rec * 0] * (SUB - 3)).astype(jnp.int32)
    par = jnp.broadcast_to(par[:, None], (SUB, LANES))
    base, own_parts, corner_parts = constants(hours, rows, cols)
    base = [jnp.asarray(c) for c in base]
    own_parts = [jnp.asarray(c) for c in own_parts]
    corner_parts = [jnp.asarray(c) for c in corner_parts]
    strip = array(hours, LANES)
    corner = array(-(-hours // (4 * SUB)) * SUB, LANES)
    block = array(RAD, hours, cols)
    field_shape = array(rows, hours, cols)
    row_scratch = pltpu.VMEM((RAD, hours, cols), F32)

    def half(rows_e, rows_o):
        return rows_e.astype(F16), rows_o.astype(F16)

    def inner_sums(field, sent, by_hour, name):
        def second(*refs):
            strips_kernel(*refs, by_hour=by_hour)

        got_strips = swap("tile", *sent)
        local = call(local_kernel, field_shape, [VM] * 5, [], name + "_local")(sent[0], field, *base)
        shape = array(hours, rows, cols) if by_hour else field_shape
        corners = call(far_corner_kernel, [corner, corner], [VM] * 4, [], name + "_corners")(par, local, *got_strips)
        got_corners = swap("rec", *corners)
        local = call(second, shape, [VM] * 8, [], name + "_strips")(
            par, local, *got_strips, *base[:2], *own_parts
        )
        return local, got_corners

    def pack_rows(factor, field, name):
        sent = call(rows_kernel, [block, block], [VM] * 3, [], name)(par, factor, field)
        return sent, swap("rec", *half(*sent))

    def prepare(*refs):
        prepare_kernel(*refs, per=per)

    numbers = pltpu.VMEM((slots, devices), jnp.int32)
    lines = slots * heights + SUB
    sent = call(
        prepare,
        jax.ShapeDtypeStruct((devices, lines, cols), BF16),
        [HB] * 5,
        [
            pltpu.VMEM((devices, lines, cols), BF16),
            numbers, numbers, numbers, pltpu.VMEM((1, devices), jnp.int32),
            pltpu.SemaphoreType.DMA((4 + 2 * PARTS,)),
        ],
        "prepare_blocks",
        out_specs=HB,
    )(*[
        far(x)
        for x in (
            footprint.reshape(devices, slots * heights, cols),
            start_hour.T, grid_row.T, receptor_slot.T, slot_count[None],
        )
    ])
    foot = lax.all_to_all(sent, AXES, split_axis=0, concat_axis=0, tiled=True)
    field, *strips = call(
        turn_kernel, [field_shape, strip, strip], [VM, HB, VM], [], "turn_control"
    )(par, sent, control)
    _, got_rows = pack_rows(jnp.full((2, LANES), CONTROL_FACTOR, F32), field, "control_rows")
    local, got_corners = inner_sums(field, strips, False, "control")
    flux, scale = call(
        flux_kernel,
        [field_shape, field_shape],
        [VM] * 11,
        [pltpu.VMEM((hours, rows, cols), F32), row_scratch],
        "flux_field",
    )(par, local, prior_flux, flux_scale, got_rows[0].astype(F32), got_corners[0], *base, *corner_parts)

    own = jnp.concatenate([observed, obs_error, jnp.zeros((LANES - 2 * per,), F32)])[None]
    sizes = dict(shift=shift, slots=slots, heights=heights, tiles=n_tile, per=per)

    def forward(*refs):
        forward_kernel(*refs, **sizes)

    foot, got_odd = lax.optimization_barrier((foot, got_rows[1]))
    needed = [got_corners[1], *base, *corner_parts]
    partial, table = call(
        forward,
        [array(devices, groups + 1, LANES), jax.ShapeDtypeStruct((devices, LANES), jnp.int32)],
        [VM] * 4 + [HB] * 8,
        [pltpu.VMEM(x.shape, x.dtype) for x in needed]
        + [pltpu.VMEM((rows, hours, cols), F32), row_scratch, row_scratch, row_scratch]
        + [
            pltpu.VMEM((slots, devices, LANES), F32),
            pltpu.SMEM((devices, LANES), jnp.int32),
            pltpu.SemaphoreType.DMA((len(needed) + 4,)),
        ],
        "block_values",
    )(par, foot, own, got_odd.astype(F32), *[far(x) for x in (flux, scale, *needed)])
    everyone = lax.all_to_all(partial, AXES, split_axis=0, concat_axis=0, tiled=True)

    def adjoint(*refs):
        adjoint_kernel(*refs, **sizes)

    weight_rows = -(-(groups + 1) // SUB) * SUB
    model_co2, factor, field = call(
        adjoint,
        [array(1, per), array(2, LANES), field_shape],
        [VM] * 5,
        [
            pltpu.VMEM((weight_rows, LANES), F32),
            pltpu.SMEM((weight_rows, LANES), F32),
            pltpu.SMEM((devices, LANES), jnp.int32),
            pltpu.SemaphoreType.DMA((2,)),
        ],
        "adjoint_field",
    )(par, table, everyone, foot, scale)
    sent_rows, got_rows = pack_rows(factor, field, "gradient_rows")
    strips = call(strip_kernel, [strip, strip], [VM] * 4, [], "gradient_pack")(par, *sent_rows, field)
    local, got_corners = inner_sums(field, strips, True, "gradient")
    got_rows = [r.astype(F32) for r in got_rows]
    gradient = call(
        finish_kernel,
        array(hours, rows, cols),
        [VM] * 12,
        [
            pltpu.VMEM((2, RAD, hours, cols), F32),
            pltpu.VMEM((hours, 2 * RAD, cols), F32),
            pltpu.VMEM((hours, rows, cols), F32),
            pltpu.SemaphoreType.DMA((2,)),
        ],
        "gradient",
        out_specs=HB,
    )(par, local, factor, *got_rows, *got_corners, *base, *corner_parts)
    return (model_co2.reshape(-1), gradient)


def solution(mesh):
    return jax.shard_map(
        per_device,
        mesh=mesh,
        in_specs=(
            P(None, "rec", "tile"),
            P(None, "rec", "tile"),
            P(None, "rec", "tile"),
            P(("rec", "tile"), None, None, None),
            P(("rec", "tile")),
            P(("rec", "tile"), None),
            P(("rec", "tile"), None),
            P(("rec", "tile"), None),
            P("rec"),
            P("rec"),
        ),
        out_specs=(P("rec"), P(None, "rec", "tile")),
        check_vma=False,
    )
```

```python
import numpy as np
import jax
import jax.numpy as jnp
from jax import lax
from jax.experimental import pallas as pl
from jax.experimental.pallas import tpu as pltpu
from jax.sharding import PartitionSpec as P

RAD = 4
TAPS = 12
AXES = ("rec", "tile")
LANES = 128
SUB = 8
FOOT_MAX = 0.02
PARTS = 4
SCALE_MAX = 2.0
HALF_TOP = 32768.0
CONTROL_FACTOR = 4096.0
F16 = jnp.float16
VMEM_LIMIT = 14 * 1024 * 1024
F32 = jnp.float32
BF16 = jnp.bfloat16


def space_taps():
    offsets = np.arange(-RAD, RAD + 1).astype(np.float64)
    values = np.exp(-2.0 * offsets * offsets / (RAD * RAD))
    return values / np.sqrt(np.sum(values * values))


def time_taps():
    offsets = np.arange(-TAPS, TAPS + 1).astype(np.float64)
    values = np.exp(-2.0 * np.abs(offsets) / TAPS)
    return values / np.sqrt(np.sum(values * values))


def banded(distance, taps, reach):
    inside = np.abs(distance) <= reach
    return np.where(inside, taps[np.clip(distance, -reach, reach) + reach], 0.0)


def two_parts(matrix):
    high = matrix.astype(np.float32).astype(jnp.bfloat16)
    low = (matrix - high.astype(np.float64)).astype(np.float32).astype(jnp.bfloat16)
    return high, low


def constants(hours, rows, cols):
    space = space_taps()
    hour = np.arange(hours)
    time_high, time_low = two_parts(banded(hour[:, None] - hour[None, :], time_taps(), TAPS))
    col = np.arange(cols)
    col_high, col_low = two_parts(banded(col[:, None] - col[None, :], space, RAD))
    col_both = np.block([[col_high, col_low], [col_high, np.zeros_like(col_high)]])
    halo_col = np.concatenate([np.arange(-RAD, 0), np.arange(cols, cols + RAD)])
    edge = banded(halo_col[:, None] - col[None, :], space, RAD)

    def strips(row_of, halo_of, targets):
        by_row = banded(np.array(row_of)[:, None] - np.array(targets)[None, :], space, RAD)
        both = by_row[:, :, None] * edge[np.array(halo_of)][:, None, :]
        return two_parts(both.reshape(len(row_of), -1))

    unused = [(-100, 0)] * (LANES - RAD * rows)
    own = []
    for side in range(2):
        own += [(row, side * RAD + j) for row in range(rows) for j in range(RAD)] + unused
    corner = [], []
    for first, targets in ((rows, rows - 1 - np.arange(RAD)), (-RAD, np.arange(RAD))):
        lanes = [
            (row, side * RAD + j) for side in range(2) for row in range(first, first + RAD) for j in range(RAD)
        ]
        for part, value in zip(corner, strips(*zip(*lanes), targets)):
            part.append(value)
    return (time_high, time_low, col_both), strips(*zip(*own), np.arange(rows)), [np.stack(c) for c in corner]


def split(value):
    high = value.astype(BF16)
    low = (value - high.astype(F32)).astype(BF16)
    return high, low


def dot(a, b):
    return jnp.dot(a, b, preferred_element_type=F32)


def lane_ids(shape):
    return lax.broadcasted_iota(jnp.int32, shape, 1)


def choose(flag, yes, no):
    return jnp.where(flag, yes, no)


def pack_strips(row_value, odd, rows):
    cols = row_value(0).shape[1]
    half = rows * RAD
    source = lax.broadcasted_iota(jnp.int32, (cols, 2 * half), 0)
    lane = lane_ids((cols, 2 * half))
    first = lane < half
    j = lane & (RAD - 1)
    at_first, at_second = choose(odd, j, cols - RAD + j), choose(odd, cols - RAD + j, j)
    wanted = jnp.where(first, at_first, at_second)
    lane_row = jnp.where(first, lane, lane - half) // RAD
    total = None
    for row in range(rows):
        high, low = split(row_value(row))
        pick = jnp.where((source == wanted) & (lane_row == row), 1.0, 0.0).astype(BF16)
        part = dot(jnp.concatenate([high, low], axis=1), jnp.concatenate([pick, pick], axis=0))
        total = part if total is None else total + part
    return total


def fold_corners(odd, strips, corner_e, corner_o):
    quarter = corner_e.shape[0]
    half, part = LANES // 2, RAD * RAD
    lane = lane_ids((quarter, LANES))
    spare = jnp.zeros((4 * quarter - strips.shape[0], LANES), F32)
    whole = jnp.concatenate([strips, spare], axis=0)
    low = high = jnp.zeros((quarter, LANES), F32)
    for q in range(LANES // (2 * part)):
        piece = whole[q * quarter : (q + 1) * quarter]
        for side in range(2):
            to = q * 2 * part + side * part
            here = (lane >= to) & (lane < to + part)
            low = choose(here, pltpu.roll(piece, (to - side * half) % LANES, 1), low)
            high = choose(here, pltpu.roll(piece, (to - side * half - (half - part)) % LANES, 1), high)
    corner_e[...] = choose(odd, low, high)
    corner_o[...] = choose(odd, high, low)


def unfold_corners(value):
    part = 2 * RAD * RAD
    pieces = [value] + [pltpu.roll(value, LANES - q * part, 1) for q in range(1, LANES // part)]
    return jnp.concatenate(pieces, axis=0)


def is_odd(par_ref, axis):
    return par_ref[axis : axis + 1, :] == 1


def rows_kernel(par_ref, after, factor_ref, field_ref, out_ref, *, even):
    odd = is_odd(par_ref, 0)
    factor = factor_ref[0:1, :]
    rows = field_ref.shape[0]
    for row in range(RAD):
        first, last = field_ref[row], field_ref[rows - 1 - row]
        out_ref[row] = (choose(odd, first, last) if even else choose(odd, last, first)) * factor


def turn_kernel(par_ref, after, control_ref, field_ref, strip_e, strip_o):
    rows = control_ref.shape[1]
    for row in range(rows):
        field_ref[row] = control_ref[:, row, :]
    write_strips(is_odd(par_ref, 1), field_ref, strip_e, strip_o)


def strip_kernel(par_ref, after, field_ref, strip_e, strip_o):
    write_strips(is_odd(par_ref, 1), field_ref, strip_e, strip_o)


def write_strips(odd, field_ref, strip_e, strip_o):
    strips = pack_strips(lambda r: field_ref[r], odd, field_ref.shape[0])
    half = LANES // 2
    left = lane_ids(strips.shape) < half
    strip_e[...] = jnp.where(left, strips, 0.0)
    strip_o[...] = jnp.where(left, pltpu.roll(strips, half, 1), 0.0)


def far_corner_kernel(par_ref, after, strip_e, strip_o, corner_e, corner_o):
    odd = is_odd(par_ref, 1)
    even_swap, odd_swap = strip_e[...], strip_o[...]
    before, after = choose(odd, even_swap, odd_swap), choose(odd, odd_swap, even_swap)
    half = LANES // 2
    both = jnp.where(lane_ids(before.shape) < half, before, pltpu.roll(after, half, 1))
    fold_corners(is_odd(par_ref, 0), both, corner_e, corner_o)


def prepare_kernel(
    foot_ref, start_ref, row_ref, slot_ref, count_ref, out_ref,
    blocks_ref, notes_ref, start_vmem, row_vmem, slot_vmem, count_vmem, sems, *, per,
):
    owners, lines, _ = foot_ref.shape
    slots = start_ref.shape[0]
    pairs = ((start_ref, start_vmem), (row_ref, row_vmem), (slot_ref, slot_vmem), (count_ref, count_vmem))
    small = [pltpu.make_async_copy(a, b, sems.at[i]) for i, (a, b) in enumerate(pairs)]
    chunk = owners // PARTS
    parts = [slice(i * chunk, (i + 1) * chunk) for i in range(PARTS)]
    loads = [
        pltpu.make_async_copy(foot_ref.at[here], blocks_ref.at[here], sems.at[4 + i])
        for i, here in enumerate(parts)
    ]
    for copy in small + loads:
        copy.start()
    stores = []
    for i, here in enumerate(parts):
        loads[i].wait()
        to = out_ref.at[here, 0:lines, :]
        stores.append(pltpu.make_async_copy(blocks_ref.at[here], to, sems.at[4 + PARTS + i]))
        stores[-1].start()
    for copy in small:
        copy.wait()
    start = start_vmem[...]
    valid = lax.broadcasted_iota(jnp.int32, start.shape, 0) < count_vmem[...]
    lanes = jnp.concatenate(
        [start >> 4, start & 15, row_vmem[...], jnp.where(valid, slot_vmem[...], per)], axis=0
    ).astype(F32)
    wide = jnp.pad(lanes, ((0, LANES - 4 * slots), (0, LANES - owners)))
    turned = jnp.transpose(wide)[0:owners]
    notes_ref[...] = jnp.broadcast_to(turned[:, None, :], notes_ref.shape).astype(BF16)
    stores.append(pltpu.make_async_copy(notes_ref, out_ref.at[:, lines : lines + SUB, :], sems.at[4 + 2 * PARTS]))
    stores[-1].start()
    for copy in stores:
        copy.wait()


def halo_sums(parts, high_ref, low_ref, first, width):
    high, low = parts
    weights = high_ref[:, first : first + width]
    return dot(high, weights) + dot(low, weights) + dot(high, low_ref[:, first : first + width])


def column_sums(value, col_both):
    cols = value.shape[1]
    high, low = split(value)
    out = dot(jnp.concatenate([high, low], axis=1), col_both)
    return out[:, :cols] + out[:, cols:]


def time_sums(value, time_high, time_low):
    high, low = split(value)
    return dot(time_high, high) + dot(time_high, low) + dot(time_low, high)


def row_sums(get, row, low, high, taps):
    total = None
    for distance in range(RAD + 1):
        here = [get(r) for r in sorted({row - distance, row + distance}) if low <= r < high]
        if not here:
            continue
        part = here[0] if len(here) == 1 else here[0] + here[1]
        part = float(taps[RAD + distance]) * part
        total = part if total is None else total + part
    return total


def local_kernel(after, field_ref, time_high, time_low, col_both, out_ref):
    rows, hours, cols = field_ref.shape
    taps = space_taps()
    for row in range(0, rows, 2):
        pair = [
            column_sums(row_sums(lambda i: field_ref[i], r, 0, rows, taps), col_both[...])
            for r in (row, row + 1)
        ]
        both = time_sums(jnp.concatenate(pair, axis=1), time_high[...], time_low[...])
        for k, r in enumerate((row, row + 1)):
            out_ref[r] = both[:, k * cols : (k + 1) * cols]


def strip_halo(par_ref, strip_e, strip_o, time_high, time_low):
    odd = is_odd(par_ref, 1)
    even_swap, odd_swap = strip_e[...], strip_o[...]
    halo = jnp.concatenate([choose(odd, even_swap, odd_swap), choose(odd, odd_swap, even_swap)], axis=1)
    return split(time_sums(halo, time_high[...], time_low[...]))


def strips_kernel(par_ref, local_ref, strip_e, strip_o, time_high, time_low, own_high, own_low, out_ref):
    rows, hours, cols = local_ref.shape
    halo = strip_halo(par_ref, strip_e, strip_o, time_high, time_low)
    for row in range(0, rows, 2):
        both = halo_sums(halo, own_high, own_low, row * cols, 2 * cols)
        for k, r in enumerate((row, row + 1)):
            out_ref[r] = local_ref[r] + both[:, k * cols : (k + 1) * cols]


def sides_kernel(
    par_ref, local_ref, strip_e, strip_o, factor_ref, got_ref, corner_ref,
    time_high, time_low, col_both, own_high, own_low, corner_high, corner_low, out_ref, halo,
):
    rows, hours, cols = local_ref.shape
    odd = par_ref[0, 0]
    halo[...] = got_ref[...] * factor_ref[1:2, :]
    consts = (time_high, time_low, col_both)
    parts = edge_parts(halo, corner_ref[...], corner_high.at[odd], corner_low.at[odd], consts)
    at_first = jnp.where(is_odd(par_ref, 0), 1.0, 0.0)
    strips = strip_halo(par_ref, strip_e, strip_o, time_high, time_low)
    for row in range(0, rows, 2):
        both = halo_sums(strips, own_high, own_low, row * cols, 2 * cols)
        for k, r in enumerate((row, row + 1)):
            value = local_ref[r] + both[:, k * cols : (k + 1) * cols]
            if r < RAD:
                value = value + parts[r] * at_first
            if r >= rows - RAD:
                value = value + parts[rows - 1 - r] * (1.0 - at_first)
            out_ref[:, r, :] = value


def edge_parts(odd, rows, first, got_e, got_o, consts, halo, factor, corner=None):
    time_high, time_low, col_both = consts
    taps = space_taps()
    for row in range(RAD):
        even, other = got_e[row], got_o[row]
        halo[row] = (choose(odd, even, other) if first else choose(odd, other, even)) * factor
    parts = []
    for k in range(0, RAD, 2):
        pair = []
        for i in (k, k + 1):
            if first:
                summed = row_sums(lambda r: halo[r + RAD], i, -RAD, 0, taps)
            else:
                summed = row_sums(lambda r: halo[r - RAD], i, RAD, 2 * RAD, taps)
            pair.append(column_sums(summed, col_both[...]))
        value = jnp.concatenate(pair, axis=1)
        width = value.shape[1]
        if corner is not None:
            parts_of, high, low = corner
            at = (k if first else RAD + k) * (width // 2)
            value = value + halo_sums(parts_of, high, low, at, width)
        both = time_sums(value, time_high[...], time_low[...])
        half = width // 2
        parts += [both[:, :half], both[:, half:]]
    return parts


def edge_parts(halo, corner, corner_high, corner_low, consts):
    time_high, time_low, col_both = consts
    hours, cols = halo.shape[1:]
    taps = space_taps()
    corner = split(unfold_corners(corner)[0:hours, 0 : corner_high.shape[0]])
    parts = []
    for k in range(0, RAD, 2):
        pair = []
        for i in (k, k + 1):
            summed = None
            for j in range(RAD - i):
                part = float(taps[RAD + i + j + 1]) * halo[j]
                summed = part if summed is None else summed + part
            pair.append(column_sums(summed, col_both[...]))
        value = jnp.concatenate(pair, axis=1) + halo_sums(corner, corner_high, corner_low, k * cols, 2 * cols)
        both = time_sums(value, time_high[...], time_low[...])
        parts += [both[:, :cols], both[:, cols:]]
    return parts


def flux_kernel(
    par_ref, local_ref, prior_ref, scale_ref, got_ref, corner_ref,
    time_high, time_low, col_both, corner_high, corner_low, flux_ref, scale_out, wide, halo,
):
    rows = local_ref.shape[0]
    odd = par_ref[0, 0]
    wide[...] = scale_ref[...].astype(F32)
    for row in range(rows):
        scale_out[row] = wide[:, row, :]
    wide[...] = prior_ref[...].astype(F32)
    for row in range(rows):
        flux_ref[row] = wide[:, row, :] + scale_out[row] * local_ref[row]
    halo[...] = got_ref[...] * (1.0 / CONTROL_FACTOR)
    consts = (time_high, time_low, col_both)
    parts = edge_parts(halo, corner_ref[...], corner_high.at[odd], corner_low.at[odd], consts)
    for k, part in enumerate(parts):
        row = jnp.where(odd == 1, k, rows - 1 - k)
        flux_ref[row] = flux_ref[row] + scale_out[row] * part


def finish_kernel(
    par_ref, model_ref, local_ref, factor_ref, got_ref, corner_ref,
    time_high, time_low, col_both, corner_high, corner_low,
    model_out, out_ref, halo, edges, total, model_own, sems,
):
    hours, rows, cols = local_ref.shape
    half = rows // 2
    odd = par_ref[0, 0]
    mine = pl.multiple_of(odd * half, half)
    rest = pl.multiple_of(half - mine, half)
    model_own[...] = model_ref[:, 0 : model_own.shape[1]]
    copies = [
        pltpu.make_async_copy(model_own, model_out, sems.at[0]),
        pltpu.make_async_copy(
            local_ref.at[:, pl.ds(rest, half), :], out_ref.at[:, pl.ds(rest, half), :], sems.at[1]
        ),
    ]
    for copy in copies:
        copy.start()
    halo[...] = got_ref[...] * factor_ref[1:2, :]
    consts = (time_high, time_low, col_both)
    parts = edge_parts(halo, corner_ref[...], corner_high.at[1 - odd], corner_low.at[1 - odd], consts)
    at_last = jnp.where(is_odd(par_ref, 0), 1.0, 0.0)
    for k, part in enumerate(parts):
        edges[:, k, :] = part * (1.0 - at_last)
        edges[:, half - 1 - k, :] = part * at_last
    total[...] = local_ref[:, pl.ds(mine, half), :] + edges[...]
    copies.append(pltpu.make_async_copy(total, out_ref.at[:, pl.ds(mine, half), :], sems.at[2]))
    copies[-1].start()
    for copy in copies:
        copy.wait()


def blocks_of(foot_ref, source, heights, slots):
    for c in range(0, slots, 2):
        both = foot_ref[source, c * heights : (c + 2) * heights, :].astype(F32)
        yield c, both[0:heights]
        yield c + 1, both[heights : 2 * heights]


def forward_kernel(
    par_ref, foot_ref, own_ref, got_ref, corner_ref, flux_hbm, scale_hbm, *refs,
    shift, slots, heights, tiles, per,
):
    distant, near = refs[0:5], refs[7:12]
    out_ref, table_ref = refs[5:7]
    flux_ref, scale_ref, halo, edges, sums, table_smem, sems = refs[12:]
    *consts, corner_high, corner_low = near
    odd = par_ref[0, 0]
    sources = foot_ref.shape[0]
    rows = flux_ref.shape[0]
    first = (rows - RAD) * odd
    pairs = list(zip(distant, near)) + [(scale_hbm.at[pl.ds(first, RAD)], scale_ref)]
    pairs += [(flux_hbm.at[r : r + RAD], flux_ref.at[r : r + RAD]) for r in range(0, rows, RAD)]
    loads = [pltpu.make_async_copy(a, b, sems.at[i]) for i, (a, b) in enumerate(pairs)]
    for load in loads:
        load.start()
    groups = out_ref.shape[1] - 1
    base = slots * heights
    lane = lane_ids((sources, LANES))
    notes = foot_ref[:, base : base + SUB, :].astype(F32)[:, 0, :].astype(jnp.int32)
    start = notes * 16 + pltpu.roll(notes, LANES - slots, 1)
    offset = start + pltpu.roll(notes, LANES - 2 * slots, 1) * (1 << shift)
    source_rec = lax.broadcasted_iota(jnp.int32, (sources, LANES), 0) // tiles
    receptor = jnp.where(notes < per, source_rec * per + notes, groups * LANES)
    table = jnp.where(lane < slots, offset, receptor)
    table_ref[...] = table
    copy = pltpu.make_async_copy(table_ref, table_smem, sems.at[len(loads)])
    copy.start()
    for load in loads[: len(near)]:
        load.wait()
    halo[...] = got_ref[...] * (1.0 / CONTROL_FACTOR)
    parts = edge_parts(halo, corner_ref[...], corner_high.at[1 - odd], corner_low.at[1 - odd], consts)
    for k, part in enumerate(parts):
        edges[k] = part
    for load in loads[len(near) :]:
        load.wait()
    for k in range(RAD):
        line = jnp.where(odd == 1, RAD - 1 - k, k)
        flux_ref[first + line] = flux_ref[first + line] + scale_ref[line] * edges[k]
    copy.wait()

    def body(source, carry):
        for c, block in blocks_of(foot_ref, source, heights, slots):
            offset = table_smem[source, c]
            row = lax.shift_right_logical(offset, shift)
            begin = jnp.bitwise_and(offset, (1 << shift) - 1)
            product = flux_ref[row, pl.ds(begin, heights), :] * block
            sums[c, pl.ds(source, 1), :] = jnp.sum(product, axis=0, keepdims=True)
        return carry

    lax.fori_loop(0, sources, body, 0)
    totals = [jnp.zeros((sources, LANES), F32) for _ in range(groups)]
    for c in range(slots):
        value = jnp.sum(sums[c], axis=1, keepdims=True)
        which = table[:, 3 * slots + c : 3 * slots + c + 1]
        for q in range(groups):
            totals[q] = totals[q] + jnp.where(which == lane + q * LANES, value, 0.0)
    for q in range(groups):
        total = jnp.sum(totals[q], axis=0, keepdims=True)
        out_ref[:, q : q + 1, :] = jnp.broadcast_to(total[None], (sources, 1, LANES))
    out_ref[:, groups : groups + 1, :] = jnp.broadcast_to(own_ref[...][None], (sources, 1, LANES))


def adjoint_kernel(
    par_ref, table_vmem, got_ref, foot_ref, scale_ref,
    model_ref, factor_ref, field_ref,
    weight_vmem, weight_smem, table_ref, sems, *, shift, slots, heights, tiles, per,
):
    load = pltpu.make_async_copy(table_vmem, table_ref, sems.at[1])
    load.start()
    sources = foot_ref.shape[0]
    groups = got_ref.shape[1] - 1
    rows, hours, _ = field_ref.shape
    model = jnp.sum(got_ref[:, 0:groups, :], axis=0)
    packed = LANES // per
    lane = lane_ids((1, LANES))
    own = jnp.zeros((1, LANES), F32)
    for q in range(groups):
        for k in range(packed):
            line = model[q : q + 1, :]
            line = line if k == 0 else pltpu.roll(line, LANES - k * per, 1)
            own = choose(par_ref[2:3, :] == q * packed + k, line, own)
    model_ref[...] = own
    weight_vmem[...] = jnp.zeros_like(weight_vmem)
    for q in range(groups):
        observed, error = jnp.zeros((1, LANES), F32), jnp.ones((1, LANES), F32)
        for k in range(packed):
            line = got_ref[(q * packed + k) * tiles, groups : groups + 1, :]
            here = (lane >= k * per) & (lane < (k + 1) * per)
            observed = jnp.where(here, line if k == 0 else pltpu.roll(line, k * per, 1), observed)
            turn = (k * per - per) % LANES
            error = jnp.where(here, line if turn == 0 else pltpu.roll(line, turn, 1), error)
        weight_vmem[q : q + 1, :] = (model[q : q + 1, :] - observed) / (error * error)
    copy = pltpu.make_async_copy(weight_vmem, weight_smem, sems.at[0])
    copy.start()
    field_ref[...] = jnp.zeros_like(field_ref)
    top = jnp.max(jnp.abs(weight_vmem[...]), keepdims=True) * (FOOT_MAX * SCALE_MAX * sources * slots)
    top = jnp.maximum(top, 1e-25)
    factor_ref[0:1, :] = jnp.broadcast_to(HALF_TOP / top, (1, LANES))
    factor_ref[1:2, :] = jnp.broadcast_to(top * (1.0 / HALF_TOP), (1, LANES))
    load.wait()
    copy.wait()

    def body(source, carry):
        for c, block in blocks_of(foot_ref, source, heights, slots):
            offset = table_ref[source, c]
            receptor = table_ref[source, 3 * slots + c]
            row = lax.shift_right_logical(offset, shift)
            begin = jnp.bitwise_and(offset, (1 << shift) - 1)
            weight = weight_smem[lax.shift_right_logical(receptor, 7), jnp.bitwise_and(receptor, LANES - 1)]
            field_ref[row, pl.ds(begin, heights), :] += block * weight
        return carry

    lax.fori_loop(0, sources, body, 0)
    for row in range(rows):
        field_ref[row] = field_ref[row] * scale_ref[row]


def swap_pairs(count, odd):
    pairs = []
    for i in range(1 if odd else 0, count - 1, 2):
        pairs += [(i, i + 1), (i + 1, i)]
    return pairs


def swap(axis, even, odd):
    count = lax.axis_size(axis)
    return (
        lax.ppermute(even, axis, swap_pairs(count, False)),
        lax.ppermute(odd, axis, swap_pairs(count, True)),
    )


VM = pl.BlockSpec(memory_space=pltpu.VMEM)
HB = pl.BlockSpec(memory_space=pltpu.HBM)


def call(kernel, out_shape, in_specs, scratch, name, out_specs=None):
    return pl.pallas_call(
        kernel,
        out_shape=out_shape,
        in_specs=in_specs,
        out_specs=jax.tree.map(lambda _: VM, out_shape) if out_specs is None else out_specs,
        scratch_shapes=scratch,
        compiler_params=pltpu.CompilerParams(vmem_limit_bytes=VMEM_LIMIT),
        name=name,
    )


def far(x):
    return pltpu.with_memory_space_constraint(x, pltpu.HBM)


def array(*shape):
    return jax.ShapeDtypeStruct(shape, F32)


def per_device(
    prior_flux,
    flux_scale,
    control,
    footprint,
    slot_count,
    start_hour,
    grid_row,
    receptor_slot,
    observed,
    obs_error,
):
    hours, rows, cols = control.shape
    n_rec, n_tile = lax.axis_size("rec"), lax.axis_size("tile")
    devices = n_rec * n_tile
    slots, heights = footprint.shape[1], footprint.shape[2]
    per = observed.shape[0]
    groups = per * n_rec // LANES
    shift = (hours - 1).bit_length()
    rec, tile = lax.axis_index("rec"), lax.axis_index("tile")
    par = jnp.stack([rec % 2, tile % 2, rec] + [rec * 0] * (SUB - 3)).astype(jnp.int32)
    par = jnp.broadcast_to(par[:, None], (SUB, LANES))
    base, own_parts, corner_parts = constants(hours, rows, cols)
    base = [jnp.asarray(c) for c in base]
    own_parts = [jnp.asarray(c) for c in own_parts]
    corner_parts = [jnp.asarray(c) for c in corner_parts]
    strip = array(hours, LANES)
    corner = array(-(-hours // (4 * SUB)) * SUB, LANES)
    block = array(RAD, hours, cols)
    field_shape = array(rows, hours, cols)
    row_scratch = pltpu.VMEM((RAD, hours, cols), F32)

    def swaps(after, field, got_strips, name):
        local = call(local_kernel, field_shape, [VM] * 5, [], name + "_local")(after, field, *base)
        corners = call(far_corner_kernel, [corner, corner], [VM] * 4, [], name + "_corners")(par, local, *got_strips)
        return local, swap("rec", *corners)

    def swap_rows(even, after, factor, field, name):
        def kernel(*refs):
            rows_kernel(*refs, even=even)

        sent = call(kernel, block, [VM] * 4, [], name)(par, after, factor, field)
        return sent, lax.ppermute(sent.astype(F16), "rec", swap_pairs(n_rec, not even))

    def prepare(*refs):
        prepare_kernel(*refs, per=per)

    numbers = pltpu.VMEM((slots, devices), jnp.int32)
    lines = slots * heights + SUB
    sent = call(
        prepare,
        jax.ShapeDtypeStruct((devices, lines, cols), BF16),
        [HB] * 5,
        [
            pltpu.VMEM((devices, slots * heights, cols), BF16),
            pltpu.VMEM((devices, SUB, LANES), BF16),
            numbers, numbers, numbers, pltpu.VMEM((1, devices), jnp.int32),
            pltpu.SemaphoreType.DMA((5 + 2 * PARTS,)),
        ],
        "prepare_blocks",
        out_specs=HB,
    )(*[
        far(x)
        for x in (
            footprint.reshape(devices, slots * heights, cols),
            start_hour.T, grid_row.T, receptor_slot.T, slot_count[None],
        )
    ])
    foot = lax.all_to_all(sent, AXES, split_axis=0, concat_axis=0, tiled=True)
    field, *strips = call(
        turn_kernel, [field_shape, strip, strip], [VM, HB, VM], [], "turn_control"
    )(par, sent, control)
    factor = jnp.full((2, LANES), CONTROL_FACTOR, F32)
    _, got_even = swap_rows(True, strips[0], factor, field, "control_even")
    _, got_odd = swap_rows(False, strips[0], factor, field, "control_odd")
    got_strips = swap("tile", *strips)
    local, got_corners = swaps(strips[0], field, got_strips, "control")
    local = call(strips_kernel, field_shape, [VM] * 8, [], "control_strips")(
        par, local, *got_strips, *base[:2], *own_parts
    )
    flux, scale = call(
        flux_kernel,
        [field_shape, field_shape],
        [VM] * 11,
        [pltpu.VMEM((hours, rows, cols), F32), row_scratch],
        "flux_field",
    )(par, local, prior_flux, flux_scale, got_even.astype(F32), got_corners[0], *base, *corner_parts)

    own = jnp.concatenate([observed, obs_error, jnp.zeros((LANES - 2 * per,), F32)])[None]
    sizes = dict(shift=shift, slots=slots, heights=heights, tiles=n_tile, per=per)

    def forward(*refs):
        forward_kernel(*refs, **sizes)

    foot, got_odd = lax.optimization_barrier((foot, got_odd))
    needed = [*base, *corner_parts]
    partial, table = call(
        forward,
        [array(devices, groups + 1, LANES), jax.ShapeDtypeStruct((devices, LANES), jnp.int32)],
        [VM] * 5 + [HB] * 7,
        [pltpu.VMEM(x.shape, x.dtype) for x in needed]
        + [pltpu.VMEM((rows, hours, cols), F32), row_scratch, row_scratch, row_scratch]
        + [
            pltpu.VMEM((slots, devices, LANES), F32),
            pltpu.SMEM((devices, LANES), jnp.int32),
            pltpu.SemaphoreType.DMA((len(needed) + rows // RAD + 2,)),
        ],
        "block_values",
    )(par, foot, own, got_odd.astype(F32), got_corners[1], *[far(x) for x in (flux, scale, *needed)])
    everyone = lax.all_to_all(partial, AXES, split_axis=0, concat_axis=0, tiled=True)

    def adjoint(*refs):
        adjoint_kernel(*refs, **sizes)

    weight_rows = -(-(groups + 1) // SUB) * SUB
    model, factor, field = call(
        adjoint,
        [array(1, LANES), array(2, LANES), field_shape],
        [VM] * 5,
        [
            pltpu.VMEM((weight_rows, LANES), F32),
            pltpu.SMEM((weight_rows, LANES), F32),
            pltpu.SMEM((devices, LANES), jnp.int32),
            pltpu.SemaphoreType.DMA((2,)),
        ],
        "adjoint_field",
    )(par, table, everyone, foot, scale)
    sent_even, got_even = swap_rows(True, factor, factor, field, "gradient_even")
    strips = call(strip_kernel, [strip, strip], [VM] * 3, [], "gradient_pack")(par, sent_even, field)
    got_strips = swap("tile", *strips)
    sent_odd, got_odd = swap_rows(False, got_strips[0], factor, field, "gradient_odd")
    local, got_corners = swaps(sent_odd, field, got_strips, "gradient")
    local = call(sides_kernel, array(hours, rows, cols), [VM] * 14, [row_scratch], "gradient_sides")(
        par, local, *got_strips, factor, got_even.astype(F32), got_corners[0], *base, *own_parts, *corner_parts
    )
    wide = pltpu.VMEM((hours, rows // 2, cols), F32)
    model_co2, gradient = call(
        finish_kernel,
        [array(1, per), array(hours, rows, cols)],
        [VM] * 11,
        [row_scratch, wide, wide, pltpu.VMEM((1, per), F32), pltpu.SemaphoreType.DMA((3,))],
        "gradient",
        out_specs=[HB, HB],
    )(par, model, local, factor, got_odd.astype(F32), got_corners[1], *base, *corner_parts)
    return (model_co2.reshape(-1), gradient)


def solution(mesh):
    return jax.shard_map(
        per_device,
        mesh=mesh,
        in_specs=(
            P(None, "rec", "tile"),
            P(None, "rec", "tile"),
            P(None, "rec", "tile"),
            P(("rec", "tile"), None, None, None),
            P(("rec", "tile")),
            P(("rec", "tile"), None),
            P(("rec", "tile"), None),
            P(("rec", "tile"), None),
            P("rec"),
            P("rec"),
        ),
        out_specs=(P("rec"), P(None, "rec", "tile")),
        check_vma=False,
    )
```

```python
import numpy as np
import jax
import jax.numpy as jnp
from jax import lax
from jax.experimental import pallas as pl
from jax.experimental.pallas import tpu as pltpu
from jax.sharding import PartitionSpec as P

RAD = 4
TAPS = 12
AXES = ("rec", "tile")
LANES = 128
SUB = 8
FOOT_MAX = 0.02
PARTS = 4
SCALE_MAX = 2.0
HALF_TOP = 32768.0
CONTROL_FACTOR = 4096.0
F16 = jnp.float16
VMEM_LIMIT = 14 * 1024 * 1024
F32 = jnp.float32
BF16 = jnp.bfloat16


def space_taps():
    offsets = np.arange(-RAD, RAD + 1).astype(np.float64)
    values = np.exp(-2.0 * offsets * offsets / (RAD * RAD))
    return values / np.sqrt(np.sum(values * values))


def time_taps():
    offsets = np.arange(-TAPS, TAPS + 1).astype(np.float64)
    values = np.exp(-2.0 * np.abs(offsets) / TAPS)
    return values / np.sqrt(np.sum(values * values))


def banded(distance, taps, reach):
    inside = np.abs(distance) <= reach
    return np.where(inside, taps[np.clip(distance, -reach, reach) + reach], 0.0)


def two_parts(matrix):
    high = matrix.astype(np.float32).astype(jnp.bfloat16)
    low = (matrix - high.astype(np.float64)).astype(np.float32).astype(jnp.bfloat16)
    return high, low


def constants(hours, rows, cols):
    space = space_taps()
    hour = np.arange(hours)
    time_high, time_low = two_parts(banded(hour[:, None] - hour[None, :], time_taps(), TAPS))
    col = np.arange(cols)
    col_high, col_low = two_parts(banded(col[:, None] - col[None, :], space, RAD))
    col_both = np.block([[col_high, col_low], [col_high, np.zeros_like(col_high)]])
    halo_col = np.concatenate([np.arange(-RAD, 0), np.arange(cols, cols + RAD)])
    edge = banded(halo_col[:, None] - col[None, :], space, RAD)

    def strips(row_of, halo_of, targets):
        by_row = banded(np.array(row_of)[:, None] - np.array(targets)[None, :], space, RAD)
        both = by_row[:, :, None] * edge[np.array(halo_of)][:, None, :]
        return two_parts(both.reshape(len(row_of), -1))

    own = [(row, side * RAD + j) for side in range(2) for row in range(rows) for j in range(RAD)]
    corner = [], []
    for first, targets in ((rows, rows - 1 - np.arange(RAD)), (-RAD, np.arange(RAD))):
        lanes = [
            (row, side * RAD + j) for side in range(2) for row in range(first, first + RAD) for j in range(RAD)
        ]
        for part, value in zip(corner, strips(*zip(*lanes), targets)):
            part.append(value)
    return (time_high, time_low, col_both), strips(*zip(*own), np.arange(rows)), [np.stack(c) for c in corner]


def split(value):
    high = value.astype(BF16)
    low = (value - high.astype(F32)).astype(BF16)
    return high, low


def dot(a, b):
    return jnp.dot(a, b, preferred_element_type=F32)


def lane_ids(shape):
    return lax.broadcasted_iota(jnp.int32, shape, 1)


def choose(flag, yes, no):
    return jnp.where(flag, yes, no)


def pack_strips(row_value, rows):
    cols = row_value(0).shape[1]
    half = rows * RAD
    source = lax.broadcasted_iota(jnp.int32, (cols, 2 * half), 0)
    lane = lane_ids((cols, 2 * half))
    first = lane < half
    j = lane & (RAD - 1)
    wanted = jnp.where(first, cols - RAD + j, j)
    lane_row = jnp.where(first, lane, lane - half) // RAD
    total = None
    for row in range(rows):
        high, low = split(row_value(row))
        pick = jnp.where((source == wanted) & (lane_row == row), 1.0, 0.0).astype(BF16)
        part = dot(jnp.concatenate([high, low], axis=1), jnp.concatenate([pick, pick], axis=0))
        total = part if total is None else total + part
    return total


def fold_corners(odd, strips, corner_e, corner_o):
    quarter = corner_e.shape[0]
    half, part = LANES // 2, RAD * RAD
    lane = lane_ids((quarter, LANES))
    spare = jnp.zeros((4 * quarter - strips.shape[0], LANES), F32)
    whole = jnp.concatenate([strips, spare], axis=0)
    low = high = jnp.zeros((quarter, LANES), F32)
    for q in range(LANES // (2 * part)):
        piece = whole[q * quarter : (q + 1) * quarter]
        for side in range(2):
            to = q * 2 * part + side * part
            here = (lane >= to) & (lane < to + part)
            low = choose(here, pltpu.roll(piece, (to - side * half) % LANES, 1), low)
            high = choose(here, pltpu.roll(piece, (to - side * half - (half - part)) % LANES, 1), high)
    corner_e[...] = choose(odd, low, high)
    corner_o[...] = choose(odd, high, low)


def unfold_corners(value):
    part = 2 * RAD * RAD
    pieces = [value] + [pltpu.roll(value, LANES - q * part, 1) for q in range(1, LANES // part)]
    return jnp.concatenate(pieces, axis=0)


def is_odd(par_ref, axis):
    return par_ref[axis : axis + 1, :] == 1


def rows_kernel(par_ref, after, factor_ref, field_ref, out_ref, *, even):
    odd = is_odd(par_ref, 0)
    factor = factor_ref[0:1, :]
    rows = field_ref.shape[0]
    for row in range(RAD):
        first, last = field_ref[row], field_ref[rows - 1 - row]
        out_ref[row] = (choose(odd, first, last) if even else choose(odd, last, first)) * factor


def turn_kernel(after, control_ref, field_ref, last_ref, first_ref):
    rows = control_ref.shape[1]
    for row in range(rows):
        field_ref[row] = control_ref[:, row, :]
    write_strips(field_ref, last_ref, first_ref)


def strip_kernel(after, field_ref, last_ref, first_ref):
    write_strips(field_ref, last_ref, first_ref)


def write_strips(field_ref, last_ref, first_ref):
    strips = pack_strips(lambda r: field_ref[r], field_ref.shape[0])
    fold, half = last_ref.shape[0], LANES // 2
    early, late = strips[0:fold], strips[fold:]
    if late.shape[0] < fold:
        late = jnp.concatenate([late, jnp.zeros((fold - late.shape[0], LANES), F32)], axis=0)
    left = lane_ids(early.shape) < half
    last_ref[...] = jnp.where(left, early, pltpu.roll(late, half, 1))
    first_ref[...] = jnp.where(left, pltpu.roll(early, half, 1), late)


def halo_columns(par_ref, before_ref, after_ref):
    before, after = before_ref[...], after_ref[...]
    half = LANES // 2
    left = lane_ids(before.shape) < half
    early = jnp.where(left, before, pltpu.roll(after, half, 1))
    late = jnp.where(left, pltpu.roll(before, half, 1), after)
    outside = jnp.where(lane_ids((1, LANES)) < half, par_ref[3:4, :], par_ref[4:5, :])
    return jnp.where(outside == 1, 0.0, jnp.concatenate([early, late], axis=0))


def far_corner_kernel(par_ref, after, before_ref, after_ref, corner_e, corner_o):
    fold_corners(is_odd(par_ref, 0), halo_columns(par_ref, before_ref, after_ref), corner_e, corner_o)


def prepare_kernel(
    after, foot_ref, start_ref, row_ref, slot_ref, count_ref, out_ref,
    blocks_ref, notes_ref, start_vmem, row_vmem, slot_vmem, count_vmem, sems, *, per,
):
    owners, lines, _ = foot_ref.shape
    slots = start_ref.shape[0]
    pairs = ((start_ref, start_vmem), (row_ref, row_vmem), (slot_ref, slot_vmem), (count_ref, count_vmem))
    small = [pltpu.make_async_copy(a, b, sems.at[i]) for i, (a, b) in enumerate(pairs)]
    chunk = owners // PARTS
    parts = [slice(i * chunk, (i + 1) * chunk) for i in range(PARTS)]
    loads = [
        pltpu.make_async_copy(foot_ref.at[here], blocks_ref.at[here], sems.at[4 + i])
        for i, here in enumerate(parts)
    ]
    for copy in small + loads:
        copy.start()
    stores = []
    for i, here in enumerate(parts):
        loads[i].wait()
        to = out_ref.at[here, 0:lines, :]
        stores.append(pltpu.make_async_copy(blocks_ref.at[here], to, sems.at[4 + PARTS + i]))
        stores[-1].start()
    for copy in small:
        copy.wait()
    start = start_vmem[...]
    valid = lax.broadcasted_iota(jnp.int32, start.shape, 0) < count_vmem[...]
    lanes = jnp.concatenate(
        [start >> 4, start & 15, row_vmem[...], jnp.where(valid, slot_vmem[...], per)], axis=0
    ).astype(F32)
    wide = jnp.pad(lanes, ((0, LANES - 4 * slots), (0, LANES - owners)))
    turned = jnp.transpose(wide)[0:owners]
    notes_ref[...] = jnp.broadcast_to(turned[:, None, :], notes_ref.shape).astype(BF16)
    stores.append(pltpu.make_async_copy(notes_ref, out_ref.at[:, lines : lines + SUB, :], sems.at[4 + 2 * PARTS]))
    stores[-1].start()
    for copy in stores:
        copy.wait()


def halo_sums(parts, high_ref, low_ref, first, width):
    high, low = parts
    weights = high_ref[:, first : first + width]
    return dot(high, weights) + dot(low, weights) + dot(high, low_ref[:, first : first + width])


def column_sums(value, col_both):
    cols = value.shape[1]
    high, low = split(value)
    out = dot(jnp.concatenate([high, low], axis=1), col_both)
    return out[:, :cols] + out[:, cols:]


def time_sums(value, time_high, time_low):
    high, low = split(value)
    return dot(time_high, high) + dot(time_high, low) + dot(time_low, high)


def row_sums(get, row, low, high, taps):
    total = None
    for distance in range(RAD + 1):
        here = [get(r) for r in sorted({row - distance, row + distance}) if low <= r < high]
        if not here:
            continue
        part = here[0] if len(here) == 1 else here[0] + here[1]
        part = float(taps[RAD + distance]) * part
        total = part if total is None else total + part
    return total


def local_kernel(after, field_ref, time_high, time_low, col_both, out_ref):
    rows, hours, cols = field_ref.shape
    taps = space_taps()
    for row in range(0, rows, 2):
        pair = [
            column_sums(row_sums(lambda i: field_ref[i], r, 0, rows, taps), col_both[...])
            for r in (row, row + 1)
        ]
        both = time_sums(jnp.concatenate(pair, axis=1), time_high[...], time_low[...])
        for k, r in enumerate((row, row + 1)):
            out_ref[r] = both[:, k * cols : (k + 1) * cols]


def strip_halo(par_ref, before_ref, after_ref, time_high, time_low):
    halo = halo_columns(par_ref, before_ref, after_ref)[0 : time_high.shape[0]]
    return split(time_sums(halo, time_high[...], time_low[...]))


def strips_kernel(par_ref, local_ref, before_ref, after_ref, time_high, time_low, own_high, own_low, out_ref):
    rows, hours, cols = local_ref.shape
    halo = strip_halo(par_ref, before_ref, after_ref, time_high, time_low)
    for row in range(0, rows, 2):
        both = halo_sums(halo, own_high, own_low, row * cols, 2 * cols)
        for k, r in enumerate((row, row + 1)):
            out_ref[r] = local_ref[r] + both[:, k * cols : (k + 1) * cols]


def sides_kernel(
    par_ref, local_ref, before_ref, after_ref, factor_ref, got_ref, corner_ref,
    time_high, time_low, col_both, own_high, own_low, corner_high, corner_low, out_ref, halo,
):
    rows, hours, cols = local_ref.shape
    odd = par_ref[0, 0]
    halo[...] = got_ref[...] * factor_ref[1:2, :]
    consts = (time_high, time_low, col_both)
    parts = edge_parts(halo, corner_ref[...], corner_high.at[odd], corner_low.at[odd], consts)
    at_first = jnp.where(is_odd(par_ref, 0), 1.0, 0.0)
    strips = strip_halo(par_ref, before_ref, after_ref, time_high, time_low)
    for row in range(0, rows, 2):
        both = halo_sums(strips, own_high, own_low, row * cols, 2 * cols)
        for k, r in enumerate((row, row + 1)):
            value = local_ref[r] + both[:, k * cols : (k + 1) * cols]
            if r < RAD:
                value = value + parts[r] * at_first
            if r >= rows - RAD:
                value = value + parts[rows - 1 - r] * (1.0 - at_first)
            out_ref[:, r, :] = value


def edge_parts(odd, rows, first, got_e, got_o, consts, halo, factor, corner=None):
    time_high, time_low, col_both = consts
    taps = space_taps()
    for row in range(RAD):
        even, other = got_e[row], got_o[row]
        halo[row] = (choose(odd, even, other) if first else choose(odd, other, even)) * factor
    parts = []
    for k in range(0, RAD, 2):
        pair = []
        for i in (k, k + 1):
            if first:
                summed = row_sums(lambda r: halo[r + RAD], i, -RAD, 0, taps)
            else:
                summed = row_sums(lambda r: halo[r - RAD], i, RAD, 2 * RAD, taps)
            pair.append(column_sums(summed, col_both[...]))
        value = jnp.concatenate(pair, axis=1)
        width = value.shape[1]
        if corner is not None:
            parts_of, high, low = corner
            at = (k if first else RAD + k) * (width // 2)
            value = value + halo_sums(parts_of, high, low, at, width)
        both = time_sums(value, time_high[...], time_low[...])
        half = width // 2
        parts += [both[:, :half], both[:, half:]]
    return parts


def edge_parts(halo, corner, corner_high, corner_low, consts):
    time_high, time_low, col_both = consts
    hours, cols = halo.shape[1:]
    taps = space_taps()
    corner = split(unfold_corners(corner)[0:hours, 0 : corner_high.shape[0]])
    parts = []
    for k in range(0, RAD, 2):
        pair = []
        for i in (k, k + 1):
            summed = None
            for j in range(RAD - i):
                part = float(taps[RAD + i + j + 1]) * halo[j]
                summed = part if summed is None else summed + part
            pair.append(column_sums(summed, col_both[...]))
        value = jnp.concatenate(pair, axis=1) + halo_sums(corner, corner_high, corner_low, k * cols, 2 * cols)
        both = time_sums(value, time_high[...], time_low[...])
        parts += [both[:, :cols], both[:, cols:]]
    return parts


def flux_kernel(
    par_ref, local_ref, prior_ref, scale_ref, got_ref, corner_ref,
    time_high, time_low, col_both, corner_high, corner_low, flux_ref, scale_out, wide, halo,
):
    rows = local_ref.shape[0]
    odd = par_ref[0, 0]
    wide[...] = scale_ref[...].astype(F32)
    for row in range(rows):
        scale_out[row] = wide[:, row, :]
    wide[...] = prior_ref[...].astype(F32)
    for row in range(rows):
        flux_ref[row] = wide[:, row, :] + scale_out[row] * local_ref[row]
    halo[...] = got_ref[...] * (1.0 / CONTROL_FACTOR)
    consts = (time_high, time_low, col_both)
    parts = edge_parts(halo, corner_ref[...], corner_high.at[odd], corner_low.at[odd], consts)
    for k, part in enumerate(parts):
        row = jnp.where(odd == 1, k, rows - 1 - k)
        flux_ref[row] = flux_ref[row] + scale_out[row] * part


def finish_kernel(
    par_ref, model_ref, local_ref, factor_ref, got_ref, corner_ref,
    time_high, time_low, col_both, corner_high, corner_low,
    model_out, out_ref, halo, edges, total, model_own, sems,
):
    hours, rows, cols = local_ref.shape
    half = rows // 2
    odd = par_ref[0, 0]
    mine = pl.multiple_of(odd * half, half)
    rest = pl.multiple_of(half - mine, half)
    model_own[...] = model_ref[:, 0 : model_own.shape[1]]
    copies = [
        pltpu.make_async_copy(model_own, model_out, sems.at[0]),
        pltpu.make_async_copy(
            local_ref.at[:, pl.ds(rest, half), :], out_ref.at[:, pl.ds(rest, half), :], sems.at[1]
        ),
    ]
    for copy in copies:
        copy.start()
    halo[...] = got_ref[...] * factor_ref[1:2, :]
    consts = (time_high, time_low, col_both)
    parts = edge_parts(halo, corner_ref[...], corner_high.at[1 - odd], corner_low.at[1 - odd], consts)
    at_last = jnp.where(is_odd(par_ref, 0), 1.0, 0.0)
    for k, part in enumerate(parts):
        edges[:, k, :] = part * (1.0 - at_last)
        edges[:, half - 1 - k, :] = part * at_last
    total[...] = local_ref[:, pl.ds(mine, half), :] + edges[...]
    copies.append(pltpu.make_async_copy(total, out_ref.at[:, pl.ds(mine, half), :], sems.at[2]))
    copies[-1].start()
    for copy in copies:
        copy.wait()


def blocks_of(foot_ref, source, heights, slots):
    for c in range(0, slots, 2):
        both = foot_ref[source, c * heights : (c + 2) * heights, :].astype(F32)
        yield c, both[0:heights]
        yield c + 1, both[heights : 2 * heights]


def forward_kernel(
    par_ref, foot_ref, own_ref, got_ref, corner_ref, flux_hbm, scale_hbm, *refs,
    shift, slots, heights, tiles, per,
):
    distant, near = refs[0:5], refs[7:12]
    out_ref, table_ref = refs[5:7]
    flux_ref, scale_ref, halo, edges, sums, table_smem, sems = refs[12:]
    *consts, corner_high, corner_low = near
    odd = par_ref[0, 0]
    sources = foot_ref.shape[0]
    rows = flux_ref.shape[0]
    first = (rows - RAD) * odd
    pairs = list(zip(distant, near)) + [(scale_hbm.at[pl.ds(first, RAD)], scale_ref)]
    pairs += [(flux_hbm.at[r : r + RAD], flux_ref.at[r : r + RAD]) for r in range(0, rows, RAD)]
    loads = [pltpu.make_async_copy(a, b, sems.at[i]) for i, (a, b) in enumerate(pairs)]
    for load in loads:
        load.start()
    groups = out_ref.shape[1] - 1
    base = slots * heights
    lane = lane_ids((sources, LANES))
    notes = foot_ref[:, base : base + SUB, :].astype(F32)[:, 0, :].astype(jnp.int32)
    start = notes * 16 + pltpu.roll(notes, LANES - slots, 1)
    offset = start + pltpu.roll(notes, LANES - 2 * slots, 1) * (1 << shift)
    source_rec = lax.broadcasted_iota(jnp.int32, (sources, LANES), 0) // tiles
    receptor = jnp.where(notes < per, source_rec * per + notes, groups * LANES)
    table = jnp.where(lane < slots, offset, receptor)
    table_ref[...] = table
    copy = pltpu.make_async_copy(table_ref, table_smem, sems.at[len(loads)])
    copy.start()
    for load in loads[: len(near)]:
        load.wait()
    halo[...] = got_ref[...] * (1.0 / CONTROL_FACTOR)
    parts = edge_parts(halo, corner_ref[...], corner_high.at[1 - odd], corner_low.at[1 - odd], consts)
    for k, part in enumerate(parts):
        edges[k] = part
    for load in loads[len(near) :]:
        load.wait()
    for k in range(RAD):
        line = jnp.where(odd == 1, RAD - 1 - k, k)
        flux_ref[first + line] = flux_ref[first + line] + scale_ref[line] * edges[k]
    copy.wait()

    def body(source, carry):
        for c, block in blocks_of(foot_ref, source, heights, slots):
            offset = table_smem[source, c]
            row = lax.shift_right_logical(offset, shift)
            begin = jnp.bitwise_and(offset, (1 << shift) - 1)
            product = flux_ref[row, pl.ds(begin, heights), :] * block
            sums[c, pl.ds(source, 1), :] = jnp.sum(product, axis=0, keepdims=True)
        return carry

    lax.fori_loop(0, sources, body, 0)
    totals = [jnp.zeros((sources, LANES), F32) for _ in range(groups)]
    for c in range(slots):
        value = jnp.sum(sums[c], axis=1, keepdims=True)
        which = table[:, 3 * slots + c : 3 * slots + c + 1]
        for q in range(groups):
            totals[q] = totals[q] + jnp.where(which == lane + q * LANES, value, 0.0)
    for q in range(groups):
        total = jnp.sum(totals[q], axis=0, keepdims=True)
        out_ref[:, q : q + 1, :] = jnp.broadcast_to(total[None], (sources, 1, LANES))
    out_ref[:, groups : groups + 1, :] = jnp.broadcast_to(own_ref[...][None], (sources, 1, LANES))


def adjoint_kernel(
    par_ref, table_vmem, got_ref, foot_ref, scale_ref,
    model_ref, factor_ref, field_ref,
    weight_vmem, weight_smem, table_ref, sems, *, shift, slots, heights, tiles, per,
):
    load = pltpu.make_async_copy(table_vmem, table_ref, sems.at[1])
    load.start()
    sources = foot_ref.shape[0]
    groups = got_ref.shape[1] - 1
    rows, hours, _ = field_ref.shape
    model = jnp.sum(got_ref[:, 0:groups, :], axis=0)
    packed = LANES // per
    lane = lane_ids((1, LANES))
    own = jnp.zeros((1, LANES), F32)
    for q in range(groups):
        for k in range(packed):
            line = model[q : q + 1, :]
            line = line if k == 0 else pltpu.roll(line, LANES - k * per, 1)
            own = choose(par_ref[2:3, :] == q * packed + k, line, own)
    model_ref[...] = own
    weight_vmem[...] = jnp.zeros_like(weight_vmem)
    for q in range(groups):
        observed, error = jnp.zeros((1, LANES), F32), jnp.ones((1, LANES), F32)
        for k in range(packed):
            line = got_ref[(q * packed + k) * tiles, groups : groups + 1, :]
            here = (lane >= k * per) & (lane < (k + 1) * per)
            observed = jnp.where(here, line if k == 0 else pltpu.roll(line, k * per, 1), observed)
            turn = (k * per - per) % LANES
            error = jnp.where(here, line if turn == 0 else pltpu.roll(line, turn, 1), error)
        weight_vmem[q : q + 1, :] = (model[q : q + 1, :] - observed) / (error * error)
    copy = pltpu.make_async_copy(weight_vmem, weight_smem, sems.at[0])
    copy.start()
    field_ref[...] = jnp.zeros_like(field_ref)
    top = jnp.max(jnp.abs(weight_vmem[...]), keepdims=True) * (FOOT_MAX * SCALE_MAX * sources * slots)
    top = jnp.maximum(top, 1e-25)
    factor_ref[0:1, :] = jnp.broadcast_to(HALF_TOP / top, (1, LANES))
    factor_ref[1:2, :] = jnp.broadcast_to(top * (1.0 / HALF_TOP), (1, LANES))
    load.wait()
    copy.wait()

    def body(source, carry):
        for c, block in blocks_of(foot_ref, source, heights, slots):
            offset = table_ref[source, c]
            receptor = table_ref[source, 3 * slots + c]
            row = lax.shift_right_logical(offset, shift)
            begin = jnp.bitwise_and(offset, (1 << shift) - 1)
            weight = weight_smem[lax.shift_right_logical(receptor, 7), jnp.bitwise_and(receptor, LANES - 1)]
            field_ref[row, pl.ds(begin, heights), :] += block * weight
        return carry

    lax.fori_loop(0, sources, body, 0)
    for row in range(rows):
        field_ref[row] = field_ref[row] * scale_ref[row]


def swap_pairs(count, odd):
    pairs = []
    for i in range(1 if odd else 0, count - 1, 2):
        pairs += [(i, i + 1), (i + 1, i)]
    return pairs


def swap(axis, even, odd):
    count = lax.axis_size(axis)
    return (
        lax.ppermute(even, axis, swap_pairs(count, False)),
        lax.ppermute(odd, axis, swap_pairs(count, True)),
    )


VM = pl.BlockSpec(memory_space=pltpu.VMEM)
HB = pl.BlockSpec(memory_space=pltpu.HBM)


def call(kernel, out_shape, in_specs, scratch, name, out_specs=None):
    return pl.pallas_call(
        kernel,
        out_shape=out_shape,
        in_specs=in_specs,
        out_specs=jax.tree.map(lambda _: VM, out_shape) if out_specs is None else out_specs,
        scratch_shapes=scratch,
        compiler_params=pltpu.CompilerParams(vmem_limit_bytes=VMEM_LIMIT),
        name=name,
    )


def far(x):
    return pltpu.with_memory_space_constraint(x, pltpu.HBM)


def array(*shape):
    return jax.ShapeDtypeStruct(shape, F32)


def per_device(
    prior_flux,
    flux_scale,
    control,
    footprint,
    slot_count,
    start_hour,
    grid_row,
    receptor_slot,
    observed,
    obs_error,
):
    hours, rows, cols = control.shape
    n_rec, n_tile = lax.axis_size("rec"), lax.axis_size("tile")
    devices = n_rec * n_tile
    slots, heights = footprint.shape[1], footprint.shape[2]
    per = observed.shape[0]
    groups = per * n_rec // LANES
    shift = (hours - 1).bit_length()
    rec, tile = lax.axis_index("rec"), lax.axis_index("tile")
    flags = [rec % 2, rec * 0, rec, tile == 0, tile == n_tile - 1] + [rec * 0] * (SUB - 5)
    par = jnp.stack([flag.astype(jnp.int32) for flag in flags])
    par = jnp.broadcast_to(par[:, None], (SUB, LANES))
    base, own_parts, corner_parts = constants(hours, rows, cols)
    base = [jnp.asarray(c) for c in base]
    own_parts = [jnp.asarray(c) for c in own_parts]
    corner_parts = [jnp.asarray(c) for c in corner_parts]
    strip = array(-(-hours // (2 * SUB)) * SUB, LANES)
    corner = array(-(-hours // (4 * SUB)) * SUB, LANES)
    block = array(RAD, hours, cols)
    field_shape = array(rows, hours, cols)
    row_scratch = pltpu.VMEM((RAD, hours, cols), F32)

    def pass_strips(last, first):
        onward = [(i, (i + 1) % n_tile) for i in range(n_tile)]
        back = [(j, i) for i, j in onward]
        return lax.ppermute(last, "tile", onward), lax.ppermute(first, "tile", back)

    def swaps(after, field, got_strips, name):
        local = call(local_kernel, field_shape, [VM] * 5, [], name + "_local")(after, field, *base)
        corners = call(far_corner_kernel, [corner, corner], [VM] * 4, [], name + "_corners")(par, local, *got_strips)
        return local, swap("rec", *corners)

    def swap_rows(even, after, factor, field, name):
        def kernel(*refs):
            rows_kernel(*refs, even=even)

        sent = call(kernel, block, [VM] * 4, [], name)(par, after, factor, field)
        return sent, lax.ppermute(sent.astype(F16), "rec", swap_pairs(n_rec, not even))

    def prepare(*refs):
        prepare_kernel(*refs, per=per)

    numbers = pltpu.VMEM((slots, devices), jnp.int32)
    lines = slots * heights + SUB
    sent = call(
        prepare,
        jax.ShapeDtypeStruct((devices, lines, cols), BF16),
        [VM] + [HB] * 5,
        [
            pltpu.VMEM((devices, slots * heights, cols), BF16),
            pltpu.VMEM((devices, SUB, LANES), BF16),
            numbers, numbers, numbers, pltpu.VMEM((1, devices), jnp.int32),
            pltpu.SemaphoreType.DMA((5 + 2 * PARTS,)),
        ],
        "prepare_blocks",
        out_specs=HB,
    )(par, *[
        far(x)
        for x in (
            footprint.reshape(devices, slots * heights, cols),
            start_hour.T, grid_row.T, receptor_slot.T, slot_count[None],
        )
    ])
    foot = lax.all_to_all(sent, AXES, split_axis=0, concat_axis=0, tiled=True)
    field, *strips = call(
        turn_kernel, [field_shape, strip, strip], [HB, VM], [], "turn_control"
    )(sent, control)
    factor = jnp.full((2, LANES), CONTROL_FACTOR, F32)
    _, got_even = swap_rows(True, strips[0], factor, field, "control_even")
    _, got_odd = swap_rows(False, strips[0], factor, field, "control_odd")
    got_strips = pass_strips(*strips)
    local, got_corners = swaps(strips[0], field, got_strips, "control")
    local = call(strips_kernel, field_shape, [VM] * 8, [], "control_strips")(
        par, local, *got_strips, *base[:2], *own_parts
    )
    flux, scale = call(
        flux_kernel,
        [field_shape, field_shape],
        [VM] * 11,
        [pltpu.VMEM((hours, rows, cols), F32), row_scratch],
        "flux_field",
    )(par, local, prior_flux, flux_scale, got_even.astype(F32), got_corners[0], *base, *corner_parts)

    own = jnp.concatenate([observed, obs_error, jnp.zeros((LANES - 2 * per,), F32)])[None]
    sizes = dict(shift=shift, slots=slots, heights=heights, tiles=n_tile, per=per)

    def forward(*refs):
        forward_kernel(*refs, **sizes)

    foot, got_odd = lax.optimization_barrier((foot, got_odd))
    needed = [*base, *corner_parts]
    partial, table = call(
        forward,
        [array(devices, groups + 1, LANES), jax.ShapeDtypeStruct((devices, LANES), jnp.int32)],
        [VM] * 5 + [HB] * 7,
        [pltpu.VMEM(x.shape, x.dtype) for x in needed]
        + [pltpu.VMEM((rows, hours, cols), F32), row_scratch, row_scratch, row_scratch]
        + [
            pltpu.VMEM((slots, devices, LANES), F32),
            pltpu.SMEM((devices, LANES), jnp.int32),
            pltpu.SemaphoreType.DMA((len(needed) + rows // RAD + 2,)),
        ],
        "block_values",
    )(par, foot, own, got_odd.astype(F32), got_corners[1], *[far(x) for x in (flux, scale, *needed)])
    everyone = lax.all_to_all(partial, AXES, split_axis=0, concat_axis=0, tiled=True)

    def adjoint(*refs):
        adjoint_kernel(*refs, **sizes)

    weight_rows = -(-(groups + 1) // SUB) * SUB
    model, factor, field = call(
        adjoint,
        [array(1, LANES), array(2, LANES), field_shape],
        [VM] * 5,
        [
            pltpu.VMEM((weight_rows, LANES), F32),
            pltpu.SMEM((weight_rows, LANES), F32),
            pltpu.SMEM((devices, LANES), jnp.int32),
            pltpu.SemaphoreType.DMA((2,)),
        ],
        "adjoint_field",
    )(par, table, everyone, foot, scale)
    sent_even, got_even = swap_rows(True, factor, factor, field, "gradient_even")
    strips = call(strip_kernel, [strip, strip], [VM] * 2, [], "gradient_pack")(sent_even, field)
    got_strips = pass_strips(*strips)
    sent_odd, got_odd = swap_rows(False, strips[0], factor, field, "gradient_odd")
    local, got_corners = swaps(sent_odd, field, got_strips, "gradient")
    local = call(sides_kernel, array(hours, rows, cols), [VM] * 14, [row_scratch], "gradient_sides")(
        par, local, *got_strips, factor, got_even.astype(F32), got_corners[0], *base, *own_parts, *corner_parts
    )
    wide = pltpu.VMEM((hours, rows // 2, cols), F32)
    model_co2, gradient = call(
        finish_kernel,
        [array(1, per), array(hours, rows, cols)],
        [VM] * 11,
        [row_scratch, wide, wide, pltpu.VMEM((1, per), F32), pltpu.SemaphoreType.DMA((3,))],
        "gradient",
        out_specs=[HB, HB],
    )(par, model, local, factor, got_odd.astype(F32), got_corners[1], *base, *corner_parts)
    return (model_co2.reshape(-1), gradient)


def solution(mesh):
    return jax.shard_map(
        per_device,
        mesh=mesh,
        in_specs=(
            P(None, "rec", "tile"),
            P(None, "rec", "tile"),
            P(None, "rec", "tile"),
            P(("rec", "tile"), None, None, None),
            P(("rec", "tile")),
            P(("rec", "tile"), None),
            P(("rec", "tile"), None),
            P(("rec", "tile"), None),
            P("rec"),
            P("rec"),
        ),
        out_specs=(P("rec"), P(None, "rec", "tile")),
        check_vma=False,
    )
```

```python
import numpy as np
import jax
import jax.numpy as jnp
from jax import lax
from jax.experimental import pallas as pl
from jax.experimental.pallas import tpu as pltpu
from jax.sharding import PartitionSpec as P

RAD = 4
TAPS = 12
AXES = ("rec", "tile")
LANES = 128
SUB = 8
FOOT_MAX = 0.02
PARTS = 4
SCALE_MAX = 2.0
HALF_TOP = 32768.0
F16 = jnp.float16
VMEM_LIMIT = 14 * 1024 * 1024
F32 = jnp.float32
BF16 = jnp.bfloat16


def space_taps():
    offsets = np.arange(-RAD, RAD + 1).astype(np.float64)
    values = np.exp(-2.0 * offsets * offsets / (RAD * RAD))
    return values / np.sqrt(np.sum(values * values))


def time_taps():
    offsets = np.arange(-TAPS, TAPS + 1).astype(np.float64)
    values = np.exp(-2.0 * np.abs(offsets) / TAPS)
    return values / np.sqrt(np.sum(values * values))


def banded(distance, taps, reach):
    inside = np.abs(distance) <= reach
    return np.where(inside, taps[np.clip(distance, -reach, reach) + reach], 0.0)


def two_parts(matrix):
    high = matrix.astype(np.float32).astype(jnp.bfloat16)
    low = (matrix - high.astype(np.float64)).astype(np.float32).astype(jnp.bfloat16)
    return high, low


def constants(hours, rows, cols):
    space = space_taps()
    hour = np.arange(hours)
    time_high, time_low = two_parts(banded(hour[:, None] - hour[None, :], time_taps(), TAPS))
    col = np.arange(cols)
    col_high, col_low = two_parts(banded(col[:, None] - col[None, :], space, RAD))
    col_both = np.block([[col_high, col_low], [col_high, np.zeros_like(col_high)]])
    halo_col = np.concatenate([np.arange(-RAD, 0), np.arange(cols, cols + RAD)])
    edge = banded(halo_col[:, None] - col[None, :], space, RAD)

    def strips(row_of, halo_of, targets):
        by_row = banded(np.array(row_of)[:, None] - np.array(targets)[None, :], space, RAD)
        both = by_row[:, :, None] * edge[np.array(halo_of)][:, None, :]
        return two_parts(both.reshape(len(row_of), -1))

    own = [(row, side * RAD + j) for side in range(2) for row in range(rows) for j in range(RAD)]
    corner = [], []
    for first, targets in ((rows, rows - 1 - np.arange(RAD)), (-RAD, np.arange(RAD))):
        lanes = [
            (row, side * RAD + j) for side in range(2) for row in range(first, first + RAD) for j in range(RAD)
        ]
        for part, value in zip(corner, strips(*zip(*lanes), targets)):
            part.append(value)
    beyond = [strips(*zip(*own), rows + np.arange(RAD)), strips(*zip(*own), -1 - np.arange(RAD))]
    return (
        (time_high, time_low, col_both),
        strips(*zip(*own), np.arange(rows)),
        [np.stack(c) for c in corner],
        [np.stack(c) for c in zip(*beyond)],
    )


def split(value):
    high = value.astype(BF16)
    low = (value - high.astype(F32)).astype(BF16)
    return high, low


def dot(a, b):
    return jnp.dot(a, b, preferred_element_type=F32)


def lane_ids(shape):
    return lax.broadcasted_iota(jnp.int32, shape, 1)


def choose(flag, yes, no):
    return jnp.where(flag, yes, no)


def pack_strips(row_value, rows):
    cols = row_value(0).shape[1]
    half = rows * RAD
    source = lax.broadcasted_iota(jnp.int32, (cols, 2 * half), 0)
    lane = lane_ids((cols, 2 * half))
    first = lane < half
    j = lane & (RAD - 1)
    wanted = jnp.where(first, cols - RAD + j, j)
    lane_row = jnp.where(first, lane, lane - half) // RAD
    total = None
    for row in range(rows):
        high, low = split(row_value(row))
        pick = jnp.where((source == wanted) & (lane_row == row), 1.0, 0.0).astype(BF16)
        part = dot(jnp.concatenate([high, low], axis=1), jnp.concatenate([pick, pick], axis=0))
        total = part if total is None else total + part
    return total


def fold_corners(odd, strips, corner_e, corner_o):
    quarter = corner_e.shape[0]
    half, part = LANES // 2, RAD * RAD
    lane = lane_ids((quarter, LANES))
    spare = jnp.zeros((4 * quarter - strips.shape[0], LANES), F32)
    whole = jnp.concatenate([strips, spare], axis=0)
    low = high = jnp.zeros((quarter, LANES), F32)
    for q in range(LANES // (2 * part)):
        piece = whole[q * quarter : (q + 1) * quarter]
        for side in range(2):
            to = q * 2 * part + side * part
            here = (lane >= to) & (lane < to + part)
            low = choose(here, pltpu.roll(piece, (to - side * half) % LANES, 1), low)
            high = choose(here, pltpu.roll(piece, (to - side * half - (half - part)) % LANES, 1), high)
    corner_e[...] = choose(odd, low, high)
    corner_o[...] = choose(odd, high, low)


def unfold_corners(value):
    part = 2 * RAD * RAD
    pieces = [value] + [pltpu.roll(value, LANES - q * part, 1) for q in range(1, LANES // part)]
    return jnp.concatenate(pieces, axis=0)


def is_odd(par_ref, axis):
    return par_ref[axis : axis + 1, :] == 1


def rows_kernel(par_ref, after, factor_ref, field_ref, out_ref, *, even):
    odd = is_odd(par_ref, 0)
    factor = factor_ref[0:1, :]
    rows = field_ref.shape[0]
    for row in range(RAD):
        first, last = field_ref[row], field_ref[rows - 1 - row]
        out_ref[row] = (choose(odd, first, last) if even else choose(odd, last, first)) * factor


def turn_kernel(after, control_ref, field_ref, last_ref, first_ref):
    rows = control_ref.shape[1]
    for row in range(rows):
        field_ref[row] = control_ref[:, row, :]
    write_strips(field_ref, last_ref, first_ref)


def strip_kernel(after, field_ref, last_ref, first_ref):
    write_strips(field_ref, last_ref, first_ref)


def write_strips(field_ref, last_ref, first_ref):
    strips = pack_strips(lambda r: field_ref[r], field_ref.shape[0])
    fold, half = last_ref.shape[0], LANES // 2
    early, late = strips[0:fold], strips[fold:]
    if late.shape[0] < fold:
        late = jnp.concatenate([late, jnp.zeros((fold - late.shape[0], LANES), F32)], axis=0)
    left = lane_ids(early.shape) < half
    last_ref[...] = jnp.where(left, early, pltpu.roll(late, half, 1))
    first_ref[...] = jnp.where(left, pltpu.roll(early, half, 1), late)


def halo_columns(par_ref, before_ref, after_ref):
    before, after = before_ref[...], after_ref[...]
    half = LANES // 2
    left = lane_ids(before.shape) < half
    early = jnp.where(left, before, pltpu.roll(after, half, 1))
    late = jnp.where(left, pltpu.roll(before, half, 1), after)
    outside = jnp.where(lane_ids((1, LANES)) < half, par_ref[3:4, :], par_ref[4:5, :])
    return jnp.where(outside == 1, 0.0, jnp.concatenate([early, late], axis=0))


def far_corner_kernel(par_ref, after, before_ref, after_ref, corner_e, corner_o):
    fold_corners(is_odd(par_ref, 0), halo_columns(par_ref, before_ref, after_ref), corner_e, corner_o)


def prepare_kernel(
    after, foot_ref, start_ref, row_ref, slot_ref, count_ref, out_ref,
    blocks_ref, notes_ref, start_vmem, row_vmem, slot_vmem, count_vmem, sems, *, per,
):
    owners, lines, _ = foot_ref.shape
    slots = start_ref.shape[0]
    pairs = ((start_ref, start_vmem), (row_ref, row_vmem), (slot_ref, slot_vmem), (count_ref, count_vmem))
    small = [pltpu.make_async_copy(a, b, sems.at[i]) for i, (a, b) in enumerate(pairs)]
    chunk = owners // PARTS
    parts = [slice(i * chunk, (i + 1) * chunk) for i in range(PARTS)]
    loads = [
        pltpu.make_async_copy(foot_ref.at[here], blocks_ref.at[here], sems.at[4 + i])
        for i, here in enumerate(parts)
    ]
    for copy in small + loads:
        copy.start()
    stores = []
    for i, here in enumerate(parts):
        loads[i].wait()
        to = out_ref.at[here, 0:lines, :]
        stores.append(pltpu.make_async_copy(blocks_ref.at[here], to, sems.at[4 + PARTS + i]))
        stores[-1].start()
    for copy in small:
        copy.wait()
    start = start_vmem[...]
    valid = lax.broadcasted_iota(jnp.int32, start.shape, 0) < count_vmem[...]
    lanes = jnp.concatenate(
        [start >> 4, start & 15, row_vmem[...], jnp.where(valid, slot_vmem[...], per)], axis=0
    ).astype(F32)
    wide = jnp.pad(lanes, ((0, LANES - 4 * slots), (0, LANES - owners)))
    turned = jnp.transpose(wide)[0:owners]
    notes_ref[...] = jnp.broadcast_to(turned[:, None, :], notes_ref.shape).astype(BF16)
    stores.append(pltpu.make_async_copy(notes_ref, out_ref.at[:, lines : lines + SUB, :], sems.at[4 + 2 * PARTS]))
    stores[-1].start()
    for copy in stores:
        copy.wait()


def halo_sums(parts, high_ref, low_ref, first, width):
    high, low = parts
    weights = high_ref[:, first : first + width]
    return dot(high, weights) + dot(low, weights) + dot(high, low_ref[:, first : first + width])


def column_sums(value, col_both):
    cols = value.shape[1]
    high, low = split(value)
    out = dot(jnp.concatenate([high, low], axis=1), col_both)
    return out[:, :cols] + out[:, cols:]


def time_sums(value, time_high, time_low):
    high, low = split(value)
    return dot(time_high, high) + dot(time_high, low) + dot(time_low, high)


def row_sums(get, row, low, high, taps):
    total = None
    for distance in range(RAD + 1):
        here = [get(r) for r in sorted({row - distance, row + distance}) if low <= r < high]
        if not here:
            continue
        part = here[0] if len(here) == 1 else here[0] + here[1]
        part = float(taps[RAD + distance]) * part
        total = part if total is None else total + part
    return total


def local_kernel(after, field_ref, time_high, time_low, col_both, out_ref):
    rows, hours, cols = field_ref.shape
    taps = space_taps()
    for row in range(0, rows, 2):
        pair = [
            column_sums(row_sums(lambda i: field_ref[i], r, 0, rows, taps), col_both[...])
            for r in (row, row + 1)
        ]
        both = time_sums(jnp.concatenate(pair, axis=1), time_high[...], time_low[...])
        for k, r in enumerate((row, row + 1)):
            out_ref[r] = both[:, k * cols : (k + 1) * cols]


def strip_halo(par_ref, before_ref, after_ref, time_high, time_low):
    halo = halo_columns(par_ref, before_ref, after_ref)[0 : time_high.shape[0]]
    return split(time_sums(halo, time_high[...], time_low[...]))


def strips_kernel(par_ref, local_ref, before_ref, after_ref, time_high, time_low, own_high, own_low, out_ref):
    rows, hours, cols = local_ref.shape
    halo = strip_halo(par_ref, before_ref, after_ref, time_high, time_low)
    for row in range(0, rows, 2):
        both = halo_sums(halo, own_high, own_low, row * cols, 2 * cols)
        for k, r in enumerate((row, row + 1)):
            out_ref[r] = local_ref[r] + both[:, k * cols : (k + 1) * cols]


def sides_kernel(
    par_ref, local_ref, before_ref, after_ref, factor_ref, got_ref, corner_ref,
    time_high, time_low, col_both, own_high, own_low, corner_high, corner_low, out_ref, halo,
):
    rows, hours, cols = local_ref.shape
    odd = par_ref[0, 0]
    halo[...] = got_ref[...] * factor_ref[1:2, :]
    consts = (time_high, time_low, col_both)
    parts = edge_parts(halo, corner_ref[...], corner_high.at[odd], corner_low.at[odd], consts)
    at_first = jnp.where(is_odd(par_ref, 0), 1.0, 0.0)
    strips = strip_halo(par_ref, before_ref, after_ref, time_high, time_low)
    for row in range(0, rows, 2):
        both = halo_sums(strips, own_high, own_low, row * cols, 2 * cols)
        for k, r in enumerate((row, row + 1)):
            value = local_ref[r] + both[:, k * cols : (k + 1) * cols]
            if r < RAD:
                value = value + parts[r] * at_first
            if r >= rows - RAD:
                value = value + parts[rows - 1 - r] * (1.0 - at_first)
            out_ref[:, r, :] = value


def beyond_sums(rows, corner, corner_high, corner_low, consts):
    time_high, time_low, col_both = consts
    cols = col_both.shape[1] // 2
    taps = space_taps()
    parts = []
    for k in range(0, RAD, 2):
        pair = []
        for i in (k, k + 1):
            summed = None
            for j in range(RAD - i):
                part = float(taps[RAD + i + j + 1]) * rows(j)
                summed = part if summed is None else summed + part
            pair.append(column_sums(summed, col_both[...]))
        value = jnp.concatenate(pair, axis=1) + halo_sums(corner, corner_high, corner_low, k * cols, 2 * cols)
        both = time_sums(value, time_high[...], time_low[...])
        parts += [both[:, :cols], both[:, cols:]]
    return parts


def edge_parts(halo, corner, corner_high, corner_low, consts):
    corner = split(unfold_corners(corner)[0 : halo.shape[1], 0 : corner_high.shape[0]])
    return beyond_sums(lambda j: halo[j], corner, corner_high, corner_low, consts)


def beyond_kernel(
    par_ref, field_ref, before_ref, after_ref, time_high, time_low, col_both, beyond_high, beyond_low,
    out_even, out_odd,
):
    rows, hours, _ = field_ref.shape
    odd = is_odd(par_ref, 0)
    halo = split(halo_columns(par_ref, before_ref, after_ref)[0:hours])
    consts = (time_high, time_low, col_both)
    to_after = beyond_sums(
        lambda j: field_ref[rows - 1 - j], halo, beyond_high.at[0], beyond_low.at[0], consts
    )
    to_before = beyond_sums(lambda j: field_ref[j], halo, beyond_high.at[1], beyond_low.at[1], consts)
    for k in range(RAD):
        out_even[k] = choose(odd, to_before[k], to_after[k]).astype(BF16)
        out_odd[k] = choose(odd, to_after[k], to_before[k]).astype(BF16)


def flux_kernel(par_ref, local_ref, prior_ref, scale_ref, got_ref, flux_ref, scale_out, wide):
    rows = local_ref.shape[0]
    odd = par_ref[0, 0]
    wide[...] = scale_ref[...].astype(F32)
    for row in range(rows):
        scale_out[row] = wide[:, row, :]
    wide[...] = prior_ref[...].astype(F32)
    for row in range(rows):
        flux_ref[row] = wide[:, row, :] + scale_out[row] * local_ref[row]
    for k in range(RAD):
        row = jnp.where(odd == 1, k, rows - 1 - k)
        flux_ref[row] = flux_ref[row] + scale_out[row] * got_ref[k].astype(F32)


def finish_kernel(
    par_ref, model_ref, local_ref, factor_ref, got_ref, corner_ref,
    time_high, time_low, col_both, corner_high, corner_low,
    model_out, out_ref, halo, edges, total, model_own, sems,
):
    hours, rows, cols = local_ref.shape
    half = rows // 2
    odd = par_ref[0, 0]
    mine = pl.multiple_of(odd * half, half)
    rest = pl.multiple_of(half - mine, half)
    model_own[...] = model_ref[:, 0 : model_own.shape[1]]
    copies = [
        pltpu.make_async_copy(model_own, model_out, sems.at[0]),
        pltpu.make_async_copy(
            local_ref.at[:, pl.ds(rest, half), :], out_ref.at[:, pl.ds(rest, half), :], sems.at[1]
        ),
    ]
    for copy in copies:
        copy.start()
    halo[...] = got_ref[...] * factor_ref[1:2, :]
    consts = (time_high, time_low, col_both)
    parts = edge_parts(halo, corner_ref[...], corner_high.at[1 - odd], corner_low.at[1 - odd], consts)
    at_last = jnp.where(is_odd(par_ref, 0), 1.0, 0.0)
    for k, part in enumerate(parts):
        edges[:, k, :] = part * (1.0 - at_last)
        edges[:, half - 1 - k, :] = part * at_last
    total[...] = local_ref[:, pl.ds(mine, half), :] + edges[...]
    copies.append(pltpu.make_async_copy(total, out_ref.at[:, pl.ds(mine, half), :], sems.at[2]))
    copies[-1].start()
    for copy in copies:
        copy.wait()


def blocks_of(foot_ref, source, heights, slots):
    for c in range(0, slots, 2):
        both = foot_ref[source, c * heights : (c + 2) * heights, :].astype(F32)
        yield c, both[0:heights]
        yield c + 1, both[heights : 2 * heights]


def load_kernel(
    par_ref, foot_ref, scale_far, *refs, shift, slots, heights, tiles, per, empty
):
    count = (len(refs) - 3) // 2
    distant, (table_ref, scale_ref), near = refs[:count], refs[count : count + 2], refs[count + 2 : -1]
    sems = refs[-1]
    flux_far, flux_ref = distant[0], near[0]
    rows = flux_ref.shape[0]
    first = (rows - RAD) * par_ref[0, 0]
    pairs = [(flux_far.at[r : r + RAD], flux_ref.at[r : r + RAD]) for r in range(0, rows, RAD)]
    pairs += list(zip(distant[1:], near[1:])) + [(scale_far.at[pl.ds(first, RAD)], scale_ref)]
    loads = [pltpu.make_async_copy(a, b, sems.at[i]) for i, (a, b) in enumerate(pairs)]
    for load in loads:
        load.start()
    sources = foot_ref.shape[0]
    base = slots * heights
    lane = lane_ids((sources, LANES))
    notes = foot_ref[:, base : base + SUB, :].astype(F32)[:, 0, :].astype(jnp.int32)
    start = notes * 16 + pltpu.roll(notes, LANES - slots, 1)
    offset = start + pltpu.roll(notes, LANES - 2 * slots, 1) * (1 << shift)
    source_rec = lax.broadcasted_iota(jnp.int32, (sources, LANES), 0) // tiles
    receptor = jnp.where(notes < per, source_rec * per + notes, empty)
    table_ref[...] = jnp.where(lane < slots, offset, receptor)
    for load in loads:
        load.wait()


def forward_kernel(
    par_ref, foot_ref, table_ref, own_ref, got_far, flux_in, scale_ref,
    out_ref, flux_ref, got_ref, sums, table_smem, sems, *, shift, slots, heights, tiles, per,
):
    load = pltpu.make_async_copy(got_far, got_ref, sems.at[1])
    load.start()
    odd = par_ref[0, 0]
    sources = foot_ref.shape[0]
    rows = flux_ref.shape[0]
    first = (rows - RAD) * odd
    groups = out_ref.shape[1] - 1
    lane = lane_ids((sources, LANES))
    table = table_ref[...]
    copy = pltpu.make_async_copy(table_ref, table_smem, sems.at[0])
    copy.start()
    load.wait()
    for k in range(RAD):
        line = jnp.where(odd == 1, RAD - 1 - k, k)
        flux_ref[first + line] = flux_in[first + line] + scale_ref[line] * got_ref[k].astype(F32)
    copy.wait()

    def body(source, carry):
        for c, block in blocks_of(foot_ref, source, heights, slots):
            offset = table_smem[source, c]
            row = lax.shift_right_logical(offset, shift)
            begin = jnp.bitwise_and(offset, (1 << shift) - 1)
            product = flux_ref[row, pl.ds(begin, heights), :] * block
            sums[c, pl.ds(source, 1), :] = jnp.sum(product, axis=0, keepdims=True)
        return carry

    lax.fori_loop(0, sources, body, 0)
    totals = [jnp.zeros((sources, LANES), F32) for _ in range(groups)]
    for c in range(slots):
        value = jnp.sum(sums[c], axis=1, keepdims=True)
        which = table[:, 3 * slots + c : 3 * slots + c + 1]
        for q in range(groups):
            totals[q] = totals[q] + jnp.where(which == lane + q * LANES, value, 0.0)
    for q in range(groups):
        total = jnp.sum(totals[q], axis=0, keepdims=True)
        out_ref[:, q : q + 1, :] = jnp.broadcast_to(total[None], (sources, 1, LANES))
    out_ref[:, groups : groups + 1, :] = jnp.broadcast_to(own_ref[...][None], (sources, 1, LANES))


def adjoint_kernel(
    par_ref, table_vmem, got_ref, foot_ref, scale_ref,
    model_ref, factor_ref, field_ref,
    weight_vmem, weight_smem, table_ref, sems, *, shift, slots, heights, tiles, per,
):
    load = pltpu.make_async_copy(table_vmem, table_ref, sems.at[1])
    load.start()
    sources = foot_ref.shape[0]
    groups = got_ref.shape[1] - 1
    rows, hours, _ = field_ref.shape
    model = jnp.sum(got_ref[:, 0:groups, :], axis=0)
    packed = LANES // per
    lane = lane_ids((1, LANES))
    own = jnp.zeros((1, LANES), F32)
    for q in range(groups):
        for k in range(packed):
            line = model[q : q + 1, :]
            line = line if k == 0 else pltpu.roll(line, LANES - k * per, 1)
            own = choose(par_ref[2:3, :] == q * packed + k, line, own)
    model_ref[...] = own
    weight_vmem[...] = jnp.zeros_like(weight_vmem)
    for q in range(groups):
        observed, error = jnp.zeros((1, LANES), F32), jnp.ones((1, LANES), F32)
        for k in range(packed):
            line = got_ref[(q * packed + k) * tiles, groups : groups + 1, :]
            here = (lane >= k * per) & (lane < (k + 1) * per)
            observed = jnp.where(here, line if k == 0 else pltpu.roll(line, k * per, 1), observed)
            turn = (k * per - per) % LANES
            error = jnp.where(here, line if turn == 0 else pltpu.roll(line, turn, 1), error)
        weight_vmem[q : q + 1, :] = (model[q : q + 1, :] - observed) / (error * error)
    copy = pltpu.make_async_copy(weight_vmem, weight_smem, sems.at[0])
    copy.start()
    field_ref[...] = jnp.zeros_like(field_ref)
    top = jnp.max(jnp.abs(weight_vmem[...]), keepdims=True) * (FOOT_MAX * SCALE_MAX * sources * slots)
    top = jnp.maximum(top, 1e-25)
    factor_ref[0:1, :] = jnp.broadcast_to(HALF_TOP / top, (1, LANES))
    factor_ref[1:2, :] = jnp.broadcast_to(top * (1.0 / HALF_TOP), (1, LANES))
    load.wait()
    copy.wait()

    def body(source, carry):
        for c, block in blocks_of(foot_ref, source, heights, slots):
            offset = table_ref[source, c]
            receptor = table_ref[source, 3 * slots + c]
            row = lax.shift_right_logical(offset, shift)
            begin = jnp.bitwise_and(offset, (1 << shift) - 1)
            weight = weight_smem[lax.shift_right_logical(receptor, 7), jnp.bitwise_and(receptor, LANES - 1)]
            field_ref[row, pl.ds(begin, heights), :] += block * weight
        return carry

    lax.fori_loop(0, sources, body, 0)
    for row in range(rows):
        field_ref[row] = field_ref[row] * scale_ref[row]


def swap_pairs(count, odd):
    pairs = []
    for i in range(1 if odd else 0, count - 1, 2):
        pairs += [(i, i + 1), (i + 1, i)]
    return pairs


def swap(axis, even, odd):
    count = lax.axis_size(axis)
    return (
        lax.ppermute(even, axis, swap_pairs(count, False)),
        lax.ppermute(odd, axis, swap_pairs(count, True)),
    )


VM = pl.BlockSpec(memory_space=pltpu.VMEM)
HB = pl.BlockSpec(memory_space=pltpu.HBM)


def call(kernel, out_shape, in_specs, scratch, name, out_specs=None, alias=None):
    return pl.pallas_call(
        kernel,
        out_shape=out_shape,
        in_specs=in_specs,
        out_specs=jax.tree.map(lambda _: VM, out_shape) if out_specs is None else out_specs,
        scratch_shapes=scratch,
        input_output_aliases={} if alias is None else alias,
        compiler_params=pltpu.CompilerParams(vmem_limit_bytes=VMEM_LIMIT),
        name=name,
    )


def far(x):
    return pltpu.with_memory_space_constraint(x, pltpu.HBM)


def array(*shape):
    return jax.ShapeDtypeStruct(shape, F32)


def per_device(
    prior_flux,
    flux_scale,
    control,
    footprint,
    slot_count,
    start_hour,
    grid_row,
    receptor_slot,
    observed,
    obs_error,
):
    hours, rows, cols = control.shape
    n_rec, n_tile = lax.axis_size("rec"), lax.axis_size("tile")
    devices = n_rec * n_tile
    slots, heights = footprint.shape[1], footprint.shape[2]
    per = observed.shape[0]
    groups = per * n_rec // LANES
    shift = (hours - 1).bit_length()
    rec, tile = lax.axis_index("rec"), lax.axis_index("tile")
    flags = [rec % 2, rec * 0, rec, tile == 0, tile == n_tile - 1] + [rec * 0] * (SUB - 5)
    par = jnp.stack([flag.astype(jnp.int32) for flag in flags])
    par = jnp.broadcast_to(par[:, None], (SUB, LANES))
    base, own_parts, corner_parts, beyond_parts = constants(hours, rows, cols)
    base = [jnp.asarray(c) for c in base]
    own_parts = [jnp.asarray(c) for c in own_parts]
    corner_parts = [jnp.asarray(c) for c in corner_parts]
    beyond_parts = [jnp.asarray(c) for c in beyond_parts]
    strip = array(-(-hours // (2 * SUB)) * SUB, LANES)
    corner = array(-(-hours // (4 * SUB)) * SUB, LANES)
    block = array(RAD, hours, cols)
    field_shape = array(rows, hours, cols)
    row_scratch = pltpu.VMEM((RAD, hours, cols), F32)

    def pass_strips(last, first):
        onward = [(i, (i + 1) % n_tile) for i in range(n_tile)]
        back = [(j, i) for i, j in onward]
        return lax.ppermute(last, "tile", onward), lax.ppermute(first, "tile", back)

    def swaps(after, field, got_strips, name):
        local = call(local_kernel, field_shape, [VM] * 5, [], name + "_local")(after, field, *base)
        corners = call(far_corner_kernel, [corner, corner], [VM] * 4, [], name + "_corners")(par, local, *got_strips)
        return local, swap("rec", *corners)

    def swap_rows(even, after, factor, field, name):
        def kernel(*refs):
            rows_kernel(*refs, even=even)

        sent = call(kernel, block, [VM] * 4, [], name)(par, after, factor, field)
        return sent, lax.ppermute(sent.astype(F16), "rec", swap_pairs(n_rec, not even))

    def prepare(*refs):
        prepare_kernel(*refs, per=per)

    numbers = pltpu.VMEM((slots, devices), jnp.int32)
    lines = slots * heights + SUB
    sent = call(
        prepare,
        jax.ShapeDtypeStruct((devices, lines, cols), BF16),
        [VM] + [HB] * 5,
        [
            pltpu.VMEM((devices, slots * heights, cols), BF16),
            pltpu.VMEM((devices, SUB, LANES), BF16),
            numbers, numbers, numbers, pltpu.VMEM((1, devices), jnp.int32),
            pltpu.SemaphoreType.DMA((5 + 2 * PARTS,)),
        ],
        "prepare_blocks",
        out_specs=HB,
    )(par, *[
        far(x)
        for x in (
            footprint.reshape(devices, slots * heights, cols),
            start_hour.T, grid_row.T, receptor_slot.T, slot_count[None],
        )
    ])
    foot = lax.all_to_all(sent, AXES, split_axis=0, concat_axis=0, tiled=True)
    field, *strips = call(
        turn_kernel, [field_shape, strip, strip], [HB, VM], [], "turn_control"
    )(sent, control)
    got_strips = pass_strips(*strips)
    local = call(local_kernel, field_shape, [VM] * 5, [], "control_local")(strips[0], field, *base)
    small = jax.ShapeDtypeStruct((RAD, hours, cols), BF16)
    sent_even, sent_odd = call(beyond_kernel, [small, small], [VM] * 9, [], "control_beyond")(
        par, field, *got_strips, *base, *beyond_parts
    )
    got_even, got_odd = swap("rec", sent_even, sent_odd)
    local = call(strips_kernel, field_shape, [VM] * 8, [], "control_strips")(
        par, local, *got_strips, *base[:2], *own_parts
    )
    flux, scale = call(
        flux_kernel, [field_shape, field_shape], [VM] * 5, [pltpu.VMEM((hours, rows, cols), F32)], "flux_field"
    )(par, local, prior_flux, flux_scale, got_even)

    own = jnp.concatenate([observed, obs_error, jnp.zeros((LANES - 2 * per,), F32)])[None]
    sizes = dict(shift=shift, slots=slots, heights=heights, tiles=n_tile, per=per)

    def forward(*refs):
        forward_kernel(*refs, **sizes)


    def load(*refs):
        load_kernel(*refs, empty=groups * LANES, **sizes)

    table, scale_near, flux_near = call(
        load,
        [jax.ShapeDtypeStruct((devices, LANES), jnp.int32), block, field_shape],
        [VM, VM, HB, HB],
        [pltpu.SemaphoreType.DMA((1 + rows // RAD,))],
        "load_flux",
    )(par, foot, far(scale), far(flux))
    table, got_odd = lax.optimization_barrier((table, got_odd))
    partial, _ = call(
        forward,
        [array(devices, groups + 1, LANES), field_shape],
        [VM] * 4 + [HB] + [VM] * 2,
        [
            pltpu.VMEM((RAD, hours, cols), BF16),
            pltpu.VMEM((slots, devices, LANES), F32),
            pltpu.SMEM((devices, LANES), jnp.int32),
            pltpu.SemaphoreType.DMA((2,)),
        ],
        "block_values",
        alias={5: 1},
    )(par, foot, table, own, far(got_odd), flux_near, scale_near)
    everyone = lax.all_to_all(partial, AXES, split_axis=0, concat_axis=0, tiled=True)

    def adjoint(*refs):
        adjoint_kernel(*refs, **sizes)

    weight_rows = -(-(groups + 1) // SUB) * SUB
    model, factor, field = call(
        adjoint,
        [array(1, LANES), array(2, LANES), field_shape],
        [VM] * 5,
        [
            pltpu.VMEM((weight_rows, LANES), F32),
            pltpu.SMEM((weight_rows, LANES), F32),
            pltpu.SMEM((devices, LANES), jnp.int32),
            pltpu.SemaphoreType.DMA((2,)),
        ],
        "adjoint_field",
    )(par, table, everyone, foot, scale)
    sent_even, got_even = swap_rows(True, factor, factor, field, "gradient_even")
    strips = call(strip_kernel, [strip, strip], [VM] * 2, [], "gradient_pack")(sent_even, field)
    got_strips = pass_strips(*strips)
    sent_odd, got_odd = swap_rows(False, strips[0], factor, field, "gradient_odd")
    local, got_corners = swaps(sent_odd, field, got_strips, "gradient")
    local = call(sides_kernel, array(hours, rows, cols), [VM] * 14, [row_scratch], "gradient_sides")(
        par, local, *got_strips, factor, got_even.astype(F32), got_corners[0], *base, *own_parts, *corner_parts
    )
    wide = pltpu.VMEM((hours, rows // 2, cols), F32)
    model_co2, gradient = call(
        finish_kernel,
        [array(1, per), array(hours, rows, cols)],
        [VM] * 11,
        [row_scratch, wide, wide, pltpu.VMEM((1, per), F32), pltpu.SemaphoreType.DMA((3,))],
        "gradient",
        out_specs=[HB, HB],
    )(par, model, local, factor, got_odd.astype(F32), got_corners[1], *base, *corner_parts)
    return (model_co2.reshape(-1), gradient)


def solution(mesh):
    return jax.shard_map(
        per_device,
        mesh=mesh,
        in_specs=(
            P(None, "rec", "tile"),
            P(None, "rec", "tile"),
            P(None, "rec", "tile"),
            P(("rec", "tile"), None, None, None),
            P(("rec", "tile")),
            P(("rec", "tile"), None),
            P(("rec", "tile"), None),
            P(("rec", "tile"), None),
            P("rec"),
            P("rec"),
        ),
        out_specs=(P("rec"), P(None, "rec", "tile")),
        check_vma=False,
    )
```

```python
import numpy as np
import jax
import jax.numpy as jnp
from jax import lax
from jax.experimental import pallas as pl
from jax.experimental.pallas import tpu as pltpu
from jax.sharding import PartitionSpec as P

RAD = 4
TAPS = 12
AXES = ("rec", "tile")
LANES = 128
SUB = 8
FOOT_MAX = 0.02
PARTS = 4
SCALE_MAX = 2.0
HALF_TOP = 32768.0
F16 = jnp.float16
VMEM_LIMIT = 14 * 1024 * 1024
F32 = jnp.float32
BF16 = jnp.bfloat16


def space_taps():
    offsets = np.arange(-RAD, RAD + 1).astype(np.float64)
    values = np.exp(-2.0 * offsets * offsets / (RAD * RAD))
    return values / np.sqrt(np.sum(values * values))


def time_taps():
    offsets = np.arange(-TAPS, TAPS + 1).astype(np.float64)
    values = np.exp(-2.0 * np.abs(offsets) / TAPS)
    return values / np.sqrt(np.sum(values * values))


def banded(distance, taps, reach):
    inside = np.abs(distance) <= reach
    return np.where(inside, taps[np.clip(distance, -reach, reach) + reach], 0.0)


def two_parts(matrix):
    high = matrix.astype(np.float32).astype(jnp.bfloat16)
    low = (matrix - high.astype(np.float64)).astype(np.float32).astype(jnp.bfloat16)
    return high, low


def constants(hours, rows, cols):
    space = space_taps()
    hour = np.arange(hours)
    time_high, time_low = two_parts(banded(hour[:, None] - hour[None, :], time_taps(), TAPS))
    col = np.arange(cols)
    col_high, col_low = two_parts(banded(col[:, None] - col[None, :], space, RAD))
    col_both = np.block([[col_high, col_low], [col_high, np.zeros_like(col_high)]])
    halo_col = np.concatenate([np.arange(-RAD, 0), np.arange(cols, cols + RAD)])
    edge = banded(halo_col[:, None] - col[None, :], space, RAD)

    def strips(row_of, halo_of, targets):
        by_row = banded(np.array(row_of)[:, None] - np.array(targets)[None, :], space, RAD)
        both = by_row[:, :, None] * edge[np.array(halo_of)][:, None, :]
        high, low = two_parts(both.reshape(len(row_of), -1))
        return np.concatenate([high, high, low], axis=0)

    own = [(row, side * RAD + j) for side in range(2) for row in range(rows) for j in range(RAD)]
    corner = []
    for first, targets in ((rows, rows - 1 - np.arange(RAD)), (-RAD, np.arange(RAD))):
        lanes = [
            (row, side * RAD + j) for side in range(2) for row in range(first, first + RAD) for j in range(RAD)
        ]
        corner.append(strips(*zip(*lanes), targets))
    beyond = [strips(*zip(*own), rows + np.arange(RAD)), strips(*zip(*own), -1 - np.arange(RAD))]
    return (
        (time_high, time_low, col_both),
        strips(*zip(*own), np.arange(rows)),
        np.stack(corner),
        np.stack(beyond),
    )


def split(value):
    high = value.astype(BF16)
    low = (value - high.astype(F32)).astype(BF16)
    return high, low


def dot(a, b):
    return jnp.dot(a, b, preferred_element_type=F32)


def lane_ids(shape):
    return lax.broadcasted_iota(jnp.int32, shape, 1)


def choose(flag, yes, no):
    return jnp.where(flag, yes, no)


def pack_strips(row_value, rows):
    cols = row_value(0).shape[1]
    half = rows * RAD
    source = lax.broadcasted_iota(jnp.int32, (cols, 2 * half), 0)
    lane = lane_ids((cols, 2 * half))
    first = lane < half
    j = lane & (RAD - 1)
    wanted = jnp.where(first, cols - RAD + j, j)
    lane_row = jnp.where(first, lane, lane - half) // RAD
    total = None
    for row in range(rows):
        high, low = split(row_value(row))
        pick = jnp.where((source == wanted) & (lane_row == row), 1.0, 0.0).astype(BF16)
        part = dot(jnp.concatenate([high, low], axis=1), jnp.concatenate([pick, pick], axis=0))
        total = part if total is None else total + part
    return total


def fold_corners(odd, strips, corner_e, corner_o):
    quarter = corner_e.shape[0]
    half, part = LANES // 2, RAD * RAD
    lane = lane_ids((quarter, LANES))
    spare = jnp.zeros((4 * quarter - strips.shape[0], LANES), F32)
    whole = jnp.concatenate([strips, spare], axis=0)
    low = high = jnp.zeros((quarter, LANES), F32)
    for q in range(LANES // (2 * part)):
        piece = whole[q * quarter : (q + 1) * quarter]
        for side in range(2):
            to = q * 2 * part + side * part
            here = (lane >= to) & (lane < to + part)
            low = choose(here, pltpu.roll(piece, (to - side * half) % LANES, 1), low)
            high = choose(here, pltpu.roll(piece, (to - side * half - (half - part)) % LANES, 1), high)
    corner_e[...] = choose(odd, low, high)
    corner_o[...] = choose(odd, high, low)


def unfold_corners(value):
    part = 2 * RAD * RAD
    pieces = [value] + [pltpu.roll(value, LANES - q * part, 1) for q in range(1, LANES // part)]
    return jnp.concatenate(pieces, axis=0)


def is_odd(par_ref, axis):
    return par_ref[axis : axis + 1, :] == 1


def rows_kernel(par_ref, after, factor_ref, field_ref, out_ref, *, even):
    odd = is_odd(par_ref, 0)
    factor = factor_ref[0:1, :]
    rows = field_ref.shape[0]
    for row in range(RAD):
        first, last = field_ref[row], field_ref[rows - 1 - row]
        out_ref[row] = (choose(odd, first, last) if even else choose(odd, last, first)) * factor


def turn_kernel(after, control_ref, field_ref, last_ref, first_ref):
    rows = control_ref.shape[1]
    for row in range(rows):
        field_ref[row] = control_ref[:, row, :]
    write_strips(field_ref, last_ref, first_ref)


def strip_kernel(after, field_ref, last_ref, first_ref):
    write_strips(field_ref, last_ref, first_ref)


def write_strips(field_ref, last_ref, first_ref):
    strips = pack_strips(lambda r: field_ref[r], field_ref.shape[0])
    fold, half = last_ref.shape[0], LANES // 2
    early, late = strips[0:fold], strips[fold:]
    if late.shape[0] < fold:
        late = jnp.concatenate([late, jnp.zeros((fold - late.shape[0], LANES), F32)], axis=0)
    left = lane_ids(early.shape) < half
    last_ref[...] = jnp.where(left, early, pltpu.roll(late, half, 1))
    first_ref[...] = jnp.where(left, pltpu.roll(early, half, 1), late)


def halo_columns(par_ref, before_ref, after_ref):
    before, after = before_ref[...], after_ref[...]
    half = LANES // 2
    left = lane_ids(before.shape) < half
    early = jnp.where(left, before, pltpu.roll(after, half, 1))
    late = jnp.where(left, pltpu.roll(before, half, 1), after)
    outside = jnp.where(lane_ids((1, LANES)) < half, par_ref[3:4, :], par_ref[4:5, :])
    return jnp.where(outside == 1, 0.0, jnp.concatenate([early, late], axis=0))


def far_corner_kernel(par_ref, after, before_ref, after_ref, corner_e, corner_o):
    fold_corners(is_odd(par_ref, 0), halo_columns(par_ref, before_ref, after_ref), corner_e, corner_o)


def prepare_kernel(
    after, foot_ref, start_ref, row_ref, slot_ref, count_ref, observed_ref, error_ref, out_ref,
    blocks_ref, notes_ref, start_vmem, row_vmem, slot_vmem, count_vmem, observed_vmem, error_vmem, sems, *, per,
):
    owners, lines, _ = foot_ref.shape
    slots = start_ref.shape[0]
    pairs = (
        (start_ref, start_vmem), (row_ref, row_vmem), (slot_ref, slot_vmem), (count_ref, count_vmem),
        (observed_ref, observed_vmem), (error_ref, error_vmem),
    )
    small = [pltpu.make_async_copy(a, b, sems.at[i]) for i, (a, b) in enumerate(pairs)]
    chunk = owners // PARTS
    parts = [slice(i * chunk, (i + 1) * chunk) for i in range(PARTS)]
    loads = [
        pltpu.make_async_copy(foot_ref.at[here], blocks_ref.at[here], sems.at[6 + i])
        for i, here in enumerate(parts)
    ]
    for copy in small + loads:
        copy.start()
    stores = []
    for i, here in enumerate(parts):
        loads[i].wait()
        to = out_ref.at[here, 0:lines, :]
        stores.append(pltpu.make_async_copy(blocks_ref.at[here], to, sems.at[6 + PARTS + i]))
        stores[-1].start()
    for copy in small:
        copy.wait()
    start = start_vmem[...]
    valid = lax.broadcasted_iota(jnp.int32, start.shape, 0) < count_vmem[...]
    lanes = jnp.concatenate(
        [start >> 4, start & 15, row_vmem[...], jnp.where(valid, slot_vmem[...], per)], axis=0
    ).astype(F32)
    wide = jnp.pad(lanes, ((0, LANES - 4 * slots), (0, LANES - owners)))
    turned = jnp.transpose(wide)[0:owners]
    spare = [jnp.zeros((1, LANES - 2 * per), F32)] if 2 * per < LANES else []
    own = jnp.concatenate([observed_vmem[...], error_vmem[...]] + spare, axis=1)
    line = lax.broadcasted_iota(jnp.int32, notes_ref.shape, 1)
    value = jnp.broadcast_to(turned[:, None, :], notes_ref.shape)
    for k in range(3):
        term = own.astype(BF16).astype(F32)
        own = own - term
        value = jnp.where(line == 1 + k, term[None], value)
    notes_ref[...] = value.astype(BF16)
    stores.append(pltpu.make_async_copy(notes_ref, out_ref.at[:, lines : lines + SUB, :], sems.at[6 + 2 * PARTS]))
    stores[-1].start()
    for copy in stores:
        copy.wait()


def halo_parts(value):
    high, low = split(value)
    lanes = [high, low] + ([high] if value.shape[1] < LANES else [])
    return jnp.concatenate(lanes, axis=1)


def halo_sums(both, weights_ref, first, width):
    used = both.shape[1]
    out = dot(both, weights_ref[0:used, first : first + width])
    if used < weights_ref.shape[0]:
        out = out + dot(both[:, : used // 2], weights_ref[used:, first : first + width])
    return out


def column_sums(value, col_both):
    cols = value.shape[1]
    high, low = split(value)
    out = dot(jnp.concatenate([high, low], axis=1), col_both)
    return out[:, :cols] + out[:, cols:]


def time_sums(value, time_high, time_low):
    high, low = split(value)
    return dot(time_high, high) + dot(time_high, low) + dot(time_low, high)


def row_sums(get, row, low, high, taps):
    total = None
    for distance in range(RAD + 1):
        here = [get(r) for r in sorted({row - distance, row + distance}) if low <= r < high]
        if not here:
            continue
        part = here[0] if len(here) == 1 else here[0] + here[1]
        part = float(taps[RAD + distance]) * part
        total = part if total is None else total + part
    return total


def local_kernel(after, field_ref, time_high, time_low, col_both, out_ref):
    rows, hours, cols = field_ref.shape
    taps = space_taps()
    for row in range(0, rows, 2):
        pair = [
            column_sums(row_sums(lambda i: field_ref[i], r, 0, rows, taps), col_both[...])
            for r in (row, row + 1)
        ]
        both = time_sums(jnp.concatenate(pair, axis=1), time_high[...], time_low[...])
        for k, r in enumerate((row, row + 1)):
            out_ref[r] = both[:, k * cols : (k + 1) * cols]


def strip_halo(par_ref, before_ref, after_ref, time_high, time_low):
    halo = halo_columns(par_ref, before_ref, after_ref)[0 : time_high.shape[0]]
    return halo_parts(time_sums(halo, time_high[...], time_low[...]))


def strips_kernel(
    par_ref, local_ref, before_ref, after_ref, time_high, time_low, own_ref, out_ref, *, by_hour
):
    rows, hours, cols = local_ref.shape
    halo = strip_halo(par_ref, before_ref, after_ref, time_high, time_low)
    for row in range(0, rows, 2):
        both = halo_sums(halo, own_ref, row * cols, 2 * cols)
        for k, r in enumerate((row, row + 1)):
            value = local_ref[r] + both[:, k * cols : (k + 1) * cols]
            if by_hour:
                out_ref[:, r, :] = value
            else:
                out_ref[r] = value


def beyond_sums(rows, corner, corner_weights, consts):
    time_high, time_low, col_both = consts
    cols = col_both.shape[1] // 2
    taps = space_taps()
    parts = []
    for k in range(0, RAD, 2):
        pair = []
        for i in (k, k + 1):
            summed = None
            for j in range(RAD - i):
                part = float(taps[RAD + i + j + 1]) * rows(j)
                summed = part if summed is None else summed + part
            pair.append(column_sums(summed, col_both[...]))
        value = jnp.concatenate(pair, axis=1) + halo_sums(corner, corner_weights, k * cols, 2 * cols)
        both = time_sums(value, time_high[...], time_low[...])
        parts += [both[:, :cols], both[:, cols:]]
    return parts


def edge_parts(halo, corner, corner_weights, consts):
    corner = halo_parts(unfold_corners(corner)[0 : halo.shape[1], 0 : corner_weights.shape[0] // 3])
    return beyond_sums(lambda j: halo[j], corner, corner_weights, consts)


def beyond_kernel(
    par_ref, field_ref, before_ref, after_ref, time_high, time_low, col_both, beyond_ref, out_even, out_odd,
):
    rows, hours, _ = field_ref.shape
    odd = is_odd(par_ref, 0)
    halo = halo_parts(halo_columns(par_ref, before_ref, after_ref)[0:hours])
    consts = (time_high, time_low, col_both)
    to_after = beyond_sums(lambda j: field_ref[rows - 1 - j], halo, beyond_ref.at[0], consts)
    to_before = beyond_sums(lambda j: field_ref[j], halo, beyond_ref.at[1], consts)
    for k in range(RAD):
        out_even[k] = choose(odd, to_before[k], to_after[k]).astype(BF16)
        out_odd[k] = choose(odd, to_after[k], to_before[k]).astype(BF16)


def flux_kernel(par_ref, local_ref, prior_ref, scale_ref, got_ref, flux_ref, scale_out, wide):
    rows = local_ref.shape[0]
    odd = par_ref[0, 0]
    wide[...] = scale_ref[...].astype(F32)
    for row in range(rows):
        scale_out[row] = wide[:, row, :]
    wide[...] = prior_ref[...].astype(F32)
    for row in range(rows):
        flux_ref[row] = wide[:, row, :] + scale_out[row] * local_ref[row]
    for k in range(RAD):
        row = jnp.where(odd == 1, k, rows - 1 - k)
        flux_ref[row] = flux_ref[row] + scale_out[row] * got_ref[k].astype(F32)


def finish_kernel(
    par_ref, model_ref, local_ref, factor_ref, got_e, got_o, corner_e, corner_o,
    time_high, time_low, col_both, corner_weights,
    model_out, out_ref, halo, edges, total, model_own, sems,
):
    hours, rows, cols = local_ref.shape
    half = rows // 2
    odd = is_odd(par_ref, 0)
    factor = factor_ref[1:2, :]
    consts = (time_high, time_low, col_both)
    model_own[...] = model_ref[:, 0 : model_own.shape[1]]
    copies = [pltpu.make_async_copy(model_own, model_out, sems.at[2])]
    copies[0].start()
    inside = lax.broadcasted_iota(jnp.int32, (hours, half, cols), 1)
    for side in range(2):
        before = side == 0
        for k in range(RAD):
            even, other = got_e[k], got_o[k]
            halo[k] = (choose(odd, even, other) if before else choose(odd, other, even)) * factor
        even, other = corner_e[...], corner_o[...]
        corner = choose(odd, even, other) if before else choose(odd, other, even)
        parts = edge_parts(halo, corner, corner_weights.at[1 - side], consts)
        for k, part in enumerate(parts):
            edges[:, k if before else half - 1 - k, :] = part
        here = slice(0, half) if before else slice(rows - half, rows)
        mine = inside < RAD if before else inside >= half - RAD
        total[:, here, :] = local_ref[:, here, :] + jnp.where(mine, edges[...], 0.0)
        copies.append(pltpu.make_async_copy(total.at[:, here, :], out_ref.at[:, here, :], sems.at[side]))
        copies[-1].start()
    for copy in copies:
        copy.wait()


def blocks_of(foot_ref, source, heights, slots):
    for c in range(0, slots, 2):
        both = foot_ref[source, c * heights : (c + 2) * heights, :].astype(F32)
        yield c, both[0:heights]
        yield c + 1, both[heights : 2 * heights]


def load_kernel(
    par_ref, foot_ref, scale_far, *refs, shift, slots, heights, tiles, per, empty
):
    count = (len(refs) - 4) // 2
    distant, near = refs[:count], refs[count + 3 : -1]
    table_ref, seen_ref, scale_ref = refs[count : count + 3]
    sems = refs[-1]
    flux_far, flux_ref = distant[0], near[0]
    rows = flux_ref.shape[0]
    first = (rows - RAD) * par_ref[0, 0]
    pairs = [(flux_far.at[r : r + RAD], flux_ref.at[r : r + RAD]) for r in range(0, rows, RAD)]
    pairs += list(zip(distant[1:], near[1:])) + [(scale_far.at[pl.ds(first, RAD)], scale_ref)]
    loads = [pltpu.make_async_copy(a, b, sems.at[i]) for i, (a, b) in enumerate(pairs)]
    for load in loads:
        load.start()
    sources = foot_ref.shape[0]
    base = slots * heights
    lane = lane_ids((sources, LANES))
    lines = foot_ref[:, base : base + SUB, :].astype(F32)
    notes = lines[:, 0, :].astype(jnp.int32)
    seen_ref[...] = lines[:, 1, :] + lines[:, 2, :] + lines[:, 3, :]
    start = notes * 16 + pltpu.roll(notes, LANES - slots, 1)
    offset = start + pltpu.roll(notes, LANES - 2 * slots, 1) * (1 << shift)
    source_rec = lax.broadcasted_iota(jnp.int32, (sources, LANES), 0) // tiles
    receptor = jnp.where(notes < per, source_rec * per + notes, empty)
    table_ref[...] = jnp.where(lane < slots, offset, receptor)
    for load in loads:
        load.wait()


def forward_kernel(
    par_ref, foot_ref, table_ref, got_far, flux_in, scale_ref,
    out_ref, flux_ref, got_ref, sums, table_smem, sems, *, shift, slots, heights, tiles, per,
):
    load = pltpu.make_async_copy(got_far, got_ref, sems.at[1])
    load.start()
    odd = par_ref[0, 0]
    sources = foot_ref.shape[0]
    rows = flux_ref.shape[0]
    first = (rows - RAD) * odd
    groups = out_ref.shape[1]
    lane = lane_ids((sources, LANES))
    table = table_ref[...]
    copy = pltpu.make_async_copy(table_ref, table_smem, sems.at[0])
    copy.start()
    load.wait()
    for k in range(RAD):
        line = jnp.where(odd == 1, RAD - 1 - k, k)
        flux_ref[first + line] = flux_in[first + line] + scale_ref[line] * got_ref[k].astype(F32)
    copy.wait()

    def body(source, carry):
        for c, block in blocks_of(foot_ref, source, heights, slots):
            offset = table_smem[source, c]
            row = lax.shift_right_logical(offset, shift)
            begin = jnp.bitwise_and(offset, (1 << shift) - 1)
            product = flux_ref[row, pl.ds(begin, heights), :] * block
            sums[c, pl.ds(source, 1), :] = jnp.sum(product, axis=0, keepdims=True)
        return carry

    lax.fori_loop(0, sources, body, 0)
    totals = [jnp.zeros((sources, LANES), F32) for _ in range(groups)]
    for c in range(slots):
        value = jnp.sum(sums[c], axis=1, keepdims=True)
        which = table[:, 3 * slots + c : 3 * slots + c + 1]
        for q in range(groups):
            totals[q] = totals[q] + jnp.where(which == lane + q * LANES, value, 0.0)
    for q in range(groups):
        total = jnp.sum(totals[q], axis=0, keepdims=True)
        out_ref[:, q : q + 1, :] = jnp.broadcast_to(total[None], (sources, 1, LANES))


def adjoint_kernel(
    par_ref, table_vmem, seen_ref, got_ref, foot_ref, scale_ref,
    model_ref, factor_ref, field_ref,
    weight_vmem, weight_smem, table_ref, sems, *, shift, slots, heights, tiles, per,
):
    load = pltpu.make_async_copy(table_vmem, table_ref, sems.at[1])
    load.start()
    sources = foot_ref.shape[0]
    groups = got_ref.shape[1]
    rows, hours, _ = field_ref.shape
    model = jnp.sum(got_ref[:, 0:groups, :], axis=0)
    packed = LANES // per
    lane = lane_ids((1, LANES))
    own = jnp.zeros((1, LANES), F32)
    for q in range(groups):
        for k in range(packed):
            line = model[q : q + 1, :]
            line = line if k == 0 else pltpu.roll(line, LANES - k * per, 1)
            own = choose(par_ref[2:3, :] == q * packed + k, line, own)
    model_ref[...] = own
    weight_vmem[...] = jnp.zeros_like(weight_vmem)
    for q in range(groups):
        observed, error = jnp.zeros((1, LANES), F32), jnp.ones((1, LANES), F32)
        for k in range(packed):
            source = (q * packed + k) * tiles
            line = seen_ref[source : source + 1, :]
            here = (lane >= k * per) & (lane < (k + 1) * per)
            observed = jnp.where(here, line if k == 0 else pltpu.roll(line, k * per, 1), observed)
            turn = (k * per - per) % LANES
            error = jnp.where(here, line if turn == 0 else pltpu.roll(line, turn, 1), error)
        weight_vmem[q : q + 1, :] = (model[q : q + 1, :] - observed) / (error * error)
    copy = pltpu.make_async_copy(weight_vmem, weight_smem, sems.at[0])
    copy.start()
    field_ref[...] = jnp.zeros_like(field_ref)
    top = jnp.max(jnp.abs(weight_vmem[...]), keepdims=True) * (FOOT_MAX * SCALE_MAX * sources * slots)
    top = jnp.maximum(top, 1e-25)
    factor_ref[0:1, :] = jnp.broadcast_to(HALF_TOP / top, (1, LANES))
    factor_ref[1:2, :] = jnp.broadcast_to(top * (1.0 / HALF_TOP), (1, LANES))
    load.wait()
    copy.wait()

    def body(source, carry):
        for c, block in blocks_of(foot_ref, source, heights, slots):
            offset = table_ref[source, c]
            receptor = table_ref[source, 3 * slots + c]
            row = lax.shift_right_logical(offset, shift)
            begin = jnp.bitwise_and(offset, (1 << shift) - 1)
            weight = weight_smem[lax.shift_right_logical(receptor, 7), jnp.bitwise_and(receptor, LANES - 1)]
            field_ref[row, pl.ds(begin, heights), :] += block * weight
        return carry

    lax.fori_loop(0, sources, body, 0)
    for row in range(rows):
        field_ref[row] = field_ref[row] * scale_ref[row]


def swap_pairs(count, odd):
    pairs = []
    for i in range(1 if odd else 0, count - 1, 2):
        pairs += [(i, i + 1), (i + 1, i)]
    return pairs


def swap(axis, even, odd):
    count = lax.axis_size(axis)
    return (
        lax.ppermute(even, axis, swap_pairs(count, False)),
        lax.ppermute(odd, axis, swap_pairs(count, True)),
    )


VM = pl.BlockSpec(memory_space=pltpu.VMEM)
HB = pl.BlockSpec(memory_space=pltpu.HBM)


def call(kernel, out_shape, in_specs, scratch, name, out_specs=None, alias=None):
    return pl.pallas_call(
        kernel,
        out_shape=out_shape,
        in_specs=in_specs,
        out_specs=jax.tree.map(lambda _: VM, out_shape) if out_specs is None else out_specs,
        scratch_shapes=scratch,
        input_output_aliases={} if alias is None else alias,
        compiler_params=pltpu.CompilerParams(vmem_limit_bytes=VMEM_LIMIT),
        name=name,
    )


def far(x):
    return pltpu.with_memory_space_constraint(x, pltpu.HBM)


def array(*shape):
    return jax.ShapeDtypeStruct(shape, F32)


def per_device(
    prior_flux,
    flux_scale,
    control,
    footprint,
    slot_count,
    start_hour,
    grid_row,
    receptor_slot,
    observed,
    obs_error,
):
    hours, rows, cols = control.shape
    n_rec, n_tile = lax.axis_size("rec"), lax.axis_size("tile")
    devices = n_rec * n_tile
    slots, heights = footprint.shape[1], footprint.shape[2]
    per = observed.shape[0]
    groups = per * n_rec // LANES
    shift = (hours - 1).bit_length()
    rec, tile = lax.axis_index("rec"), lax.axis_index("tile")
    flags = [rec % 2, rec * 0, rec, tile == 0, tile == n_tile - 1] + [rec * 0] * (SUB - 5)
    par = jnp.stack([flag.astype(jnp.int32) for flag in flags])
    par = jnp.broadcast_to(par[:, None], (SUB, LANES))
    base, own_parts, corner_parts, beyond_parts = constants(hours, rows, cols)
    base = [jnp.asarray(c) for c in base]
    own_parts = jnp.asarray(own_parts)
    corner_parts = jnp.asarray(corner_parts)
    beyond_parts = jnp.asarray(beyond_parts)
    strip = array(-(-hours // (2 * SUB)) * SUB, LANES)
    corner = array(-(-hours // (4 * SUB)) * SUB, LANES)
    block = array(RAD, hours, cols)
    field_shape = array(rows, hours, cols)
    row_scratch = pltpu.VMEM((RAD, hours, cols), F32)

    def pass_strips(last, first):
        onward = [(i, (i + 1) % n_tile) for i in range(n_tile)]
        back = [(j, i) for i, j in onward]
        return lax.ppermute(last, "tile", onward), lax.ppermute(first, "tile", back)

    def swaps(after, field, got_strips, name):
        local = call(local_kernel, field_shape, [VM] * 5, [], name + "_local")(after, field, *base)
        corners = call(far_corner_kernel, [corner, corner], [VM] * 4, [], name + "_corners")(par, local, *got_strips)
        return local, swap("rec", *corners)

    def strip_sums(local, got_strips, by_hour, name):
        def kernel(*refs):
            strips_kernel(*refs, by_hour=by_hour)

        shape = array(hours, rows, cols) if by_hour else field_shape
        return call(kernel, shape, [VM] * 7, [], name)(par, local, *got_strips, *base[:2], own_parts)

    def swap_rows(even, after, factor, field, name):
        def kernel(*refs):
            rows_kernel(*refs, even=even)

        sent = call(kernel, block, [VM] * 4, [], name)(par, after, factor, field)
        return sent, lax.ppermute(sent.astype(F16), "rec", swap_pairs(n_rec, not even))

    def prepare(*refs):
        prepare_kernel(*refs, per=per)

    numbers = pltpu.VMEM((slots, devices), jnp.int32)
    lines = slots * heights + SUB
    sent = call(
        prepare,
        jax.ShapeDtypeStruct((devices, lines, cols), BF16),
        [VM] + [HB] * 7,
        [
            pltpu.VMEM((devices, slots * heights, cols), BF16),
            pltpu.VMEM((devices, SUB, LANES), BF16),
            numbers, numbers, numbers, pltpu.VMEM((1, devices), jnp.int32),
            pltpu.VMEM((1, per), F32), pltpu.VMEM((1, per), F32),
            pltpu.SemaphoreType.DMA((7 + 2 * PARTS,)),
        ],
        "prepare_blocks",
        out_specs=HB,
    )(par, *[
        far(x)
        for x in (
            footprint.reshape(devices, slots * heights, cols),
            start_hour.T, grid_row.T, receptor_slot.T, slot_count[None], observed[None], obs_error[None],
        )
    ])
    foot = lax.all_to_all(sent, AXES, split_axis=0, concat_axis=0, tiled=True)
    field, *strips = call(
        turn_kernel, [field_shape, strip, strip], [HB, VM], [], "turn_control"
    )(sent, control)
    got_strips = pass_strips(*strips)
    local = call(local_kernel, field_shape, [VM] * 5, [], "control_local")(strips[0], field, *base)
    small = jax.ShapeDtypeStruct((RAD, hours, cols), BF16)
    sent_even, sent_odd = call(beyond_kernel, [small, small], [VM] * 8, [], "control_beyond")(
        par, field, *got_strips, *base, beyond_parts
    )
    got_even, got_odd = swap("rec", sent_even, sent_odd)
    local = strip_sums(local, got_strips, False, "control_strips")
    flux, scale = call(
        flux_kernel, [field_shape, field_shape], [VM] * 5, [pltpu.VMEM((hours, rows, cols), F32)], "flux_field"
    )(par, local, prior_flux, flux_scale, got_even)

    sizes = dict(shift=shift, slots=slots, heights=heights, tiles=n_tile, per=per)

    def forward(*refs):
        forward_kernel(*refs, **sizes)


    def load(*refs):
        load_kernel(*refs, empty=groups * LANES, **sizes)

    table, seen, scale_near, flux_near = call(
        load,
        [jax.ShapeDtypeStruct((devices, LANES), jnp.int32), array(devices, LANES), block, field_shape],
        [VM, VM, HB, HB],
        [pltpu.SemaphoreType.DMA((1 + rows // RAD,))],
        "load_flux",
    )(par, foot, far(scale), far(flux))
    table, got_odd = lax.optimization_barrier((table, got_odd))
    partial, _ = call(
        forward,
        [array(devices, groups, LANES), field_shape],
        [VM] * 3 + [HB] + [VM] * 2,
        [
            pltpu.VMEM((RAD, hours, cols), BF16),
            pltpu.VMEM((slots, devices, LANES), F32),
            pltpu.SMEM((devices, LANES), jnp.int32),
            pltpu.SemaphoreType.DMA((2,)),
        ],
        "block_values",
        alias={4: 1},
    )(par, foot, table, far(got_odd), flux_near, scale_near)
    everyone = lax.all_to_all(partial, AXES, split_axis=0, concat_axis=0, tiled=True)

    def adjoint(*refs):
        adjoint_kernel(*refs, **sizes)

    weight_rows = -(-(groups + 1) // SUB) * SUB
    model, factor, field = call(
        adjoint,
        [array(1, LANES), array(2, LANES), field_shape],
        [VM] * 6,
        [
            pltpu.VMEM((weight_rows, LANES), F32),
            pltpu.SMEM((weight_rows, LANES), F32),
            pltpu.SMEM((devices, LANES), jnp.int32),
            pltpu.SemaphoreType.DMA((2,)),
        ],
        "adjoint_field",
    )(par, table, seen, everyone, foot, scale)
    sent_even, got_even = swap_rows(True, factor, factor, field, "gradient_even")
    strips = call(strip_kernel, [strip, strip], [VM] * 2, [], "gradient_pack")(sent_even, field)
    got_strips = pass_strips(*strips)
    sent_odd, got_odd = swap_rows(False, strips[0], factor, field, "gradient_odd")
    local, got_corners = swaps(sent_odd, field, got_strips, "gradient")
    local = strip_sums(local, got_strips, True, "gradient_strips")
    model_co2, gradient = call(
        finish_kernel,
        [array(1, per), array(hours, rows, cols)],
        [VM] * 12,
        [
            row_scratch,
            pltpu.VMEM((hours, rows // 2, cols), F32),
            pltpu.VMEM((hours, rows, cols), F32),
            pltpu.VMEM((1, per), F32),
            pltpu.SemaphoreType.DMA((3,)),
        ],
        "gradient",
        out_specs=[HB, HB],
    )(par, model, local, factor, got_even.astype(F32), got_odd.astype(F32), *got_corners, *base, corner_parts)
    return (model_co2.reshape(-1), gradient)


def solution(mesh):
    return jax.shard_map(
        per_device,
        mesh=mesh,
        in_specs=(
            P(None, "rec", "tile"),
            P(None, "rec", "tile"),
            P(None, "rec", "tile"),
            P(("rec", "tile"), None, None, None),
            P(("rec", "tile")),
            P(("rec", "tile"), None),
            P(("rec", "tile"), None),
            P(("rec", "tile"), None),
            P("rec"),
            P("rec"),
        ),
        out_specs=(P("rec"), P(None, "rec", "tile")),
        check_vma=False,
    )
```

```python
import numpy as np
import jax
import jax.numpy as jnp
from jax import lax
from jax.experimental import pallas as pl
from jax.experimental.pallas import tpu as pltpu
from jax.sharding import PartitionSpec as P

RAD = 4
TAPS = 12
AXES = ("rec", "tile")
LANES = 128
SUB = 8
FOOT_MAX = 0.02
PARTS = 4
SCALE_MAX = 2.0
HALF_TOP = 32768.0
F16 = jnp.float16
VMEM_LIMIT = 14 * 1024 * 1024
F32 = jnp.float32
BF16 = jnp.bfloat16


def space_taps():
    offsets = np.arange(-RAD, RAD + 1).astype(np.float64)
    values = np.exp(-2.0 * offsets * offsets / (RAD * RAD))
    return values / np.sqrt(np.sum(values * values))


def time_taps():
    offsets = np.arange(-TAPS, TAPS + 1).astype(np.float64)
    values = np.exp(-2.0 * np.abs(offsets) / TAPS)
    return values / np.sqrt(np.sum(values * values))


def banded(distance, taps, reach):
    inside = np.abs(distance) <= reach
    return np.where(inside, taps[np.clip(distance, -reach, reach) + reach], 0.0)


def two_parts(matrix):
    high = matrix.astype(np.float32).astype(jnp.bfloat16)
    low = (matrix - high.astype(np.float64)).astype(np.float32).astype(jnp.bfloat16)
    return high, low


def constants(hours, rows, cols):
    space = space_taps()
    hour = np.arange(hours)
    time_high, time_low = two_parts(banded(hour[:, None] - hour[None, :], time_taps(), TAPS))
    col = np.arange(cols)
    col_high, col_low = two_parts(banded(col[:, None] - col[None, :], space, RAD))
    col_both = np.block([[col_high, col_low], [col_high, np.zeros_like(col_high)]])
    halo_col = np.concatenate([np.arange(-RAD, 0), np.arange(cols, cols + RAD)])
    edge = banded(halo_col[:, None] - col[None, :], space, RAD)

    def strips(row_of, halo_of, targets):
        by_row = banded(np.array(row_of)[:, None] - np.array(targets)[None, :], space, RAD)
        both = by_row[:, :, None] * edge[np.array(halo_of)][:, None, :]
        high, low = two_parts(both.reshape(len(row_of), -1))
        return np.concatenate([high, high, low], axis=0)

    own = [(row, side * RAD + j) for side in range(2) for row in range(rows) for j in range(RAD)]
    corner = []
    for first, targets in ((rows, rows - 1 - np.arange(RAD)), (-RAD, np.arange(RAD))):
        lanes = [
            (row, side * RAD + j) for side in range(2) for row in range(first, first + RAD) for j in range(RAD)
        ]
        corner.append(strips(*zip(*lanes), targets))
    beyond = [strips(*zip(*own), rows + np.arange(RAD)), strips(*zip(*own), -1 - np.arange(RAD))]
    return (
        (time_high, time_low, col_both),
        strips(*zip(*own), np.arange(rows)),
        np.stack(corner),
        np.stack(beyond),
    )


def split(value):
    high = value.astype(BF16)
    low = (value - high.astype(F32)).astype(BF16)
    return high, low


def dot(a, b):
    return jnp.dot(a, b, preferred_element_type=F32)


def lane_ids(shape):
    return lax.broadcasted_iota(jnp.int32, shape, 1)


def choose(flag, yes, no):
    return jnp.where(flag, yes, no)


def pack_strips(row_value, rows):
    cols = row_value(0).shape[1]
    half = rows * RAD
    source = lax.broadcasted_iota(jnp.int32, (cols, 2 * half), 0)
    lane = lane_ids((cols, 2 * half))
    first = lane < half
    j = lane & (RAD - 1)
    wanted = jnp.where(first, cols - RAD + j, j)
    lane_row = jnp.where(first, lane, lane - half) // RAD
    total = None
    for row in range(rows):
        high, low = split(row_value(row))
        pick = jnp.where((source == wanted) & (lane_row == row), 1.0, 0.0).astype(BF16)
        part = dot(jnp.concatenate([high, low], axis=1), jnp.concatenate([pick, pick], axis=0))
        total = part if total is None else total + part
    return total


def fold_corners(odd, strips, corner_e, corner_o):
    quarter = corner_e.shape[0]
    half, part = LANES // 2, RAD * RAD
    lane = lane_ids((quarter, LANES))
    spare = jnp.zeros((4 * quarter - strips.shape[0], LANES), F32)
    whole = jnp.concatenate([strips, spare], axis=0)
    low = high = jnp.zeros((quarter, LANES), F32)
    for q in range(LANES // (2 * part)):
        piece = whole[q * quarter : (q + 1) * quarter]
        for side in range(2):
            to = q * 2 * part + side * part
            here = (lane >= to) & (lane < to + part)
            low = choose(here, pltpu.roll(piece, (to - side * half) % LANES, 1), low)
            high = choose(here, pltpu.roll(piece, (to - side * half - (half - part)) % LANES, 1), high)
    corner_e[...] = choose(odd, low, high)
    corner_o[...] = choose(odd, high, low)


def unfold_corners(value):
    part = 2 * RAD * RAD
    pieces = [value] + [pltpu.roll(value, LANES - q * part, 1) for q in range(1, LANES // part)]
    return jnp.concatenate(pieces, axis=0)


def is_odd(par_ref, axis):
    return par_ref[axis : axis + 1, :] == 1


def rows_kernel(par_ref, after, factor_ref, field_ref, out_ref, *, even):
    odd = is_odd(par_ref, 0)
    factor = factor_ref[0:1, :]
    rows = field_ref.shape[0]
    for row in range(RAD):
        first, last = field_ref[row], field_ref[rows - 1 - row]
        out_ref[row] = (choose(odd, first, last) if even else choose(odd, last, first)) * factor


def turn_kernel(after, control_ref, field_ref, last_ref, first_ref):
    rows = control_ref.shape[1]
    for row in range(rows):
        field_ref[row] = control_ref[:, row, :]
    write_strips(field_ref, last_ref, first_ref)


def strip_kernel(after, field_ref, last_ref, first_ref):
    write_strips(field_ref, last_ref, first_ref)


def write_strips(field_ref, last_ref, first_ref):
    strips = pack_strips(lambda r: field_ref[r], field_ref.shape[0])
    fold, half = last_ref.shape[0], LANES // 2
    early, late = strips[0:fold], strips[fold:]
    if late.shape[0] < fold:
        late = jnp.concatenate([late, jnp.zeros((fold - late.shape[0], LANES), F32)], axis=0)
    left = lane_ids(early.shape) < half
    last_ref[...] = jnp.where(left, early, pltpu.roll(late, half, 1))
    first_ref[...] = jnp.where(left, pltpu.roll(early, half, 1), late)


def halo_columns(par_ref, before_ref, after_ref):
    before, after = before_ref[...], after_ref[...]
    half = LANES // 2
    left = lane_ids(before.shape) < half
    early = jnp.where(left, before, pltpu.roll(after, half, 1))
    late = jnp.where(left, pltpu.roll(before, half, 1), after)
    outside = jnp.where(lane_ids((1, LANES)) < half, par_ref[3:4, :], par_ref[4:5, :])
    return jnp.where(outside == 1, 0.0, jnp.concatenate([early, late], axis=0))


def far_corner_kernel(par_ref, after, before_ref, after_ref, corner_e, corner_o):
    fold_corners(is_odd(par_ref, 0), halo_columns(par_ref, before_ref, after_ref), corner_e, corner_o)


def prepare_kernel(
    after, foot_ref, start_ref, row_ref, slot_ref, count_ref, observed_ref, error_ref, out_ref,
    blocks_ref, notes_ref, start_vmem, row_vmem, slot_vmem, count_vmem, observed_vmem, error_vmem, sems, *, per,
):
    owners, lines, _ = foot_ref.shape
    slots = start_ref.shape[0]
    pairs = (
        (start_ref, start_vmem), (row_ref, row_vmem), (slot_ref, slot_vmem), (count_ref, count_vmem),
        (observed_ref, observed_vmem), (error_ref, error_vmem),
    )
    small = [pltpu.make_async_copy(a, b, sems.at[i]) for i, (a, b) in enumerate(pairs)]
    chunk = owners // PARTS
    parts = [slice(i * chunk, (i + 1) * chunk) for i in range(PARTS)]
    loads = [
        pltpu.make_async_copy(foot_ref.at[here], blocks_ref.at[here], sems.at[6 + i])
        for i, here in enumerate(parts)
    ]
    for copy in small + loads:
        copy.start()
    stores = []
    for i, here in enumerate(parts):
        loads[i].wait()
        to = out_ref.at[here, 0:lines, :]
        stores.append(pltpu.make_async_copy(blocks_ref.at[here], to, sems.at[6 + PARTS + i]))
        stores[-1].start()
    for copy in small:
        copy.wait()
    start = start_vmem[...]
    valid = lax.broadcasted_iota(jnp.int32, start.shape, 0) < count_vmem[...]
    lanes = jnp.concatenate(
        [start >> 4, start & 15, row_vmem[...], jnp.where(valid, slot_vmem[...], per)], axis=0
    ).astype(F32)
    wide = jnp.pad(lanes, ((0, LANES - 4 * slots), (0, LANES - owners)))
    turned = jnp.transpose(wide)[0:owners]
    spare = [jnp.zeros((1, LANES - 2 * per), F32)] if 2 * per < LANES else []
    own = jnp.concatenate([observed_vmem[...], error_vmem[...]] + spare, axis=1)
    line = lax.broadcasted_iota(jnp.int32, notes_ref.shape, 1)
    value = jnp.broadcast_to(turned[:, None, :], notes_ref.shape)
    for k in range(3):
        term = own.astype(BF16).astype(F32)
        own = own - term
        value = jnp.where(line == 1 + k, term[None], value)
    notes_ref[...] = value.astype(BF16)
    stores.append(pltpu.make_async_copy(notes_ref, out_ref.at[:, lines : lines + SUB, :], sems.at[6 + 2 * PARTS]))
    stores[-1].start()
    for copy in stores:
        copy.wait()


def halo_parts(value):
    high, low = split(value)
    lanes = [high, low] + ([high] if value.shape[1] < LANES else [])
    return jnp.concatenate(lanes, axis=1)


def halo_sums(both, weights_ref, first, width):
    used = both.shape[1]
    out = dot(both, weights_ref[0:used, first : first + width])
    if used < weights_ref.shape[0]:
        out = out + dot(both[:, : used // 2], weights_ref[used:, first : first + width])
    return out


def column_sums(value, col_both):
    cols = value.shape[1]
    high, low = split(value)
    out = dot(jnp.concatenate([high, low], axis=1), col_both)
    return out[:, :cols] + out[:, cols:]


def time_sums(value, time_high, time_low):
    high, low = split(value)
    return dot(time_high, high) + dot(time_high, low) + dot(time_low, high)


def row_sums(get, row, low, high, taps):
    total = None
    for distance in range(RAD + 1):
        here = [get(r) for r in sorted({row - distance, row + distance}) if low <= r < high]
        if not here:
            continue
        part = here[0] if len(here) == 1 else here[0] + here[1]
        part = float(taps[RAD + distance]) * part
        total = part if total is None else total + part
    return total


def local_kernel(after, field_ref, time_high, time_low, col_both, out_ref):
    rows, hours, cols = field_ref.shape
    taps = space_taps()
    for row in range(0, rows, 2):
        pair = [
            column_sums(row_sums(lambda i: field_ref[i], r, 0, rows, taps), col_both[...])
            for r in (row, row + 1)
        ]
        both = time_sums(jnp.concatenate(pair, axis=1), time_high[...], time_low[...])
        for k, r in enumerate((row, row + 1)):
            out_ref[r] = both[:, k * cols : (k + 1) * cols]


def strip_halo(par_ref, before_ref, after_ref, time_high, time_low):
    halo = halo_columns(par_ref, before_ref, after_ref)[0 : time_high.shape[0]]
    return halo_parts(time_sums(halo, time_high[...], time_low[...]))


def strips_kernel(
    par_ref, local_ref, before_ref, after_ref, time_high, time_low, own_ref, out_ref, *, by_hour
):
    rows, hours, cols = local_ref.shape
    halo = strip_halo(par_ref, before_ref, after_ref, time_high, time_low)
    for row in range(0, rows, 2):
        both = halo_sums(halo, own_ref, row * cols, 2 * cols)
        for k, r in enumerate((row, row + 1)):
            value = local_ref[r] + both[:, k * cols : (k + 1) * cols]
            if by_hour:
                out_ref[:, r, :] = value
            else:
                out_ref[r] = value


def beyond_sums(rows, corner, corner_weights, consts):
    time_high, time_low, col_both = consts
    cols = col_both.shape[1] // 2
    taps = space_taps()
    parts = []
    for k in range(0, RAD, 2):
        pair = []
        for i in (k, k + 1):
            summed = None
            for j in range(RAD - i):
                part = float(taps[RAD + i + j + 1]) * rows(j)
                summed = part if summed is None else summed + part
            pair.append(column_sums(summed, col_both[...]))
        value = jnp.concatenate(pair, axis=1) + halo_sums(corner, corner_weights, k * cols, 2 * cols)
        both = time_sums(value, time_high[...], time_low[...])
        parts += [both[:, :cols], both[:, cols:]]
    return parts


def edge_parts(halo, corner, corner_weights, consts):
    corner = halo_parts(unfold_corners(corner)[0 : halo.shape[1], 0 : corner_weights.shape[0] // 3])
    return beyond_sums(lambda j: halo[j], corner, corner_weights, consts)


def beyond_kernel(
    par_ref, field_ref, before_ref, after_ref, time_high, time_low, col_both, beyond_ref, out_even, out_odd,
):
    rows, hours, _ = field_ref.shape
    odd = is_odd(par_ref, 0)
    halo = halo_parts(halo_columns(par_ref, before_ref, after_ref)[0:hours])
    consts = (time_high, time_low, col_both)
    to_after = beyond_sums(lambda j: field_ref[rows - 1 - j], halo, beyond_ref.at[0], consts)
    to_before = beyond_sums(lambda j: field_ref[j], halo, beyond_ref.at[1], consts)
    for k in range(RAD):
        out_even[k] = choose(odd, to_before[k], to_after[k]).astype(BF16)
        out_odd[k] = choose(odd, to_after[k], to_before[k]).astype(BF16)


def flux_kernel(par_ref, local_ref, prior_ref, scale_ref, got_ref, flux_ref, scale_out, wide):
    rows = local_ref.shape[0]
    odd = par_ref[0, 0]
    wide[...] = scale_ref[...].astype(F32)
    for row in range(rows):
        scale_out[row] = wide[:, row, :]
    wide[...] = prior_ref[...].astype(F32)
    for row in range(rows):
        flux_ref[row] = wide[:, row, :] + scale_out[row] * local_ref[row]
    for k in range(RAD):
        row = jnp.where(odd == 1, k, rows - 1 - k)
        flux_ref[row] = flux_ref[row] + scale_out[row] * got_ref[k].astype(F32)


def even_kernel(
    par_ref, local_ref, factor_ref, got_ref, corner_ref, time_high, time_low, col_both, corner_weights,
    out_ref, halo,
):
    rows, hours, cols = local_ref.shape
    odd = par_ref[0, 0]
    for row in range(RAD, rows - RAD):
        out_ref[:, row, :] = local_ref[row]
    halo[...] = got_ref[...] * factor_ref[1:2, :]
    consts = (time_high, time_low, col_both)
    parts = edge_parts(halo, corner_ref[...], corner_weights.at[odd], consts)
    at_first = jnp.where(is_odd(par_ref, 0), 1.0, 0.0)
    for k, part in enumerate(parts):
        out_ref[:, k, :] = local_ref[k] + part * at_first
        out_ref[:, rows - 1 - k, :] = local_ref[rows - 1 - k] + part * (1.0 - at_first)


def finish_kernel(
    par_ref, model_ref, local_ref, factor_ref, got_ref, corner_ref,
    time_high, time_low, col_both, corner_weights,
    model_out, out_ref, halo, edges, total, model_own, sems,
):
    hours, rows, cols = local_ref.shape
    half = rows // 2
    odd = par_ref[0, 0]
    mine = pl.multiple_of(odd * half, half)
    rest = pl.multiple_of(half - mine, half)
    model_own[...] = model_ref[:, 0 : model_own.shape[1]]
    copies = [
        pltpu.make_async_copy(model_own, model_out, sems.at[0]),
        pltpu.make_async_copy(
            local_ref.at[:, pl.ds(rest, half), :], out_ref.at[:, pl.ds(rest, half), :], sems.at[1]
        ),
    ]
    for copy in copies:
        copy.start()
    halo[...] = got_ref[...] * factor_ref[1:2, :]
    consts = (time_high, time_low, col_both)
    parts = edge_parts(halo, corner_ref[...], corner_weights.at[1 - odd], consts)
    for k, part in enumerate(parts):
        edges[:, jnp.where(odd == 1, half - 1 - k, k), :] = part
    inside = lax.broadcasted_iota(jnp.int32, edges.shape, 1) // RAD
    total[...] = local_ref[:, pl.ds(mine, half), :] + jnp.where(inside == odd, edges[...], 0.0)
    copies.append(pltpu.make_async_copy(total, out_ref.at[:, pl.ds(mine, half), :], sems.at[2]))
    copies[-1].start()
    for copy in copies:
        copy.wait()


def blocks_of(foot_ref, source, heights, slots):
    for c in range(0, slots, 2):
        both = foot_ref[source, c * heights : (c + 2) * heights, :].astype(F32)
        yield c, both[0:heights]
        yield c + 1, both[heights : 2 * heights]


def load_kernel(
    par_ref, foot_ref, scale_far, *refs, shift, slots, heights, tiles, per, empty
):
    count = (len(refs) - 4) // 2
    distant, near = refs[:count], refs[count + 3 : -1]
    table_ref, seen_ref, scale_ref = refs[count : count + 3]
    sems = refs[-1]
    flux_far, flux_ref = distant[0], near[0]
    rows = flux_ref.shape[0]
    first = (rows - RAD) * par_ref[0, 0]
    pairs = [(flux_far.at[r : r + RAD], flux_ref.at[r : r + RAD]) for r in range(0, rows, RAD)]
    pairs += list(zip(distant[1:], near[1:])) + [(scale_far.at[pl.ds(first, RAD)], scale_ref)]
    loads = [pltpu.make_async_copy(a, b, sems.at[i]) for i, (a, b) in enumerate(pairs)]
    for load in loads:
        load.start()
    sources = foot_ref.shape[0]
    base = slots * heights
    lane = lane_ids((sources, LANES))
    lines = foot_ref[:, base : base + SUB, :].astype(F32)
    notes = lines[:, 0, :].astype(jnp.int32)
    seen_ref[...] = lines[:, 1, :] + lines[:, 2, :] + lines[:, 3, :]
    start = notes * 16 + pltpu.roll(notes, LANES - slots, 1)
    offset = start + pltpu.roll(notes, LANES - 2 * slots, 1) * (1 << shift)
    source_rec = lax.broadcasted_iota(jnp.int32, (sources, LANES), 0) // tiles
    receptor = jnp.where(notes < per, source_rec * per + notes, empty)
    table_ref[...] = jnp.where(lane < slots, offset, receptor)
    for load in loads:
        load.wait()


def forward_kernel(
    par_ref, foot_ref, table_ref, got_far, flux_in, scale_ref,
    out_ref, flux_ref, got_ref, sums, table_smem, sems, *, shift, slots, heights, tiles, per,
):
    load = pltpu.make_async_copy(got_far, got_ref, sems.at[1])
    load.start()
    odd = par_ref[0, 0]
    sources = foot_ref.shape[0]
    rows = flux_ref.shape[0]
    first = (rows - RAD) * odd
    groups = out_ref.shape[1]
    lane = lane_ids((sources, LANES))
    table = table_ref[...]
    copy = pltpu.make_async_copy(table_ref, table_smem, sems.at[0])
    copy.start()
    load.wait()
    for k in range(RAD):
        line = jnp.where(odd == 1, RAD - 1 - k, k)
        flux_ref[first + line] = flux_in[first + line] + scale_ref[line] * got_ref[k].astype(F32)
    copy.wait()

    def body(source, carry):
        for c, block in blocks_of(foot_ref, source, heights, slots):
            offset = table_smem[source, c]
            row = lax.shift_right_logical(offset, shift)
            begin = jnp.bitwise_and(offset, (1 << shift) - 1)
            product = flux_ref[row, pl.ds(begin, heights), :] * block
            sums[c, pl.ds(source, 1), :] = jnp.sum(product, axis=0, keepdims=True)
        return carry

    lax.fori_loop(0, sources, body, 0)
    totals = [jnp.zeros((sources, LANES), F32) for _ in range(groups)]
    for c in range(slots):
        value = jnp.sum(sums[c], axis=1, keepdims=True)
        which = table[:, 3 * slots + c : 3 * slots + c + 1]
        for q in range(groups):
            totals[q] = totals[q] + jnp.where(which == lane + q * LANES, value, 0.0)
    for q in range(groups):
        total = jnp.sum(totals[q], axis=0, keepdims=True)
        out_ref[:, q : q + 1, :] = jnp.broadcast_to(total[None], (sources, 1, LANES))


def adjoint_kernel(
    par_ref, table_vmem, seen_ref, got_ref, foot_ref, scale_ref,
    model_ref, factor_ref, field_ref, rows_even, last_ref, first_ref,
    weight_rows, table_ref, sem, *, shift, slots, heights, tiles, per,
):
    load = pltpu.make_async_copy(table_vmem, table_ref, sem)
    load.start()
    sources = foot_ref.shape[0]
    groups = got_ref.shape[1]
    rows, hours, _ = field_ref.shape
    model = jnp.sum(got_ref[:, 0:groups, :], axis=0)
    packed = LANES // per
    lane = lane_ids((1, LANES))
    own = jnp.zeros((1, LANES), F32)
    for q in range(groups):
        for k in range(packed):
            line = model[q : q + 1, :]
            line = line if k == 0 else pltpu.roll(line, LANES - k * per, 1)
            own = choose(par_ref[2:3, :] == q * packed + k, line, own)
    model_ref[...] = own
    weights = []
    for q in range(groups):
        observed, error = jnp.zeros((1, LANES), F32), jnp.ones((1, LANES), F32)
        for k in range(packed):
            source = (q * packed + k) * tiles
            line = seen_ref[source : source + 1, :]
            here = (lane >= k * per) & (lane < (k + 1) * per)
            observed = jnp.where(here, line if k == 0 else pltpu.roll(line, k * per, 1), observed)
            turn = (k * per - per) % LANES
            error = jnp.where(here, line if turn == 0 else pltpu.roll(line, turn, 1), error)
        weights.append((model[q : q + 1, :] - observed) / (error * error))
    lanes = lane_ids((sources, LANES))
    table = table_vmem[...]
    for c in range(slots):
        which = table[:, 3 * slots + c : 3 * slots + c + 1]
        found = jnp.zeros((sources, LANES), F32)
        for q in range(groups):
            found = jnp.where(which == lanes + q * LANES, weights[q], found)
        weight_rows[c] = jnp.broadcast_to(jnp.sum(found, axis=1, keepdims=True), (sources, LANES))
    field_ref[...] = jnp.zeros_like(field_ref)
    largest = jnp.abs(weights[0])
    for weight in weights[1:]:
        largest = jnp.maximum(largest, jnp.abs(weight))
    top = jnp.max(largest, keepdims=True) * (FOOT_MAX * SCALE_MAX * sources * slots)
    top = jnp.maximum(top, 1e-25)
    factor_ref[0:1, :] = jnp.broadcast_to(HALF_TOP / top, (1, LANES))
    factor_ref[1:2, :] = jnp.broadcast_to(top * (1.0 / HALF_TOP), (1, LANES))
    load.wait()

    def body(source, carry):
        for c, block in blocks_of(foot_ref, source, heights, slots):
            offset = table_ref[source, c]
            row = lax.shift_right_logical(offset, shift)
            begin = jnp.bitwise_and(offset, (1 << shift) - 1)
            weight = weight_rows[c, pl.ds(source, 1), :]
            field_ref[row, pl.ds(begin, heights), :] += block * weight
        return carry

    lax.fori_loop(0, sources, body, 0)
    for row in range(rows):
        field_ref[row] = field_ref[row] * scale_ref[row]
    rows_kernel(par_ref, None, factor_ref, field_ref, rows_even, even=True)
    write_strips(field_ref, last_ref, first_ref)


def swap_pairs(count, odd):
    pairs = []
    for i in range(1 if odd else 0, count - 1, 2):
        pairs += [(i, i + 1), (i + 1, i)]
    return pairs


def swap(axis, even, odd):
    count = lax.axis_size(axis)
    return (
        lax.ppermute(even, axis, swap_pairs(count, False)),
        lax.ppermute(odd, axis, swap_pairs(count, True)),
    )


VM = pl.BlockSpec(memory_space=pltpu.VMEM)
HB = pl.BlockSpec(memory_space=pltpu.HBM)


def call(kernel, out_shape, in_specs, scratch, name, out_specs=None, alias=None):
    return pl.pallas_call(
        kernel,
        out_shape=out_shape,
        in_specs=in_specs,
        out_specs=jax.tree.map(lambda _: VM, out_shape) if out_specs is None else out_specs,
        scratch_shapes=scratch,
        input_output_aliases={} if alias is None else alias,
        compiler_params=pltpu.CompilerParams(vmem_limit_bytes=VMEM_LIMIT),
        name=name,
    )


def far(x):
    return pltpu.with_memory_space_constraint(x, pltpu.HBM)


def array(*shape):
    return jax.ShapeDtypeStruct(shape, F32)


def per_device(
    prior_flux,
    flux_scale,
    control,
    footprint,
    slot_count,
    start_hour,
    grid_row,
    receptor_slot,
    observed,
    obs_error,
):
    hours, rows, cols = control.shape
    n_rec, n_tile = lax.axis_size("rec"), lax.axis_size("tile")
    devices = n_rec * n_tile
    slots, heights = footprint.shape[1], footprint.shape[2]
    per = observed.shape[0]
    groups = per * n_rec // LANES
    shift = (hours - 1).bit_length()
    rec, tile = lax.axis_index("rec"), lax.axis_index("tile")
    flags = [rec % 2, rec * 0, rec, tile == 0, tile == n_tile - 1] + [rec * 0] * (SUB - 5)
    par = jnp.stack([flag.astype(jnp.int32) for flag in flags])
    par = jnp.broadcast_to(par[:, None], (SUB, LANES))
    base, own_parts, corner_parts, beyond_parts = constants(hours, rows, cols)
    base = [jnp.asarray(c) for c in base]
    own_parts = jnp.asarray(own_parts)
    corner_parts = jnp.asarray(corner_parts)
    beyond_parts = jnp.asarray(beyond_parts)
    strip = array(-(-hours // (2 * SUB)) * SUB, LANES)
    corner = array(-(-hours // (4 * SUB)) * SUB, LANES)
    block = array(RAD, hours, cols)
    field_shape = array(rows, hours, cols)
    row_scratch = pltpu.VMEM((RAD, hours, cols), F32)

    def pass_strips(last, first):
        onward = [(i, (i + 1) % n_tile) for i in range(n_tile)]
        back = [(j, i) for i, j in onward]
        return lax.ppermute(last, "tile", onward), lax.ppermute(first, "tile", back)

    def swaps(after, field, got_strips, name):
        local = call(local_kernel, field_shape, [VM] * 5, [], name + "_local")(after, field, *base)
        corners = call(far_corner_kernel, [corner, corner], [VM] * 4, [], name + "_corners")(par, local, *got_strips)
        return local, swap("rec", *corners)

    def strip_sums(local, got_strips, by_hour, name):
        def kernel(*refs):
            strips_kernel(*refs, by_hour=by_hour)

        shape = array(hours, rows, cols) if by_hour else field_shape
        return call(kernel, shape, [VM] * 7, [], name)(par, local, *got_strips, *base[:2], own_parts)

    def swap_rows(even, after, factor, field, name):
        def kernel(*refs):
            rows_kernel(*refs, even=even)

        sent = call(kernel, block, [VM] * 4, [], name)(par, after, factor, field)
        return sent, lax.ppermute(sent.astype(F16), "rec", swap_pairs(n_rec, not even))

    def prepare(*refs):
        prepare_kernel(*refs, per=per)

    numbers = pltpu.VMEM((slots, devices), jnp.int32)
    lines = slots * heights + SUB
    sent = call(
        prepare,
        jax.ShapeDtypeStruct((devices, lines, cols), BF16),
        [VM] + [HB] * 7,
        [
            pltpu.VMEM((devices, slots * heights, cols), BF16),
            pltpu.VMEM((devices, SUB, LANES), BF16),
            numbers, numbers, numbers, pltpu.VMEM((1, devices), jnp.int32),
            pltpu.VMEM((1, per), F32), pltpu.VMEM((1, per), F32),
            pltpu.SemaphoreType.DMA((7 + 2 * PARTS,)),
        ],
        "prepare_blocks",
        out_specs=HB,
    )(par, *[
        far(x)
        for x in (
            footprint.reshape(devices, slots * heights, cols),
            start_hour.T, grid_row.T, receptor_slot.T, slot_count[None], observed[None], obs_error[None],
        )
    ])
    foot = lax.all_to_all(sent, AXES, split_axis=0, concat_axis=0, tiled=True)
    field, *strips = call(
        turn_kernel, [field_shape, strip, strip], [HB, VM], [], "turn_control"
    )(sent, control)
    got_strips = pass_strips(*strips)
    local = call(local_kernel, field_shape, [VM] * 5, [], "control_local")(strips[0], field, *base)
    small = jax.ShapeDtypeStruct((RAD, hours, cols), BF16)
    sent_even, sent_odd = call(beyond_kernel, [small, small], [VM] * 8, [], "control_beyond")(
        par, field, *got_strips, *base, beyond_parts
    )
    got_even, got_odd = swap("rec", sent_even, sent_odd)
    local = strip_sums(local, got_strips, False, "control_strips")
    flux, scale = call(
        flux_kernel, [field_shape, field_shape], [VM] * 5, [pltpu.VMEM((hours, rows, cols), F32)], "flux_field"
    )(par, local, prior_flux, flux_scale, got_even)

    sizes = dict(shift=shift, slots=slots, heights=heights, tiles=n_tile, per=per)

    def forward(*refs):
        forward_kernel(*refs, **sizes)


    def load(*refs):
        load_kernel(*refs, empty=groups * LANES, **sizes)

    table, seen, scale_near, flux_near = call(
        load,
        [jax.ShapeDtypeStruct((devices, LANES), jnp.int32), array(devices, LANES), block, field_shape],
        [VM, VM, HB, HB],
        [pltpu.SemaphoreType.DMA((1 + rows // RAD,))],
        "load_flux",
    )(par, foot, far(scale), far(flux))
    table, got_odd = lax.optimization_barrier((table, got_odd))
    partial, _ = call(
        forward,
        [array(devices, groups, LANES), field_shape],
        [VM] * 3 + [HB] + [VM] * 2,
        [
            pltpu.VMEM((RAD, hours, cols), BF16),
            pltpu.VMEM((slots, devices, LANES), F32),
            pltpu.SMEM((devices, LANES), jnp.int32),
            pltpu.SemaphoreType.DMA((2,)),
        ],
        "block_values",
        alias={4: 1},
    )(par, foot, table, far(got_odd), flux_near, scale_near)
    everyone = lax.all_to_all(partial, AXES, split_axis=0, concat_axis=0, tiled=True)

    def adjoint(*refs):
        adjoint_kernel(*refs, **sizes)

    model, factor, field, sent_even, *strips = call(
        adjoint,
        [array(1, LANES), array(2, LANES), field_shape, block, strip, strip],
        [VM] * 6,
        [
            pltpu.VMEM((slots, devices, LANES), F32),
            pltpu.SMEM((devices, LANES), jnp.int32),
            pltpu.SemaphoreType.DMA,
        ],
        "adjoint_field",
    )(par, table, seen, everyone, foot, scale)
    got_even = lax.ppermute(sent_even.astype(F16), "rec", swap_pairs(n_rec, False))
    got_strips = pass_strips(*strips)
    sent_odd, got_odd = swap_rows(False, strips[0], factor, field, "gradient_odd")
    local, got_corners = swaps(sent_odd, field, got_strips, "gradient")
    local = strip_sums(local, got_strips, False, "gradient_strips")
    local = call(even_kernel, array(hours, rows, cols), [VM] * 9, [row_scratch], "gradient_with_even")(
        par, local, factor, got_even.astype(F32), got_corners[0], *base, corner_parts
    )
    wide = pltpu.VMEM((hours, rows // 2, cols), F32)
    model_co2, gradient = call(
        finish_kernel,
        [array(1, per), array(hours, rows, cols)],
        [VM] * 10,
        [row_scratch, wide, wide, pltpu.VMEM((1, per), F32), pltpu.SemaphoreType.DMA((3,))],
        "gradient",
        out_specs=[HB, HB],
    )(par, model, local, factor, got_odd.astype(F32), got_corners[1], *base, corner_parts)
    return (model_co2.reshape(-1), gradient)


def solution(mesh):
    return jax.shard_map(
        per_device,
        mesh=mesh,
        in_specs=(
            P(None, "rec", "tile"),
            P(None, "rec", "tile"),
            P(None, "rec", "tile"),
            P(("rec", "tile"), None, None, None),
            P(("rec", "tile")),
            P(("rec", "tile"), None),
            P(("rec", "tile"), None),
            P(("rec", "tile"), None),
            P("rec"),
            P("rec"),
        ),
        out_specs=(P("rec"), P(None, "rec", "tile")),
        check_vma=False,
    )
```

```python
import numpy as np
import jax
import jax.numpy as jnp
from jax import lax
from jax.experimental import pallas as pl
from jax.experimental.pallas import tpu as pltpu
from jax.sharding import PartitionSpec as P

RAD = 4
TAPS = 12
AXES = ("rec", "tile")
LANES = 128
SUB = 8
FOOT_MAX = 0.02
PARTS = 4
SCALE_MAX = 2.0
HALF_TOP = 32768.0
F16 = jnp.float16
VMEM_LIMIT = 14 * 1024 * 1024
F32 = jnp.float32
BF16 = jnp.bfloat16


def space_taps():
    offsets = np.arange(-RAD, RAD + 1).astype(np.float64)
    values = np.exp(-2.0 * offsets * offsets / (RAD * RAD))
    return values / np.sqrt(np.sum(values * values))


def time_taps():
    offsets = np.arange(-TAPS, TAPS + 1).astype(np.float64)
    values = np.exp(-2.0 * np.abs(offsets) / TAPS)
    return values / np.sqrt(np.sum(values * values))


def banded(distance, taps, reach):
    inside = np.abs(distance) <= reach
    return np.where(inside, taps[np.clip(distance, -reach, reach) + reach], 0.0)


def two_parts(matrix):
    high = matrix.astype(np.float32).astype(jnp.bfloat16)
    low = (matrix - high.astype(np.float64)).astype(np.float32).astype(jnp.bfloat16)
    return high, low


def constants(hours, rows, cols):
    space = space_taps()
    hour = np.arange(hours)
    time_high, time_low = two_parts(banded(hour[:, None] - hour[None, :], time_taps(), TAPS))
    col = np.arange(cols)
    col_high, col_low = two_parts(banded(col[:, None] - col[None, :], space, RAD))
    col_both = np.block([[col_high, col_low], [col_high, np.zeros_like(col_high)]])
    halo_col = np.concatenate([np.arange(-RAD, 0), np.arange(cols, cols + RAD)])
    edge = banded(halo_col[:, None] - col[None, :], space, RAD)

    def strips(row_of, halo_of, targets):
        by_row = banded(np.array(row_of)[:, None] - np.array(targets)[None, :], space, RAD)
        both = by_row[:, :, None] * edge[np.array(halo_of)][:, None, :]
        high, low = two_parts(both.reshape(len(row_of), -1))
        return np.concatenate([high, high, low], axis=0)

    own = [(row, side * RAD + j) for side in range(2) for row in range(rows) for j in range(RAD)]
    corner = []
    for first, targets in ((rows, rows - 1 - np.arange(RAD)), (-RAD, np.arange(RAD))):
        lanes = [
            (row, side * RAD + j) for side in range(2) for row in range(first, first + RAD) for j in range(RAD)
        ]
        corner.append(strips(*zip(*lanes), targets))
    beyond = [strips(*zip(*own), rows + np.arange(RAD)), strips(*zip(*own), -1 - np.arange(RAD))]
    return (
        (time_high, time_low, col_both),
        strips(*zip(*own), np.arange(rows)),
        np.stack(corner),
        np.stack(beyond),
    )


def split(value):
    high = value.astype(BF16)
    low = (value - high.astype(F32)).astype(BF16)
    return high, low


def dot(a, b):
    return jnp.dot(a, b, preferred_element_type=F32)


def lane_ids(shape):
    return lax.broadcasted_iota(jnp.int32, shape, 1)


def choose(flag, yes, no):
    return jnp.where(flag, yes, no)


def pack_strips(row_value, rows):
    cols = row_value(0).shape[1]
    half = rows * RAD
    source = lax.broadcasted_iota(jnp.int32, (cols, 2 * half), 0)
    lane = lane_ids((cols, 2 * half))
    first = lane < half
    j = lane & (RAD - 1)
    wanted = jnp.where(first, cols - RAD + j, j)
    lane_row = jnp.where(first, lane, lane - half) // RAD
    total = None
    for row in range(rows):
        high, low = split(row_value(row))
        pick = jnp.where((source == wanted) & (lane_row == row), 1.0, 0.0).astype(BF16)
        part = dot(jnp.concatenate([high, low], axis=1), jnp.concatenate([pick, pick], axis=0))
        total = part if total is None else total + part
    return total


def fold_corners(strips, last_ref, first_ref):
    quarter = last_ref.shape[0]
    half, part = LANES // 2, RAD * RAD
    lane = lane_ids((quarter, LANES))
    spare = jnp.zeros((4 * quarter - strips.shape[0], LANES), F32)
    whole = jnp.concatenate([strips, spare], axis=0)
    low = high = jnp.zeros((quarter, LANES), F32)
    for q in range(LANES // (2 * part)):
        piece = whole[q * quarter : (q + 1) * quarter]
        for side in range(2):
            to = q * 2 * part + side * part
            here = (lane >= to) & (lane < to + part)
            low = choose(here, pltpu.roll(piece, (to - side * half) % LANES, 1), low)
            high = choose(here, pltpu.roll(piece, (to - side * half - (half - part)) % LANES, 1), high)
    last_ref[...] = high
    first_ref[...] = low


def unfold_corners(value):
    part = 2 * RAD * RAD
    pieces = [value] + [pltpu.roll(value, LANES - q * part, 1) for q in range(1, LANES // part)]
    return jnp.concatenate(pieces, axis=0)


def is_odd(par_ref, axis):
    return par_ref[axis : axis + 1, :] == 1


def rows_kernel(par_ref, after, factor_ref, field_ref, out_ref, *, even):
    odd = is_odd(par_ref, 0)
    factor = factor_ref[0:1, :]
    rows = field_ref.shape[0]
    for row in range(RAD):
        first, last = field_ref[row], field_ref[rows - 1 - row]
        out_ref[row] = (choose(odd, first, last) if even else choose(odd, last, first)) * factor


def turn_kernel(after, control_ref, field_ref, last_ref, first_ref):
    rows = control_ref.shape[1]
    for row in range(rows):
        field_ref[row] = control_ref[:, row, :]
    write_strips(field_ref, last_ref, first_ref)


def strip_kernel(after, field_ref, last_ref, first_ref):
    write_strips(field_ref, last_ref, first_ref)


def write_strips(field_ref, last_ref, first_ref):
    strips = pack_strips(lambda r: field_ref[r], field_ref.shape[0])
    fold, half = last_ref.shape[0], LANES // 2
    early, late = strips[0:fold], strips[fold:]
    if late.shape[0] < fold:
        late = jnp.concatenate([late, jnp.zeros((fold - late.shape[0], LANES), F32)], axis=0)
    left = lane_ids(early.shape) < half
    last_ref[...] = jnp.where(left, early, pltpu.roll(late, half, 1))
    first_ref[...] = jnp.where(left, pltpu.roll(early, half, 1), late)


def halo_columns(par_ref, before_ref, after_ref):
    before, after = before_ref[...], after_ref[...]
    half = LANES // 2
    left = lane_ids(before.shape) < half
    early = jnp.where(left, before, pltpu.roll(after, half, 1))
    late = jnp.where(left, pltpu.roll(before, half, 1), after)
    outside = jnp.where(lane_ids((1, LANES)) < half, par_ref[3:4, :], par_ref[4:5, :])
    return jnp.where(outside == 1, 0.0, jnp.concatenate([early, late], axis=0))


def far_corner_kernel(par_ref, after, before_ref, after_ref, last_ref, first_ref):
    fold_corners(halo_columns(par_ref, before_ref, after_ref), last_ref, first_ref)


def prepare_kernel(
    after, foot_ref, start_ref, row_ref, slot_ref, count_ref, observed_ref, error_ref, out_ref,
    blocks_ref, notes_ref, start_vmem, row_vmem, slot_vmem, count_vmem, observed_vmem, error_vmem, sems, *, per,
):
    owners, lines, _ = foot_ref.shape
    slots = start_ref.shape[0]
    pairs = (
        (start_ref, start_vmem), (row_ref, row_vmem), (slot_ref, slot_vmem), (count_ref, count_vmem),
        (observed_ref, observed_vmem), (error_ref, error_vmem),
    )
    small = [pltpu.make_async_copy(a, b, sems.at[i]) for i, (a, b) in enumerate(pairs)]
    chunk = owners // PARTS
    parts = [slice(i * chunk, (i + 1) * chunk) for i in range(PARTS)]
    loads = [
        pltpu.make_async_copy(foot_ref.at[here], blocks_ref.at[here], sems.at[6 + i])
        for i, here in enumerate(parts)
    ]
    for copy in small + loads:
        copy.start()
    stores = []
    for i, here in enumerate(parts):
        loads[i].wait()
        to = out_ref.at[here, 0:lines, :]
        stores.append(pltpu.make_async_copy(blocks_ref.at[here], to, sems.at[6 + PARTS + i]))
        stores[-1].start()
    for copy in small:
        copy.wait()
    start = start_vmem[...]
    valid = lax.broadcasted_iota(jnp.int32, start.shape, 0) < count_vmem[...]
    lanes = jnp.concatenate(
        [start >> 4, start & 15, row_vmem[...], jnp.where(valid, slot_vmem[...], per)], axis=0
    ).astype(F32)
    wide = jnp.pad(lanes, ((0, LANES - 4 * slots), (0, LANES - owners)))
    turned = jnp.transpose(wide)[0:owners]
    spare = [jnp.zeros((1, LANES - 2 * per), F32)] if 2 * per < LANES else []
    own = jnp.concatenate([observed_vmem[...], error_vmem[...]] + spare, axis=1)
    line = lax.broadcasted_iota(jnp.int32, notes_ref.shape, 1)
    value = jnp.broadcast_to(turned[:, None, :], notes_ref.shape)
    for k in range(3):
        term = own.astype(BF16).astype(F32)
        own = own - term
        value = jnp.where(line == 1 + k, term[None], value)
    notes_ref[...] = value.astype(BF16)
    stores.append(pltpu.make_async_copy(notes_ref, out_ref.at[:, lines : lines + SUB, :], sems.at[6 + 2 * PARTS]))
    stores[-1].start()
    for copy in stores:
        copy.wait()


def halo_parts(value):
    high, low = split(value)
    lanes = [high, low] + ([high] if value.shape[1] < LANES else [])
    return jnp.concatenate(lanes, axis=1)


def halo_sums(both, weights_ref, first, width):
    used = both.shape[1]
    out = dot(both, weights_ref[0:used, first : first + width])
    if used < weights_ref.shape[0]:
        out = out + dot(both[:, : used // 2], weights_ref[used:, first : first + width])
    return out


def column_sums(value, col_both):
    cols = value.shape[1]
    high, low = split(value)
    out = dot(jnp.concatenate([high, low], axis=1), col_both)
    return out[:, :cols] + out[:, cols:]


def time_sums(value, time_high, time_low):
    high, low = split(value)
    return dot(time_high, high) + dot(time_high, low) + dot(time_low, high)


def row_sums(get, row, low, high, taps):
    total = None
    for distance in range(RAD + 1):
        here = [get(r) for r in sorted({row - distance, row + distance}) if low <= r < high]
        if not here:
            continue
        part = here[0] if len(here) == 1 else here[0] + here[1]
        part = float(taps[RAD + distance]) * part
        total = part if total is None else total + part
    return total


def local_kernel(after, field_ref, time_high, time_low, col_both, out_ref):
    rows, hours, cols = field_ref.shape
    taps = space_taps()
    for row in range(0, rows, 2):
        pair = [
            column_sums(row_sums(lambda i: field_ref[i], r, 0, rows, taps), col_both[...])
            for r in (row, row + 1)
        ]
        both = time_sums(jnp.concatenate(pair, axis=1), time_high[...], time_low[...])
        for k, r in enumerate((row, row + 1)):
            out_ref[r] = both[:, k * cols : (k + 1) * cols]


def strip_halo(par_ref, before_ref, after_ref, time_high, time_low):
    halo = halo_columns(par_ref, before_ref, after_ref)[0 : time_high.shape[0]]
    return halo_parts(time_sums(halo, time_high[...], time_low[...]))


def strips_kernel(
    par_ref, local_ref, before_ref, after_ref, time_high, time_low, own_ref, out_ref, *, by_hour
):
    rows, hours, cols = local_ref.shape
    halo = strip_halo(par_ref, before_ref, after_ref, time_high, time_low)
    for row in range(0, rows, 2):
        both = halo_sums(halo, own_ref, row * cols, 2 * cols)
        for k, r in enumerate((row, row + 1)):
            value = local_ref[r] + both[:, k * cols : (k + 1) * cols]
            if by_hour:
                out_ref[:, r, :] = value
            else:
                out_ref[r] = value


def beyond_sums(rows, corner, corner_weights, consts):
    time_high, time_low, col_both = consts
    cols = col_both.shape[1] // 2
    taps = space_taps()
    parts = []
    for k in range(0, RAD, 2):
        pair = []
        for i in (k, k + 1):
            summed = None
            for j in range(RAD - i):
                part = float(taps[RAD + i + j + 1]) * rows(j)
                summed = part if summed is None else summed + part
            pair.append(column_sums(summed, col_both[...]))
        value = jnp.concatenate(pair, axis=1) + halo_sums(corner, corner_weights, k * cols, 2 * cols)
        both = time_sums(value, time_high[...], time_low[...])
        parts += [both[:, :cols], both[:, cols:]]
    return parts


def edge_parts(halo, corner, corner_weights, consts):
    corner = halo_parts(unfold_corners(corner)[0 : halo.shape[1], 0 : corner_weights.shape[0] // 3])
    return beyond_sums(lambda j: halo[j], corner, corner_weights, consts)


def beyond_kernel(
    par_ref, field_ref, before_ref, after_ref, time_high, time_low, col_both, beyond_ref, out_even, out_odd,
):
    rows, hours, _ = field_ref.shape
    odd = is_odd(par_ref, 0)
    halo = halo_parts(halo_columns(par_ref, before_ref, after_ref)[0:hours])
    consts = (time_high, time_low, col_both)
    to_after = beyond_sums(lambda j: field_ref[rows - 1 - j], halo, beyond_ref.at[0], consts)
    to_before = beyond_sums(lambda j: field_ref[j], halo, beyond_ref.at[1], consts)
    for k in range(RAD):
        out_even[k] = choose(odd, to_before[k], to_after[k]).astype(BF16)
        out_odd[k] = choose(odd, to_after[k], to_before[k]).astype(BF16)


def flux_kernel(par_ref, local_ref, prior_ref, scale_ref, got_ref, flux_ref, scale_out, wide):
    rows = local_ref.shape[0]
    odd = par_ref[0, 0]
    wide[...] = scale_ref[...].astype(F32)
    for row in range(rows):
        scale_out[row] = wide[:, row, :]
    wide[...] = prior_ref[...].astype(F32)
    for row in range(rows):
        flux_ref[row] = wide[:, row, :] + scale_out[row] * local_ref[row]
    for k in range(RAD):
        row = jnp.where(odd == 1, k, rows - 1 - k)
        flux_ref[row] = flux_ref[row] + scale_out[row] * got_ref[k].astype(F32)


def finish_kernel(
    par_ref, model_ref, local_ref, factor_ref, got_e, got_o, corner_before, corner_after,
    time_high, time_low, col_both, corner_weights,
    model_out, out_ref, halo, edges, total, model_own, sems,
):
    hours, rows, cols = local_ref.shape
    half = rows // 2
    odd = is_odd(par_ref, 0)
    factor = factor_ref[1:2, :]
    consts = (time_high, time_low, col_both)
    model_own[...] = model_ref[:, 0 : model_own.shape[1]]
    copies = [pltpu.make_async_copy(model_own, model_out, sems.at[2])]
    copies[0].start()
    inside = lax.broadcasted_iota(jnp.int32, (hours, half, cols), 1)
    for side in range(2):
        before = side == 0
        for k in range(RAD):
            even, other = got_e[k], got_o[k]
            halo[k] = (choose(odd, even, other) if before else choose(odd, other, even)) * factor
        corner = corner_before[...] if before else corner_after[...]
        corner = jnp.where(par_ref[5 + side : 6 + side, :] == 1, 0.0, corner)
        parts = edge_parts(halo, corner, corner_weights.at[1 - side], consts)
        for k, part in enumerate(parts):
            edges[:, k if before else half - 1 - k, :] = part
        here = slice(0, half) if before else slice(rows - half, rows)
        mine = inside < RAD if before else inside >= half - RAD
        total[:, here, :] = local_ref[:, here, :] + jnp.where(mine, edges[...], 0.0)
        copies.append(pltpu.make_async_copy(total.at[:, here, :], out_ref.at[:, here, :], sems.at[side]))
        copies[-1].start()
    for copy in copies:
        copy.wait()


def blocks_of(foot_ref, source, heights, slots):
    for c in range(0, slots, 2):
        both = foot_ref[source, c * heights : (c + 2) * heights, :].astype(F32)
        yield c, both[0:heights]
        yield c + 1, both[heights : 2 * heights]


def load_kernel(
    par_ref, foot_ref, scale_far, *refs, shift, slots, heights, tiles, per, empty
):
    count = (len(refs) - 4) // 2
    distant, near = refs[:count], refs[count + 3 : -1]
    table_ref, seen_ref, scale_ref = refs[count : count + 3]
    sems = refs[-1]
    flux_far, flux_ref = distant[0], near[0]
    rows = flux_ref.shape[0]
    first = (rows - RAD) * par_ref[0, 0]
    pairs = [(flux_far.at[r : r + RAD], flux_ref.at[r : r + RAD]) for r in range(0, rows, RAD)]
    pairs += list(zip(distant[1:], near[1:])) + [(scale_far.at[pl.ds(first, RAD)], scale_ref)]
    loads = [pltpu.make_async_copy(a, b, sems.at[i]) for i, (a, b) in enumerate(pairs)]
    for load in loads:
        load.start()
    sources = foot_ref.shape[0]
    base = slots * heights
    lane = lane_ids((sources, LANES))
    lines = foot_ref[:, base : base + SUB, :].astype(F32)
    notes = lines[:, 0, :].astype(jnp.int32)
    seen_ref[...] = lines[:, 1, :] + lines[:, 2, :] + lines[:, 3, :]
    start = notes * 16 + pltpu.roll(notes, LANES - slots, 1)
    offset = start + pltpu.roll(notes, LANES - 2 * slots, 1) * (1 << shift)
    source_rec = lax.broadcasted_iota(jnp.int32, (sources, LANES), 0) // tiles
    receptor = jnp.where(notes < per, source_rec * per + notes, empty)
    table_ref[...] = jnp.where(lane < slots, offset, receptor)
    for load in loads:
        load.wait()


def forward_kernel(
    par_ref, foot_ref, table_ref, got_far, flux_in, scale_ref,
    out_ref, flux_ref, got_ref, sums, table_smem, sems, *, shift, slots, heights, tiles, per,
):
    load = pltpu.make_async_copy(got_far, got_ref, sems.at[1])
    load.start()
    odd = par_ref[0, 0]
    sources = foot_ref.shape[0]
    rows = flux_ref.shape[0]
    first = (rows - RAD) * odd
    groups = out_ref.shape[1]
    lane = lane_ids((sources, LANES))
    table = table_ref[...]
    copy = pltpu.make_async_copy(table_ref, table_smem, sems.at[0])
    copy.start()
    load.wait()
    for k in range(RAD):
        line = jnp.where(odd == 1, RAD - 1 - k, k)
        flux_ref[first + line] = flux_in[first + line] + scale_ref[line] * got_ref[k].astype(F32)
    copy.wait()

    def body(source, carry):
        for c, block in blocks_of(foot_ref, source, heights, slots):
            offset = table_smem[source, c]
            row = lax.shift_right_logical(offset, shift)
            begin = jnp.bitwise_and(offset, (1 << shift) - 1)
            product = flux_ref[row, pl.ds(begin, heights), :] * block
            sums[c, pl.ds(source, 1), :] = jnp.sum(product, axis=0, keepdims=True)
        return carry

    lax.fori_loop(0, sources, body, 0)
    totals = [jnp.zeros((sources, LANES), F32) for _ in range(groups)]
    for c in range(slots):
        value = jnp.sum(sums[c], axis=1, keepdims=True)
        which = table[:, 3 * slots + c : 3 * slots + c + 1]
        for q in range(groups):
            totals[q] = totals[q] + jnp.where(which == lane + q * LANES, value, 0.0)
    for q in range(groups):
        total = jnp.sum(totals[q], axis=0, keepdims=True)
        out_ref[:, q : q + 1, :] = jnp.broadcast_to(total[None], (sources, 1, LANES))


def adjoint_kernel(
    par_ref, table_vmem, seen_ref, got_ref, foot_ref, scale_ref,
    model_ref, factor_ref, field_ref, rows_even, last_ref, first_ref,
    weight_rows, table_ref, sem, *, shift, slots, heights, tiles, per,
):
    load = pltpu.make_async_copy(table_vmem, table_ref, sem)
    load.start()
    sources = foot_ref.shape[0]
    groups = got_ref.shape[1]
    rows, hours, _ = field_ref.shape
    model = jnp.sum(got_ref[:, 0:groups, :], axis=0)
    packed = LANES // per
    lane = lane_ids((1, LANES))
    own = jnp.zeros((1, LANES), F32)
    for q in range(groups):
        for k in range(packed):
            line = model[q : q + 1, :]
            line = line if k == 0 else pltpu.roll(line, LANES - k * per, 1)
            own = choose(par_ref[2:3, :] == q * packed + k, line, own)
    model_ref[...] = own
    weights = []
    for q in range(groups):
        observed, error = jnp.zeros((1, LANES), F32), jnp.ones((1, LANES), F32)
        for k in range(packed):
            source = (q * packed + k) * tiles
            line = seen_ref[source : source + 1, :]
            here = (lane >= k * per) & (lane < (k + 1) * per)
            observed = jnp.where(here, line if k == 0 else pltpu.roll(line, k * per, 1), observed)
            turn = (k * per - per) % LANES
            error = jnp.where(here, line if turn == 0 else pltpu.roll(line, turn, 1), error)
        weights.append((model[q : q + 1, :] - observed) / (error * error))
    lanes = lane_ids((sources, LANES))
    table = table_vmem[...]
    for c in range(slots):
        which = table[:, 3 * slots + c : 3 * slots + c + 1]
        found = jnp.zeros((sources, LANES), F32)
        for q in range(groups):
            found = jnp.where(which == lanes + q * LANES, weights[q], found)
        weight_rows[c] = jnp.broadcast_to(jnp.sum(found, axis=1, keepdims=True), (sources, LANES))
    field_ref[...] = jnp.zeros_like(field_ref)
    largest = jnp.abs(weights[0])
    for weight in weights[1:]:
        largest = jnp.maximum(largest, jnp.abs(weight))
    top = jnp.max(largest, keepdims=True) * (FOOT_MAX * SCALE_MAX * sources * slots)
    top = jnp.maximum(top, 1e-25)
    factor_ref[0:1, :] = jnp.broadcast_to(HALF_TOP / top, (1, LANES))
    factor_ref[1:2, :] = jnp.broadcast_to(top * (1.0 / HALF_TOP), (1, LANES))
    load.wait()

    def body(source, carry):
        for c, block in blocks_of(foot_ref, source, heights, slots):
            offset = table_ref[source, c]
            row = lax.shift_right_logical(offset, shift)
            begin = jnp.bitwise_and(offset, (1 << shift) - 1)
            weight = weight_rows[c, pl.ds(source, 1), :]
            field_ref[row, pl.ds(begin, heights), :] += block * weight
        return carry

    lax.fori_loop(0, sources, body, 0)
    for row in range(rows):
        field_ref[row] = field_ref[row] * scale_ref[row]
    rows_kernel(par_ref, None, factor_ref, field_ref, rows_even, even=True)
    write_strips(field_ref, last_ref, first_ref)


def swap_pairs(count, odd):
    pairs = []
    for i in range(1 if odd else 0, count - 1, 2):
        pairs += [(i, i + 1), (i + 1, i)]
    return pairs


def swap(axis, even, odd):
    count = lax.axis_size(axis)
    return (
        lax.ppermute(even, axis, swap_pairs(count, False)),
        lax.ppermute(odd, axis, swap_pairs(count, True)),
    )


VM = pl.BlockSpec(memory_space=pltpu.VMEM)
HB = pl.BlockSpec(memory_space=pltpu.HBM)


def call(kernel, out_shape, in_specs, scratch, name, out_specs=None, alias=None):
    return pl.pallas_call(
        kernel,
        out_shape=out_shape,
        in_specs=in_specs,
        out_specs=jax.tree.map(lambda _: VM, out_shape) if out_specs is None else out_specs,
        scratch_shapes=scratch,
        input_output_aliases={} if alias is None else alias,
        compiler_params=pltpu.CompilerParams(vmem_limit_bytes=VMEM_LIMIT),
        name=name,
    )


def far(x):
    return pltpu.with_memory_space_constraint(x, pltpu.HBM)


def array(*shape):
    return jax.ShapeDtypeStruct(shape, F32)


def per_device(
    prior_flux,
    flux_scale,
    control,
    footprint,
    slot_count,
    start_hour,
    grid_row,
    receptor_slot,
    observed,
    obs_error,
):
    hours, rows, cols = control.shape
    n_rec, n_tile = lax.axis_size("rec"), lax.axis_size("tile")
    devices = n_rec * n_tile
    slots, heights = footprint.shape[1], footprint.shape[2]
    per = observed.shape[0]
    groups = per * n_rec // LANES
    shift = (hours - 1).bit_length()
    rec, tile = lax.axis_index("rec"), lax.axis_index("tile")
    flags = [rec % 2, rec * 0, rec, tile == 0, tile == n_tile - 1, rec == 0, rec == n_rec - 1]
    flags += [rec * 0] * (SUB - len(flags))
    par = jnp.stack([flag.astype(jnp.int32) for flag in flags])
    par = jnp.broadcast_to(par[:, None], (SUB, LANES))
    base, own_parts, corner_parts, beyond_parts = constants(hours, rows, cols)
    base = [jnp.asarray(c) for c in base]
    own_parts = jnp.asarray(own_parts)
    corner_parts = jnp.asarray(corner_parts)
    beyond_parts = jnp.asarray(beyond_parts)
    strip = array(-(-hours // (2 * SUB)) * SUB, LANES)
    corner = array(-(-hours // (4 * SUB)) * SUB, LANES)
    block = array(RAD, hours, cols)
    field_shape = array(rows, hours, cols)
    row_scratch = pltpu.VMEM((RAD, hours, cols), F32)

    def pass_on(axis, last, first):
        count = lax.axis_size(axis)
        onward = [(i, (i + 1) % count) for i in range(count)]
        back = [(j, i) for i, j in onward]
        return lax.ppermute(last, axis, onward), lax.ppermute(first, axis, back)

    def swaps(after, field, got_strips, name):
        local = call(local_kernel, field_shape, [VM] * 5, [], name + "_local")(after, field, *base)
        corners = call(far_corner_kernel, [corner, corner], [VM] * 4, [], name + "_corners")(par, local, *got_strips)
        return local, pass_on("rec", *corners)

    def strip_sums(local, got_strips, by_hour, name):
        def kernel(*refs):
            strips_kernel(*refs, by_hour=by_hour)

        shape = array(hours, rows, cols) if by_hour else field_shape
        return call(kernel, shape, [VM] * 7, [], name)(par, local, *got_strips, *base[:2], own_parts)

    def swap_rows(even, after, factor, field, name):
        def kernel(*refs):
            rows_kernel(*refs, even=even)

        sent = call(kernel, block, [VM] * 4, [], name)(par, after, factor, field)
        return sent, lax.ppermute(sent.astype(F16), "rec", swap_pairs(n_rec, not even))

    def prepare(*refs):
        prepare_kernel(*refs, per=per)

    numbers = pltpu.VMEM((slots, devices), jnp.int32)
    lines = slots * heights + SUB
    sent = call(
        prepare,
        jax.ShapeDtypeStruct((devices, lines, cols), BF16),
        [VM] + [HB] * 7,
        [
            pltpu.VMEM((devices, slots * heights, cols), BF16),
            pltpu.VMEM((devices, SUB, LANES), BF16),
            numbers, numbers, numbers, pltpu.VMEM((1, devices), jnp.int32),
            pltpu.VMEM((1, per), F32), pltpu.VMEM((1, per), F32),
            pltpu.SemaphoreType.DMA((7 + 2 * PARTS,)),
        ],
        "prepare_blocks",
        out_specs=HB,
    )(par, *[
        far(x)
        for x in (
            footprint.reshape(devices, slots * heights, cols),
            start_hour.T, grid_row.T, receptor_slot.T, slot_count[None], observed[None], obs_error[None],
        )
    ])
    foot = lax.all_to_all(sent, AXES, split_axis=0, concat_axis=0, tiled=True)
    field, *strips = call(
        turn_kernel, [field_shape, strip, strip], [HB, VM], [], "turn_control"
    )(sent, control)
    got_strips = pass_on("tile", *strips)
    local = call(local_kernel, field_shape, [VM] * 5, [], "control_local")(strips[0], field, *base)
    small = jax.ShapeDtypeStruct((RAD, hours, cols), BF16)
    sent_even, sent_odd = call(beyond_kernel, [small, small], [VM] * 8, [], "control_beyond")(
        par, field, *got_strips, *base, beyond_parts
    )
    got_even, got_odd = swap("rec", sent_even, sent_odd)
    local = strip_sums(local, got_strips, False, "control_strips")
    flux, scale = call(
        flux_kernel, [field_shape, field_shape], [VM] * 5, [pltpu.VMEM((hours, rows, cols), F32)], "flux_field"
    )(par, local, prior_flux, flux_scale, got_even)

    sizes = dict(shift=shift, slots=slots, heights=heights, tiles=n_tile, per=per)

    def forward(*refs):
        forward_kernel(*refs, **sizes)


    def load(*refs):
        load_kernel(*refs, empty=groups * LANES, **sizes)

    table, seen, scale_near, flux_near = call(
        load,
        [jax.ShapeDtypeStruct((devices, LANES), jnp.int32), array(devices, LANES), block, field_shape],
        [VM, VM, HB, HB],
        [pltpu.SemaphoreType.DMA((1 + rows // RAD,))],
        "load_flux",
    )(par, foot, far(scale), far(flux))
    table, got_odd = lax.optimization_barrier((table, got_odd))
    partial, _ = call(
        forward,
        [array(devices, groups, LANES), field_shape],
        [VM] * 3 + [HB] + [VM] * 2,
        [
            pltpu.VMEM((RAD, hours, cols), BF16),
            pltpu.VMEM((slots, devices, LANES), F32),
            pltpu.SMEM((devices, LANES), jnp.int32),
            pltpu.SemaphoreType.DMA((2,)),
        ],
        "block_values",
        alias={4: 1},
    )(par, foot, table, far(got_odd), flux_near, scale_near)
    everyone = lax.all_to_all(partial, AXES, split_axis=0, concat_axis=0, tiled=True)

    def adjoint(*refs):
        adjoint_kernel(*refs, **sizes)

    model, factor, field, sent_even, *strips = call(
        adjoint,
        [array(1, LANES), array(2, LANES), field_shape, block, strip, strip],
        [VM] * 6,
        [
            pltpu.VMEM((slots, devices, LANES), F32),
            pltpu.SMEM((devices, LANES), jnp.int32),
            pltpu.SemaphoreType.DMA,
        ],
        "adjoint_field",
    )(par, table, seen, everyone, foot, scale)
    got_even = lax.ppermute(sent_even.astype(F16), "rec", swap_pairs(n_rec, False))
    got_strips = pass_on("tile", *strips)
    sent_odd, got_odd = swap_rows(False, strips[0], factor, field, "gradient_odd")
    local, got_corners = swaps(sent_odd, field, got_strips, "gradient")
    local = strip_sums(local, got_strips, True, "gradient_strips")
    model_co2, gradient = call(
        finish_kernel,
        [array(1, per), array(hours, rows, cols)],
        [VM] * 12,
        [
            row_scratch,
            pltpu.VMEM((hours, rows // 2, cols), F32),
            pltpu.VMEM((hours, rows, cols), F32),
            pltpu.VMEM((1, per), F32),
            pltpu.SemaphoreType.DMA((3,)),
        ],
        "gradient",
        out_specs=[HB, HB],
    )(par, model, local, factor, got_even.astype(F32), got_odd.astype(F32), *got_corners, *base, corner_parts)
    return (model_co2.reshape(-1), gradient)


def solution(mesh):
    return jax.shard_map(
        per_device,
        mesh=mesh,
        in_specs=(
            P(None, "rec", "tile"),
            P(None, "rec", "tile"),
            P(None, "rec", "tile"),
            P(("rec", "tile"), None, None, None),
            P(("rec", "tile")),
            P(("rec", "tile"), None),
            P(("rec", "tile"), None),
            P(("rec", "tile"), None),
            P("rec"),
            P("rec"),
        ),
        out_specs=(P("rec"), P(None, "rec", "tile")),
        check_vma=False,
    )
```

```python
import numpy as np
import jax
import jax.numpy as jnp
from jax import lax
from jax.experimental import pallas as pl
from jax.experimental.pallas import tpu as pltpu
from jax.sharding import PartitionSpec as P

RAD = 4
TAPS = 12
AXES = ("rec", "tile")
LANES = 128
SUB = 8
FOOT_MAX = 0.02
PARTS = 4
PIECES = 3
SCALE_MAX = 2.0
HALF_TOP = 32768.0
F16 = jnp.float16
VMEM_LIMIT = 14 * 1024 * 1024
F32 = jnp.float32
BF16 = jnp.bfloat16


def space_taps():
    offsets = np.arange(-RAD, RAD + 1).astype(np.float64)
    values = np.exp(-2.0 * offsets * offsets / (RAD * RAD))
    return values / np.sqrt(np.sum(values * values))


def time_taps():
    offsets = np.arange(-TAPS, TAPS + 1).astype(np.float64)
    values = np.exp(-2.0 * np.abs(offsets) / TAPS)
    return values / np.sqrt(np.sum(values * values))


def banded(distance, taps, reach):
    inside = np.abs(distance) <= reach
    return np.where(inside, taps[np.clip(distance, -reach, reach) + reach], 0.0)


def two_parts(matrix):
    high = matrix.astype(np.float32).astype(jnp.bfloat16)
    low = (matrix - high.astype(np.float64)).astype(np.float32).astype(jnp.bfloat16)
    return high, low


def constants(hours, rows, cols):
    space = space_taps()
    hour = np.arange(hours)
    time_high, time_low = two_parts(banded(hour[:, None] - hour[None, :], time_taps(), TAPS))
    col = np.arange(cols)
    col_high, col_low = two_parts(banded(col[:, None] - col[None, :], space, RAD))
    col_both = np.block([[col_high, col_low], [col_high, np.zeros_like(col_high)]])
    halo_col = np.concatenate([np.arange(-RAD, 0), np.arange(cols, cols + RAD)])
    edge = banded(halo_col[:, None] - col[None, :], space, RAD)

    def strips(row_of, halo_of, targets):
        by_row = banded(np.array(row_of)[:, None] - np.array(targets)[None, :], space, RAD)
        both = by_row[:, :, None] * edge[np.array(halo_of)][:, None, :]
        high, low = two_parts(both.reshape(len(row_of), -1))
        return np.concatenate([high, high, low], axis=0)

    own = [(row, side * RAD + j) for side in range(2) for row in range(rows) for j in range(RAD)]
    corner = []
    for first, targets in ((rows, rows - 1 - np.arange(RAD)), (-RAD, np.arange(RAD))):
        lanes = [
            (row, side * RAD + j) for side in range(2) for row in range(first, first + RAD) for j in range(RAD)
        ]
        corner.append(strips(*zip(*lanes), targets))
    beyond = [strips(*zip(*own), rows + np.arange(RAD)), strips(*zip(*own), -1 - np.arange(RAD))]
    return (
        (time_high, time_low, col_both),
        strips(*zip(*own), np.arange(rows)),
        np.stack(corner),
        np.stack(beyond),
    )


def split(value):
    high = value.astype(BF16)
    low = (value - high.astype(F32)).astype(BF16)
    return high, low


def dot(a, b):
    return jnp.dot(a, b, preferred_element_type=F32)


def lane_ids(shape):
    return lax.broadcasted_iota(jnp.int32, shape, 1)


def choose(flag, yes, no):
    return jnp.where(flag, yes, no)


def pack_strips(row_value, rows):
    cols = row_value(0).shape[1]
    half = rows * RAD
    source = lax.broadcasted_iota(jnp.int32, (cols, 2 * half), 0)
    lane = lane_ids((cols, 2 * half))
    first = lane < half
    j = lane & (RAD - 1)
    wanted = jnp.where(first, cols - RAD + j, j)
    lane_row = jnp.where(first, lane, lane - half) // RAD
    total = None
    for row in range(rows):
        high, low = split(row_value(row))
        pick = jnp.where((source == wanted) & (lane_row == row), 1.0, 0.0).astype(BF16)
        part = dot(jnp.concatenate([high, low], axis=1), jnp.concatenate([pick, pick], axis=0))
        total = part if total is None else total + part
    return total


def fold_corners(strips, last_ref, first_ref):
    quarter = last_ref.shape[0]
    half, part = LANES // 2, RAD * RAD
    lane = lane_ids((quarter, LANES))
    spare = jnp.zeros((4 * quarter - strips.shape[0], LANES), F32)
    whole = jnp.concatenate([strips, spare], axis=0)
    low = high = jnp.zeros((quarter, LANES), F32)
    for q in range(LANES // (2 * part)):
        piece = whole[q * quarter : (q + 1) * quarter]
        for side in range(2):
            to = q * 2 * part + side * part
            here = (lane >= to) & (lane < to + part)
            low = choose(here, pltpu.roll(piece, (to - side * half) % LANES, 1), low)
            high = choose(here, pltpu.roll(piece, (to - side * half - (half - part)) % LANES, 1), high)
    last_ref[...] = high
    first_ref[...] = low


def unfold_corners(value):
    part = 2 * RAD * RAD
    pieces = [value] + [pltpu.roll(value, LANES - q * part, 1) for q in range(1, LANES // part)]
    return jnp.concatenate(pieces, axis=0)


def is_odd(par_ref, axis):
    return par_ref[axis : axis + 1, :] == 1


def rows_kernel(par_ref, after, factor_ref, field_ref, out_ref, *, even):
    odd = is_odd(par_ref, 0)
    factor = factor_ref[0:1, :]
    rows = field_ref.shape[0]
    for row in range(RAD):
        first, last = field_ref[row], field_ref[rows - 1 - row]
        out_ref[row] = (choose(odd, first, last) if even else choose(odd, last, first)) * factor


def turn_kernel(after, control_ref, field_ref, last_ref, first_ref, flags_ref, *, n_rec, n_tile):
    rec, tile = lax.axis_index("rec"), lax.axis_index("tile")
    flags = [
        rec % 2, rec * 0, rec, jnp.where(tile == 0, 1, 0), jnp.where(tile == n_tile - 1, 1, 0),
        jnp.where(rec == 0, 1, 0), jnp.where(rec == n_rec - 1, 1, 0),
    ]
    line = lax.broadcasted_iota(jnp.int32, flags_ref.shape, 0)
    value = jnp.zeros(flags_ref.shape, jnp.int32)
    for k, flag in enumerate(flags):
        value = jnp.where(line == k, flag.astype(jnp.int32), value)
    flags_ref[...] = value
    rows = control_ref.shape[1]
    for row in range(rows):
        field_ref[row] = control_ref[:, row, :]
    write_strips(field_ref, last_ref, first_ref)


def strip_kernel(after, field_ref, last_ref, first_ref):
    write_strips(field_ref, last_ref, first_ref)


def write_strips(field_ref, last_ref, first_ref):
    strips = pack_strips(lambda r: field_ref[r], field_ref.shape[0])
    fold, half = last_ref.shape[0], LANES // 2
    early, late = strips[0:fold], strips[fold:]
    if late.shape[0] < fold:
        late = jnp.concatenate([late, jnp.zeros((fold - late.shape[0], LANES), F32)], axis=0)
    left = lane_ids(early.shape) < half
    last_ref[...] = jnp.where(left, early, pltpu.roll(late, half, 1))
    first_ref[...] = jnp.where(left, pltpu.roll(early, half, 1), late)


def halo_columns(par_ref, before_ref, after_ref):
    before, after = before_ref[...], after_ref[...]
    half = LANES // 2
    left = lane_ids(before.shape) < half
    early = jnp.where(left, before, pltpu.roll(after, half, 1))
    late = jnp.where(left, pltpu.roll(before, half, 1), after)
    outside = jnp.where(lane_ids((1, LANES)) < half, par_ref[3:4, :], par_ref[4:5, :])
    return jnp.where(outside == 1, 0.0, jnp.concatenate([early, late], axis=0))


def far_corner_kernel(par_ref, after, before_ref, after_ref, last_ref, first_ref):
    fold_corners(halo_columns(par_ref, before_ref, after_ref), last_ref, first_ref)


def prepare_kernel(
    foot_ref, start_ref, row_ref, slot_ref, count_ref, observed_ref, error_ref, out_ref,
    blocks_ref, notes_ref, start_vmem, row_vmem, slot_vmem, count_vmem, observed_vmem, error_vmem, sems, *, per,
):
    owners, lines, _ = foot_ref.shape
    slots = start_ref.shape[0]
    pairs = (
        (start_ref, start_vmem), (row_ref, row_vmem), (slot_ref, slot_vmem), (count_ref, count_vmem),
        (observed_ref, observed_vmem), (error_ref, error_vmem),
    )
    small = [pltpu.make_async_copy(a, b, sems.at[i]) for i, (a, b) in enumerate(pairs)]
    chunk = owners // PARTS
    parts = [slice(i * chunk, (i + 1) * chunk) for i in range(PARTS)]
    loads = [
        pltpu.make_async_copy(foot_ref.at[here], blocks_ref.at[here], sems.at[6 + i])
        for i, here in enumerate(parts)
    ]
    for copy in small + loads:
        copy.start()
    stores = []
    for i, here in enumerate(parts):
        loads[i].wait()
        to = out_ref.at[here, 0:lines, :]
        stores.append(pltpu.make_async_copy(blocks_ref.at[here], to, sems.at[6 + PARTS + i]))
        stores[-1].start()
    for copy in small:
        copy.wait()
    start = start_vmem[...]
    valid = lax.broadcasted_iota(jnp.int32, start.shape, 0) < count_vmem[...]
    lanes = jnp.concatenate(
        [start >> 4, start & 15, row_vmem[...], jnp.where(valid, slot_vmem[...], per)], axis=0
    ).astype(F32)
    wide = jnp.pad(lanes, ((0, LANES - 4 * slots), (0, LANES - owners)))
    turned = jnp.transpose(wide)[0:owners]
    spare = [jnp.zeros((1, LANES - 2 * per), F32)] if 2 * per < LANES else []
    own = jnp.concatenate([observed_vmem[...], error_vmem[...]] + spare, axis=1)
    line = lax.broadcasted_iota(jnp.int32, notes_ref.shape, 1)
    value = jnp.broadcast_to(turned[:, None, :], notes_ref.shape)
    for k in range(3):
        term = own.astype(BF16).astype(F32)
        own = own - term
        value = jnp.where(line == 1 + k, term[None], value)
    notes_ref[...] = value.astype(BF16)
    stores.append(pltpu.make_async_copy(notes_ref, out_ref.at[:, lines : lines + SUB, :], sems.at[6 + 2 * PARTS]))
    stores[-1].start()
    for copy in stores:
        copy.wait()


def halo_parts(value):
    high, low = split(value)
    lanes = [high, low] + ([high] if value.shape[1] < LANES else [])
    return jnp.concatenate(lanes, axis=1)


def halo_sums(both, weights_ref, first, width):
    used = both.shape[1]
    out = dot(both, weights_ref[0:used, first : first + width])
    if used < weights_ref.shape[0]:
        out = out + dot(both[:, : used // 2], weights_ref[used:, first : first + width])
    return out


def column_sums(value, col_both):
    cols = value.shape[1]
    high, low = split(value)
    out = dot(jnp.concatenate([high, low], axis=1), col_both)
    return out[:, :cols] + out[:, cols:]


def time_sums(value, time_high, time_low):
    high, low = split(value)
    return dot(time_high, high) + dot(time_high, low) + dot(time_low, high)


def row_sums(get, row, low, high, taps):
    total = None
    for distance in range(RAD + 1):
        here = [get(r) for r in sorted({row - distance, row + distance}) if low <= r < high]
        if not here:
            continue
        part = here[0] if len(here) == 1 else here[0] + here[1]
        part = float(taps[RAD + distance]) * part
        total = part if total is None else total + part
    return total


def local_kernel(after, field_ref, time_high, time_low, col_both, out_ref):
    rows, hours, cols = field_ref.shape
    taps = space_taps()
    for row in range(0, rows, 2):
        pair = [
            column_sums(row_sums(lambda i: field_ref[i], r, 0, rows, taps), col_both[...])
            for r in (row, row + 1)
        ]
        both = time_sums(jnp.concatenate(pair, axis=1), time_high[...], time_low[...])
        for k, r in enumerate((row, row + 1)):
            out_ref[r] = both[:, k * cols : (k + 1) * cols]


def strip_halo(par_ref, before_ref, after_ref, time_high, time_low):
    halo = halo_columns(par_ref, before_ref, after_ref)[0 : time_high.shape[0]]
    return halo_parts(time_sums(halo, time_high[...], time_low[...]))


def strips_kernel(
    par_ref, local_ref, before_ref, after_ref, time_high, time_low, own_ref, out_ref, *, by_hour
):
    rows, hours, cols = local_ref.shape
    halo = strip_halo(par_ref, before_ref, after_ref, time_high, time_low)
    for row in range(0, rows, 2):
        both = halo_sums(halo, own_ref, row * cols, 2 * cols)
        for k, r in enumerate((row, row + 1)):
            value = local_ref[r] + both[:, k * cols : (k + 1) * cols]
            if by_hour:
                out_ref[:, r, :] = value
            else:
                out_ref[r] = value


def beyond_sums(rows, corner, corner_weights, consts):
    time_high, time_low, col_both = consts
    cols = col_both.shape[1] // 2
    taps = space_taps()
    parts = []
    for k in range(0, RAD, 2):
        pair = []
        for i in (k, k + 1):
            summed = None
            for j in range(RAD - i):
                part = float(taps[RAD + i + j + 1]) * rows(j)
                summed = part if summed is None else summed + part
            pair.append(column_sums(summed, col_both[...]))
        value = jnp.concatenate(pair, axis=1) + halo_sums(corner, corner_weights, k * cols, 2 * cols)
        both = time_sums(value, time_high[...], time_low[...])
        parts += [both[:, :cols], both[:, cols:]]
    return parts


def edge_parts(halo, corner, corner_weights, consts):
    corner = halo_parts(unfold_corners(corner)[0 : halo.shape[1], 0 : corner_weights.shape[0] // 3])
    return beyond_sums(lambda j: halo[j], corner, corner_weights, consts)


def beyond_kernel(
    par_ref, field_ref, before_ref, after_ref, time_high, time_low, col_both, beyond_ref, out_even, out_odd,
):
    rows, hours, _ = field_ref.shape
    odd = is_odd(par_ref, 0)
    halo = halo_parts(halo_columns(par_ref, before_ref, after_ref)[0:hours])
    consts = (time_high, time_low, col_both)
    to_after = beyond_sums(lambda j: field_ref[rows - 1 - j], halo, beyond_ref.at[0], consts)
    to_before = beyond_sums(lambda j: field_ref[j], halo, beyond_ref.at[1], consts)
    for k in range(RAD):
        out_even[k] = choose(odd, to_before[k], to_after[k]).astype(BF16)
        out_odd[k] = choose(odd, to_after[k], to_before[k]).astype(BF16)


def flux_kernel(par_ref, local_ref, prior_ref, scale_ref, got_ref, flux_ref, scale_out, wide):
    rows = local_ref.shape[0]
    odd = par_ref[0, 0]
    wide[...] = scale_ref[...].astype(F32)
    for row in range(rows):
        scale_out[row] = wide[:, row, :]
    wide[...] = prior_ref[...].astype(F32)
    for row in range(rows):
        flux_ref[row] = wide[:, row, :] + scale_out[row] * local_ref[row]
    for k in range(RAD):
        row = jnp.where(odd == 1, k, rows - 1 - k)
        flux_ref[row] = flux_ref[row] + scale_out[row] * got_ref[k].astype(F32)


def finish_kernel(
    par_ref, model_ref, local_ref, factor_ref, got_e, got_o, corner_before, corner_after,
    time_high, time_low, col_both, corner_weights,
    model_out, out_ref, halo, edges, total, model_own, sems,
):
    hours, rows, cols = local_ref.shape
    half = rows // 2
    odd = is_odd(par_ref, 0)
    factor = factor_ref[1:2, :]
    consts = (time_high, time_low, col_both)
    model_own[...] = model_ref[:, 0 : model_own.shape[1]]
    copies = [pltpu.make_async_copy(model_own, model_out, sems.at[2 * PIECES])]
    copies[0].start()
    inside = lax.broadcasted_iota(jnp.int32, (hours // PIECES, half, cols), 1)
    for side in range(2):
        before = side == 0
        for k in range(RAD):
            even, other = got_e[k], got_o[k]
            halo[k] = (choose(odd, even, other) if before else choose(odd, other, even)) * factor
        corner = corner_before[...] if before else corner_after[...]
        corner = jnp.where(par_ref[5 + side : 6 + side, :] == 1, 0.0, corner)
        parts = edge_parts(halo, corner, corner_weights.at[1 - side], consts)
        for k, part in enumerate(parts):
            edges[:, k if before else half - 1 - k, :] = part
        here = slice(0, half) if before else slice(rows - half, rows)
        for piece in range(PIECES):
            span = slice(piece * hours // PIECES, (piece + 1) * hours // PIECES)
            mine = inside < RAD if before else inside >= half - RAD
            total[span, here, :] = local_ref[span, here, :] + jnp.where(mine, edges[span], 0.0)
            copy = pltpu.make_async_copy(
                total.at[span, here, :], out_ref.at[span, here, :], sems.at[side * PIECES + piece]
            )
            copy.start()
            copies.append(copy)
    for copy in copies:
        copy.wait()


def blocks_of(foot_ref, source, heights, slots):
    for c in range(0, slots, 2):
        both = foot_ref[source, c * heights : (c + 2) * heights, :].astype(F32)
        yield c, both[0:heights]
        yield c + 1, both[heights : 2 * heights]


def load_kernel(
    par_ref, foot_ref, scale_far, *refs, shift, slots, heights, tiles, per, empty
):
    count = (len(refs) - 4) // 2
    distant, near = refs[:count], refs[count + 3 : -1]
    table_ref, seen_ref, scale_ref = refs[count : count + 3]
    sems = refs[-1]
    flux_far, flux_ref = distant[0], near[0]
    rows = flux_ref.shape[0]
    first = (rows - RAD) * par_ref[0, 0]
    pairs = [(flux_far.at[r : r + RAD], flux_ref.at[r : r + RAD]) for r in range(0, rows, RAD)]
    pairs += list(zip(distant[1:], near[1:])) + [(scale_far.at[pl.ds(first, RAD)], scale_ref)]
    loads = [pltpu.make_async_copy(a, b, sems.at[i]) for i, (a, b) in enumerate(pairs)]
    for load in loads:
        load.start()
    sources = foot_ref.shape[0]
    base = slots * heights
    lane = lane_ids((sources, LANES))
    lines = foot_ref[:, base : base + SUB, :].astype(F32)
    notes = lines[:, 0, :].astype(jnp.int32)
    seen_ref[...] = lines[:, 1, :] + lines[:, 2, :] + lines[:, 3, :]
    start = notes * 16 + pltpu.roll(notes, LANES - slots, 1)
    offset = start + pltpu.roll(notes, LANES - 2 * slots, 1) * (1 << shift)
    source_rec = lax.broadcasted_iota(jnp.int32, (sources, LANES), 0) // tiles
    receptor = jnp.where(notes < per, source_rec * per + notes, empty)
    table_ref[...] = jnp.where(lane < slots, offset, receptor)
    for load in loads:
        load.wait()


def forward_kernel(
    par_ref, foot_ref, table_ref, got_far, flux_in, scale_ref,
    out_ref, flux_ref, got_ref, sums, table_smem, sems, *, shift, slots, heights, tiles, per,
):
    load = pltpu.make_async_copy(got_far, got_ref, sems.at[1])
    load.start()
    odd = par_ref[0, 0]
    sources = foot_ref.shape[0]
    rows = flux_ref.shape[0]
    first = (rows - RAD) * odd
    groups = out_ref.shape[1]
    lane = lane_ids((sources, LANES))
    table = table_ref[...]
    copy = pltpu.make_async_copy(table_ref, table_smem, sems.at[0])
    copy.start()
    load.wait()
    for k in range(RAD):
        line = jnp.where(odd == 1, RAD - 1 - k, k)
        flux_ref[first + line] = flux_in[first + line] + scale_ref[line] * got_ref[k].astype(F32)
    copy.wait()

    def body(source, carry):
        for c, block in blocks_of(foot_ref, source, heights, slots):
            offset = table_smem[source, c]
            row = lax.shift_right_logical(offset, shift)
            begin = jnp.bitwise_and(offset, (1 << shift) - 1)
            product = flux_ref[row, pl.ds(begin, heights), :] * block
            sums[c, pl.ds(source, 1), :] = jnp.sum(product, axis=0, keepdims=True)
        return carry

    lax.fori_loop(0, sources, body, 0)
    totals = [jnp.zeros((sources, LANES), F32) for _ in range(groups)]
    for c in range(slots):
        value = jnp.sum(sums[c], axis=1, keepdims=True)
        which = table[:, 3 * slots + c : 3 * slots + c + 1]
        for q in range(groups):
            totals[q] = totals[q] + jnp.where(which == lane + q * LANES, value, 0.0)
    for q in range(groups):
        total = jnp.sum(totals[q], axis=0, keepdims=True)
        out_ref[:, q : q + 1, :] = jnp.broadcast_to(total[None], (sources, 1, LANES))


def adjoint_kernel(
    par_ref, table_vmem, seen_ref, got_ref, foot_ref, scale_ref,
    model_ref, factor_ref, field_ref, rows_even, last_ref, first_ref,
    weight_rows, table_ref, sem, *, shift, slots, heights, tiles, per,
):
    load = pltpu.make_async_copy(table_vmem, table_ref, sem)
    load.start()
    sources = foot_ref.shape[0]
    groups = got_ref.shape[1]
    rows, hours, _ = field_ref.shape
    model = jnp.sum(got_ref[:, 0:groups, :], axis=0)
    packed = LANES // per
    lane = lane_ids((1, LANES))
    own = jnp.zeros((1, LANES), F32)
    for q in range(groups):
        for k in range(packed):
            line = model[q : q + 1, :]
            line = line if k == 0 else pltpu.roll(line, LANES - k * per, 1)
            own = choose(par_ref[2:3, :] == q * packed + k, line, own)
    model_ref[...] = own
    weights = []
    for q in range(groups):
        observed, error = jnp.zeros((1, LANES), F32), jnp.ones((1, LANES), F32)
        for k in range(packed):
            source = (q * packed + k) * tiles
            line = seen_ref[source : source + 1, :]
            here = (lane >= k * per) & (lane < (k + 1) * per)
            observed = jnp.where(here, line if k == 0 else pltpu.roll(line, k * per, 1), observed)
            turn = (k * per - per) % LANES
            error = jnp.where(here, line if turn == 0 else pltpu.roll(line, turn, 1), error)
        weights.append((model[q : q + 1, :] - observed) / (error * error))
    lanes = lane_ids((sources, LANES))
    table = table_vmem[...]
    for c in range(slots):
        which = table[:, 3 * slots + c : 3 * slots + c + 1]
        found = jnp.zeros((sources, LANES), F32)
        for q in range(groups):
            found = jnp.where(which == lanes + q * LANES, weights[q], found)
        weight_rows[c] = jnp.broadcast_to(jnp.sum(found, axis=1, keepdims=True), (sources, LANES))
    field_ref[...] = jnp.zeros_like(field_ref)
    largest = jnp.abs(weights[0])
    for weight in weights[1:]:
        largest = jnp.maximum(largest, jnp.abs(weight))
    top = jnp.max(largest, keepdims=True) * (FOOT_MAX * SCALE_MAX * sources * slots)
    top = jnp.maximum(top, 1e-25)
    factor_ref[0:1, :] = jnp.broadcast_to(HALF_TOP / top, (1, LANES))
    factor_ref[1:2, :] = jnp.broadcast_to(top * (1.0 / HALF_TOP), (1, LANES))
    load.wait()

    def body(source, carry):
        for c, block in blocks_of(foot_ref, source, heights, slots):
            offset = table_ref[source, c]
            row = lax.shift_right_logical(offset, shift)
            begin = jnp.bitwise_and(offset, (1 << shift) - 1)
            weight = weight_rows[c, pl.ds(source, 1), :]
            field_ref[row, pl.ds(begin, heights), :] += block * weight
        return carry

    lax.fori_loop(0, sources, body, 0)
    for row in range(rows):
        field_ref[row] = field_ref[row] * scale_ref[row]
    rows_kernel(par_ref, None, factor_ref, field_ref, rows_even, even=True)
    write_strips(field_ref, last_ref, first_ref)


def swap_pairs(count, odd):
    pairs = []
    for i in range(1 if odd else 0, count - 1, 2):
        pairs += [(i, i + 1), (i + 1, i)]
    return pairs


def swap(axis, even, odd):
    count = lax.axis_size(axis)
    return (
        lax.ppermute(even, axis, swap_pairs(count, False)),
        lax.ppermute(odd, axis, swap_pairs(count, True)),
    )


VM = pl.BlockSpec(memory_space=pltpu.VMEM)
HB = pl.BlockSpec(memory_space=pltpu.HBM)


def call(kernel, out_shape, in_specs, scratch, name, out_specs=None, alias=None):
    return pl.pallas_call(
        kernel,
        out_shape=out_shape,
        in_specs=in_specs,
        out_specs=jax.tree.map(lambda _: VM, out_shape) if out_specs is None else out_specs,
        scratch_shapes=scratch,
        input_output_aliases={} if alias is None else alias,
        compiler_params=pltpu.CompilerParams(vmem_limit_bytes=VMEM_LIMIT),
        name=name,
    )


def far(x):
    return pltpu.with_memory_space_constraint(x, pltpu.HBM)


def array(*shape):
    return jax.ShapeDtypeStruct(shape, F32)


def per_device(
    prior_flux,
    flux_scale,
    control,
    footprint,
    slot_count,
    start_hour,
    grid_row,
    receptor_slot,
    observed,
    obs_error,
):
    hours, rows, cols = control.shape
    n_rec, n_tile = lax.axis_size("rec"), lax.axis_size("tile")
    devices = n_rec * n_tile
    slots, heights = footprint.shape[1], footprint.shape[2]
    per = observed.shape[0]
    groups = per * n_rec // LANES
    shift = (hours - 1).bit_length()
    base, own_parts, corner_parts, beyond_parts = constants(hours, rows, cols)
    base = [jnp.asarray(c) for c in base]
    own_parts = jnp.asarray(own_parts)
    corner_parts = jnp.asarray(corner_parts)
    beyond_parts = jnp.asarray(beyond_parts)
    strip = array(-(-hours // (2 * SUB)) * SUB, LANES)
    corner = array(-(-hours // (4 * SUB)) * SUB, LANES)
    block = array(RAD, hours, cols)
    field_shape = array(rows, hours, cols)
    row_scratch = pltpu.VMEM((RAD, hours, cols), F32)

    def pass_on(axis, last, first):
        count = lax.axis_size(axis)
        onward = [(i, (i + 1) % count) for i in range(count)]
        back = [(j, i) for i, j in onward]
        return lax.ppermute(last, axis, onward), lax.ppermute(first, axis, back)

    def swaps(after, field, got_strips, name):
        local = call(local_kernel, field_shape, [VM] * 5, [], name + "_local")(after, field, *base)
        corners = call(far_corner_kernel, [corner, corner], [VM] * 4, [], name + "_corners")(par, local, *got_strips)
        return local, pass_on("rec", *corners)

    def strip_sums(local, got_strips, by_hour, name):
        def kernel(*refs):
            strips_kernel(*refs, by_hour=by_hour)

        shape = array(hours, rows, cols) if by_hour else field_shape
        return call(kernel, shape, [VM] * 7, [], name)(par, local, *got_strips, *base[:2], own_parts)

    def swap_rows(even, after, factor, field, name):
        def kernel(*refs):
            rows_kernel(*refs, even=even)

        sent = call(kernel, block, [VM] * 4, [], name)(par, after, factor, field)
        return sent, lax.ppermute(sent.astype(F16), "rec", swap_pairs(n_rec, not even))

    def prepare(*refs):
        prepare_kernel(*refs, per=per)

    numbers = pltpu.VMEM((slots, devices), jnp.int32)
    lines = slots * heights + SUB
    sent = call(
        prepare,
        jax.ShapeDtypeStruct((devices, lines, cols), BF16),
        [HB] * 7,
        [
            pltpu.VMEM((devices, slots * heights, cols), BF16),
            pltpu.VMEM((devices, SUB, LANES), BF16),
            numbers, numbers, numbers, pltpu.VMEM((1, devices), jnp.int32),
            pltpu.VMEM((1, per), F32), pltpu.VMEM((1, per), F32),
            pltpu.SemaphoreType.DMA((7 + 2 * PARTS,)),
        ],
        "prepare_blocks",
        out_specs=HB,
    )(*[
        far(x)
        for x in (
            footprint.reshape(devices, slots * heights, cols),
            start_hour.T, grid_row.T, receptor_slot.T, slot_count[None], observed[None], obs_error[None],
        )
    ])
    foot = lax.all_to_all(sent, AXES, split_axis=0, concat_axis=0, tiled=True)
    def turn(*refs):
        turn_kernel(*refs, n_rec=n_rec, n_tile=n_tile)

    field, *strips, par = call(
        turn,
        [field_shape, strip, strip, jax.ShapeDtypeStruct((SUB, LANES), jnp.int32)],
        [HB, VM],
        [],
        "turn_control",
    )(sent, control)
    got_strips = pass_on("tile", *strips)
    local = call(local_kernel, field_shape, [VM] * 5, [], "control_local")(strips[0], field, *base)
    small = jax.ShapeDtypeStruct((RAD, hours, cols), BF16)
    sent_even, sent_odd = call(beyond_kernel, [small, small], [VM] * 8, [], "control_beyond")(
        par, field, *got_strips, *base, beyond_parts
    )
    got_even, got_odd = swap("rec", sent_even, sent_odd)
    local = strip_sums(local, got_strips, False, "control_strips")
    flux, scale = call(
        flux_kernel, [field_shape, field_shape], [VM] * 5, [pltpu.VMEM((hours, rows, cols), F32)], "flux_field"
    )(par, local, prior_flux, flux_scale, got_even)

    sizes = dict(shift=shift, slots=slots, heights=heights, tiles=n_tile, per=per)

    def forward(*refs):
        forward_kernel(*refs, **sizes)


    def load(*refs):
        load_kernel(*refs, empty=groups * LANES, **sizes)

    table, seen, scale_near, flux_near = call(
        load,
        [jax.ShapeDtypeStruct((devices, LANES), jnp.int32), array(devices, LANES), block, field_shape],
        [VM, VM, HB, HB],
        [pltpu.SemaphoreType.DMA((1 + rows // RAD,))],
        "load_flux",
    )(par, foot, far(scale), far(flux))
    table, got_odd = lax.optimization_barrier((table, got_odd))
    partial, _ = call(
        forward,
        [array(devices, groups, LANES), field_shape],
        [VM] * 3 + [HB] + [VM] * 2,
        [
            pltpu.VMEM((RAD, hours, cols), BF16),
            pltpu.VMEM((slots, devices, LANES), F32),
            pltpu.SMEM((devices, LANES), jnp.int32),
            pltpu.SemaphoreType.DMA((2,)),
        ],
        "block_values",
        alias={4: 1},
    )(par, foot, table, far(got_odd), flux_near, scale_near)
    everyone = lax.all_to_all(partial, AXES, split_axis=0, concat_axis=0, tiled=True)

    def adjoint(*refs):
        adjoint_kernel(*refs, **sizes)

    model, factor, field, sent_even, *strips = call(
        adjoint,
        [array(1, LANES), array(2, LANES), field_shape, block, strip, strip],
        [VM] * 6,
        [
            pltpu.VMEM((slots, devices, LANES), F32),
            pltpu.SMEM((devices, LANES), jnp.int32),
            pltpu.SemaphoreType.DMA,
        ],
        "adjoint_field",
    )(par, table, seen, everyone, foot, scale)
    got_even = lax.ppermute(sent_even.astype(F16), "rec", swap_pairs(n_rec, False))
    got_strips = pass_on("tile", *strips)
    sent_odd, got_odd = swap_rows(False, strips[0], factor, field, "gradient_odd")
    local, got_corners = swaps(sent_odd, field, got_strips, "gradient")
    local = strip_sums(local, got_strips, True, "gradient_strips")
    model_co2, gradient = call(
        finish_kernel,
        [array(1, per), array(hours, rows, cols)],
        [VM] * 12,
        [
            row_scratch,
            pltpu.VMEM((hours, rows // 2, cols), F32),
            pltpu.VMEM((hours, rows, cols), F32),
            pltpu.VMEM((1, per), F32),
            pltpu.SemaphoreType.DMA((2 * PIECES + 1,)),
        ],
        "gradient",
        out_specs=[HB, HB],
    )(par, model, local, factor, got_even.astype(F32), got_odd.astype(F32), *got_corners, *base, corner_parts)
    return (model_co2.reshape(-1), gradient)


def solution(mesh):
    return jax.shard_map(
        per_device,
        mesh=mesh,
        in_specs=(
            P(None, "rec", "tile"),
            P(None, "rec", "tile"),
            P(None, "rec", "tile"),
            P(("rec", "tile"), None, None, None),
            P(("rec", "tile")),
            P(("rec", "tile"), None),
            P(("rec", "tile"), None),
            P(("rec", "tile"), None),
            P("rec"),
            P("rec"),
        ),
        out_specs=(P("rec"), P(None, "rec", "tile")),
        check_vma=False,
    )
```

```python
import numpy as np
import jax
import jax.numpy as jnp
from jax import lax
from jax.experimental import pallas as pl
from jax.experimental.pallas import tpu as pltpu
from jax.sharding import PartitionSpec as P

RAD = 4
TAPS = 12
AXES = ("rec", "tile")
LANES = 128
SUB = 8
FOOT_MAX = 0.02
PARTS = 4
PIECES = 3
SCALE_MAX = 2.0
HALF_TOP = 32768.0
F16 = jnp.float16
VMEM_LIMIT = 14 * 1024 * 1024
F32 = jnp.float32
BF16 = jnp.bfloat16


def space_taps():
    offsets = np.arange(-RAD, RAD + 1).astype(np.float64)
    values = np.exp(-2.0 * offsets * offsets / (RAD * RAD))
    return values / np.sqrt(np.sum(values * values))


def time_taps():
    offsets = np.arange(-TAPS, TAPS + 1).astype(np.float64)
    values = np.exp(-2.0 * np.abs(offsets) / TAPS)
    return values / np.sqrt(np.sum(values * values))


def banded(distance, taps, reach):
    inside = np.abs(distance) <= reach
    return np.where(inside, taps[np.clip(distance, -reach, reach) + reach], 0.0)


def two_parts(matrix):
    high = matrix.astype(np.float32).astype(jnp.bfloat16)
    low = (matrix - high.astype(np.float64)).astype(np.float32).astype(jnp.bfloat16)
    return high, low


def constants(hours, rows, cols):
    space = space_taps()
    hour = np.arange(hours)
    time_high, time_low = two_parts(banded(hour[:, None] - hour[None, :], time_taps(), TAPS))
    col = np.arange(cols)
    col_high, col_low = two_parts(banded(col[:, None] - col[None, :], space, RAD))
    col_both = np.block([[col_high, col_low], [col_high, np.zeros_like(col_high)]])
    halo_col = np.concatenate([np.arange(-RAD, 0), np.arange(cols, cols + RAD)])
    edge = banded(halo_col[:, None] - col[None, :], space, RAD)

    def strips(row_of, halo_of, targets):
        by_row = banded(np.array(row_of)[:, None] - np.array(targets)[None, :], space, RAD)
        both = by_row[:, :, None] * edge[np.array(halo_of)][:, None, :]
        high, low = two_parts(both.reshape(len(row_of), -1))
        return np.concatenate([high, high, low], axis=0)

    own = [(row, side * RAD + j) for side in range(2) for row in range(rows) for j in range(RAD)]
    corner = []
    for first, targets in ((rows, rows - 1 - np.arange(RAD)), (-RAD, np.arange(RAD))):
        lanes = [
            (row, side * RAD + j) for side in range(2) for row in range(first, first + RAD) for j in range(RAD)
        ]
        corner.append(strips(*zip(*lanes), targets))
    beyond = [strips(*zip(*own), rows + np.arange(RAD)), strips(*zip(*own), -1 - np.arange(RAD))]
    return (
        (time_high, time_low, col_both),
        strips(*zip(*own), np.arange(rows)),
        np.stack(corner),
        np.stack(beyond),
    )


def split(value):
    high = value.astype(BF16)
    low = (value - high.astype(F32)).astype(BF16)
    return high, low


def dot(a, b):
    return jnp.dot(a, b, preferred_element_type=F32)


def lane_ids(shape):
    return lax.broadcasted_iota(jnp.int32, shape, 1)


def choose(flag, yes, no):
    return jnp.where(flag, yes, no)


def pack_strips(row_value, rows):
    cols = row_value(0).shape[1]
    half = rows * RAD
    source = lax.broadcasted_iota(jnp.int32, (cols, 2 * half), 0)
    lane = lane_ids((cols, 2 * half))
    first = lane < half
    j = lane & (RAD - 1)
    wanted = jnp.where(first, cols - RAD + j, j)
    lane_row = jnp.where(first, lane, lane - half) // RAD
    total = None
    for row in range(rows):
        high, low = split(row_value(row))
        pick = jnp.where((source == wanted) & (lane_row == row), 1.0, 0.0).astype(BF16)
        part = dot(jnp.concatenate([high, low], axis=1), jnp.concatenate([pick, pick], axis=0))
        total = part if total is None else total + part
    return total


def fold_corners(strips, last_ref, first_ref):
    quarter = last_ref.shape[0]
    half, part = LANES // 2, RAD * RAD
    lane = lane_ids((quarter, LANES))
    spare = jnp.zeros((4 * quarter - strips.shape[0], LANES), F32)
    whole = jnp.concatenate([strips, spare], axis=0)
    low = high = jnp.zeros((quarter, LANES), F32)
    for q in range(LANES // (2 * part)):
        piece = whole[q * quarter : (q + 1) * quarter]
        for side in range(2):
            to = q * 2 * part + side * part
            here = (lane >= to) & (lane < to + part)
            low = choose(here, pltpu.roll(piece, (to - side * half) % LANES, 1), low)
            high = choose(here, pltpu.roll(piece, (to - side * half - (half - part)) % LANES, 1), high)
    last_ref[...] = high
    first_ref[...] = low


def unfold_corners(value):
    part = 2 * RAD * RAD
    pieces = [value] + [pltpu.roll(value, LANES - q * part, 1) for q in range(1, LANES // part)]
    return jnp.concatenate(pieces, axis=0)


def is_odd(par_ref, axis):
    return par_ref[axis : axis + 1, :] == 1


def rows_kernel(par_ref, after, factor_ref, field_ref, out_ref, *, even):
    odd = is_odd(par_ref, 0)
    factor = factor_ref[0:1, :]
    rows = field_ref.shape[0]
    for row in range(RAD):
        first, last = field_ref[row], field_ref[rows - 1 - row]
        out_ref[row] = (choose(odd, first, last) if even else choose(odd, last, first)) * factor


def turn_kernel(after, control_ref, field_ref, last_ref, first_ref, flags_ref, *, n_rec, n_tile):
    rec, tile = lax.axis_index("rec"), lax.axis_index("tile")
    flags = [
        rec % 2, rec * 0, rec, jnp.where(tile == 0, 1, 0), jnp.where(tile == n_tile - 1, 1, 0),
        jnp.where(rec == 0, 1, 0), jnp.where(rec == n_rec - 1, 1, 0),
    ]
    line = lax.broadcasted_iota(jnp.int32, flags_ref.shape, 0)
    value = jnp.zeros(flags_ref.shape, jnp.int32)
    for k, flag in enumerate(flags):
        value = jnp.where(line == k, flag.astype(jnp.int32), value)
    flags_ref[...] = value
    rows = control_ref.shape[1]
    for row in range(rows):
        field_ref[row] = control_ref[:, row, :]
    write_strips(field_ref, last_ref, first_ref)


def strip_kernel(after, field_ref, last_ref, first_ref):
    write_strips(field_ref, last_ref, first_ref)


def write_strips(field_ref, last_ref, first_ref):
    strips = pack_strips(lambda r: field_ref[r], field_ref.shape[0])
    fold, half = last_ref.shape[0], LANES // 2
    early, late = strips[0:fold], strips[fold:]
    if late.shape[0] < fold:
        late = jnp.concatenate([late, jnp.zeros((fold - late.shape[0], LANES), F32)], axis=0)
    left = lane_ids(early.shape) < half
    last_ref[...] = jnp.where(left, early, pltpu.roll(late, half, 1))
    first_ref[...] = jnp.where(left, pltpu.roll(early, half, 1), late)


def halo_columns(par_ref, before_ref, after_ref):
    before, after = before_ref[...], after_ref[...]
    half = LANES // 2
    left = lane_ids(before.shape) < half
    early = jnp.where(left, before, pltpu.roll(after, half, 1))
    late = jnp.where(left, pltpu.roll(before, half, 1), after)
    outside = jnp.where(lane_ids((1, LANES)) < half, par_ref[3:4, :], par_ref[4:5, :])
    return jnp.where(outside == 1, 0.0, jnp.concatenate([early, late], axis=0))


def far_corner_kernel(par_ref, after, before_ref, after_ref, last_ref, first_ref):
    fold_corners(halo_columns(par_ref, before_ref, after_ref), last_ref, first_ref)


def prepare_kernel(
    foot_ref, start_ref, row_ref, slot_ref, count_ref, observed_ref, error_ref, out_ref,
    blocks_ref, notes_ref, start_vmem, row_vmem, slot_vmem, count_vmem, observed_vmem, error_vmem, sems, *, per,
):
    owners, lines, _ = foot_ref.shape
    slots = start_ref.shape[0]
    pairs = (
        (start_ref, start_vmem), (row_ref, row_vmem), (slot_ref, slot_vmem), (count_ref, count_vmem),
        (observed_ref, observed_vmem), (error_ref, error_vmem),
    )
    small = [pltpu.make_async_copy(a, b, sems.at[i]) for i, (a, b) in enumerate(pairs)]
    chunk = owners // PARTS
    parts = [slice(i * chunk, (i + 1) * chunk) for i in range(PARTS)]
    loads = [
        pltpu.make_async_copy(foot_ref.at[here], blocks_ref.at[here], sems.at[6 + i])
        for i, here in enumerate(parts)
    ]
    for copy in small + loads:
        copy.start()
    stores = []
    for i, here in enumerate(parts):
        loads[i].wait()
        to = out_ref.at[here, 0:lines, :]
        stores.append(pltpu.make_async_copy(blocks_ref.at[here], to, sems.at[6 + PARTS + i]))
        stores[-1].start()
    for copy in small:
        copy.wait()
    start = start_vmem[...]
    valid = lax.broadcasted_iota(jnp.int32, start.shape, 0) < count_vmem[...]
    lanes = jnp.concatenate(
        [start >> 4, start & 15, row_vmem[...], jnp.where(valid, slot_vmem[...], per)], axis=0
    ).astype(F32)
    wide = jnp.pad(lanes, ((0, LANES - 4 * slots), (0, LANES - owners)))
    turned = jnp.transpose(wide)[0:owners]
    spare = [jnp.zeros((1, LANES - 2 * per), F32)] if 2 * per < LANES else []
    own = jnp.concatenate([observed_vmem[...], error_vmem[...]] + spare, axis=1)
    line = lax.broadcasted_iota(jnp.int32, notes_ref.shape, 1)
    value = jnp.broadcast_to(turned[:, None, :], notes_ref.shape)
    for k in range(3):
        term = own.astype(BF16).astype(F32)
        own = own - term
        value = jnp.where(line == 1 + k, term[None], value)
    notes_ref[...] = value.astype(BF16)
    stores.append(pltpu.make_async_copy(notes_ref, out_ref.at[:, lines : lines + SUB, :], sems.at[6 + 2 * PARTS]))
    stores[-1].start()
    for copy in stores:
        copy.wait()


def halo_parts(value):
    high, low = split(value)
    lanes = [high, low] + ([high] if value.shape[1] < LANES else [])
    return jnp.concatenate(lanes, axis=1)


def halo_sums(both, weights_ref, first, width):
    used = both.shape[1]
    out = dot(both, weights_ref[0:used, first : first + width])
    if used < weights_ref.shape[0]:
        out = out + dot(both[:, : used // 2], weights_ref[used:, first : first + width])
    return out


def column_sums(value, col_both):
    cols = value.shape[1]
    high, low = split(value)
    out = dot(jnp.concatenate([high, low], axis=1), col_both)
    return out[:, :cols] + out[:, cols:]


def time_sums(value, time_high, time_low):
    high, low = split(value)
    return dot(time_high, high) + dot(time_high, low) + dot(time_low, high)


def row_sums(get, row, low, high, taps):
    total = None
    for distance in range(RAD + 1):
        here = [get(r) for r in sorted({row - distance, row + distance}) if low <= r < high]
        if not here:
            continue
        part = here[0] if len(here) == 1 else here[0] + here[1]
        part = float(taps[RAD + distance]) * part
        total = part if total is None else total + part
    return total


def local_kernel(after, field_ref, time_high, time_low, col_both, out_ref):
    rows, hours, cols = field_ref.shape
    taps = space_taps()
    for row in range(0, rows, 2):
        pair = [
            column_sums(row_sums(lambda i: field_ref[i], r, 0, rows, taps), col_both[...])
            for r in (row, row + 1)
        ]
        both = time_sums(jnp.concatenate(pair, axis=1), time_high[...], time_low[...])
        for k, r in enumerate((row, row + 1)):
            out_ref[r] = both[:, k * cols : (k + 1) * cols]


def strip_halo(par_ref, before_ref, after_ref, time_high, time_low):
    halo = halo_columns(par_ref, before_ref, after_ref)[0 : time_high.shape[0]]
    return halo_parts(time_sums(halo, time_high[...], time_low[...]))


def strips_kernel(
    par_ref, local_ref, before_ref, after_ref, time_high, time_low, own_ref, out_ref, *, by_hour
):
    rows, hours, cols = local_ref.shape
    halo = strip_halo(par_ref, before_ref, after_ref, time_high, time_low)
    for row in range(0, rows, 2):
        both = halo_sums(halo, own_ref, row * cols, 2 * cols)
        for k, r in enumerate((row, row + 1)):
            value = local_ref[r] + both[:, k * cols : (k + 1) * cols]
            if by_hour:
                out_ref[:, r, :] = value
            else:
                out_ref[r] = value


def beyond_sums(rows, corner, corner_weights, consts):
    time_high, time_low, col_both = consts
    cols = col_both.shape[1] // 2
    taps = space_taps()
    parts = []
    for k in range(0, RAD, 2):
        pair = []
        for i in (k, k + 1):
            summed = None
            for j in range(RAD - i):
                part = float(taps[RAD + i + j + 1]) * rows(j)
                summed = part if summed is None else summed + part
            pair.append(column_sums(summed, col_both[...]))
        value = jnp.concatenate(pair, axis=1) + halo_sums(corner, corner_weights, k * cols, 2 * cols)
        both = time_sums(value, time_high[...], time_low[...])
        parts += [both[:, :cols], both[:, cols:]]
    return parts


def edge_parts(halo, corner, corner_weights, consts):
    corner = halo_parts(unfold_corners(corner)[0 : halo.shape[1], 0 : corner_weights.shape[0] // 3])
    return beyond_sums(lambda j: halo[j], corner, corner_weights, consts)


def beyond_kernel(
    par_ref, field_ref, before_ref, after_ref, time_high, time_low, col_both, beyond_ref, out_even, out_odd,
):
    rows, hours, _ = field_ref.shape
    odd = is_odd(par_ref, 0)
    halo = halo_parts(halo_columns(par_ref, before_ref, after_ref)[0:hours])
    consts = (time_high, time_low, col_both)
    to_after = beyond_sums(lambda j: field_ref[rows - 1 - j], halo, beyond_ref.at[0], consts)
    to_before = beyond_sums(lambda j: field_ref[j], halo, beyond_ref.at[1], consts)
    for k in range(RAD):
        out_even[k] = choose(odd, to_before[k], to_after[k]).astype(BF16)
        out_odd[k] = choose(odd, to_after[k], to_before[k]).astype(BF16)


def flux_kernel(par_ref, local_ref, prior_ref, scale_ref, got_ref, flux_ref, scale_out, wide):
    rows = local_ref.shape[0]
    odd = par_ref[0, 0]
    wide[...] = scale_ref[...].astype(F32)
    for row in range(rows):
        scale_out[row] = wide[:, row, :]
    wide[...] = prior_ref[...].astype(F32)
    for row in range(rows):
        flux_ref[row] = wide[:, row, :] + scale_out[row] * local_ref[row]
    for k in range(RAD):
        row = jnp.where(odd == 1, k, rows - 1 - k)
        flux_ref[row] = flux_ref[row] + scale_out[row] * got_ref[k].astype(F32)


def finish_kernel(
    par_ref, model_ref, local_ref, factor_ref, got_e, got_o, corner_before, corner_after,
    time_high, time_low, col_both, corner_weights,
    model_out, out_ref, halo, edges, total, model_own, sems,
):
    hours, rows, cols = local_ref.shape
    half = rows // 2
    odd = is_odd(par_ref, 0)
    factor = factor_ref[1:2, :]
    consts = (time_high, time_low, col_both)
    model_own[...] = model_ref[:, 0 : model_own.shape[1]]
    copies = [pltpu.make_async_copy(model_own, model_out, sems.at[2 * PIECES])]
    copies[0].start()
    inside = lax.broadcasted_iota(jnp.int32, (hours // PIECES, half, cols), 1)
    for side in range(2):
        before = side == 0
        for k in range(RAD):
            even, other = got_e[k], got_o[k]
            halo[side, k] = (choose(odd, even, other) if before else choose(odd, other, even)) * factor
        corner = corner_before[...] if before else corner_after[...]
        corner = jnp.where(par_ref[5 + side : 6 + side, :] == 1, 0.0, corner)
        parts = edge_parts(halo.at[side], corner, corner_weights.at[1 - side], consts)
        for k, part in enumerate(parts):
            edges[side, :, k if before else half - 1 - k, :] = part
        here = slice(0, half) if before else slice(rows - half, rows)
        for piece in range(PIECES):
            span = slice(piece * hours // PIECES, (piece + 1) * hours // PIECES)
            mine = inside < RAD if before else inside >= half - RAD
            total[span, here, :] = local_ref[span, here, :] + jnp.where(mine, edges[side, span], 0.0)
            copy = pltpu.make_async_copy(
                total.at[span, here, :], out_ref.at[span, here, :], sems.at[side * PIECES + piece]
            )
            copy.start()
            copies.append(copy)
    for copy in copies:
        copy.wait()


def blocks_of(foot_ref, source, heights, slots):
    for c in range(0, slots, 2):
        both = foot_ref[source, c * heights : (c + 2) * heights, :].astype(F32)
        yield c, both[0:heights]
        yield c + 1, both[heights : 2 * heights]


def load_kernel(
    par_ref, foot_ref, scale_far, *refs, shift, slots, heights, tiles, per, empty
):
    count = (len(refs) - 4) // 2
    distant, near = refs[:count], refs[count + 3 : -1]
    table_ref, seen_ref, scale_ref = refs[count : count + 3]
    sems = refs[-1]
    flux_far, flux_ref = distant[0], near[0]
    rows = flux_ref.shape[0]
    first = (rows - RAD) * par_ref[0, 0]
    pairs = [(flux_far.at[r : r + RAD], flux_ref.at[r : r + RAD]) for r in range(0, rows, RAD)]
    pairs += list(zip(distant[1:], near[1:])) + [(scale_far.at[pl.ds(first, RAD)], scale_ref)]
    loads = [pltpu.make_async_copy(a, b, sems.at[i]) for i, (a, b) in enumerate(pairs)]
    for load in loads:
        load.start()
    sources = foot_ref.shape[0]
    base = slots * heights
    lane = lane_ids((sources, LANES))
    lines = foot_ref[:, base : base + SUB, :].astype(F32)
    notes = lines[:, 0, :].astype(jnp.int32)
    seen_ref[...] = lines[:, 1, :] + lines[:, 2, :] + lines[:, 3, :]
    start = notes * 16 + pltpu.roll(notes, LANES - slots, 1)
    offset = start + pltpu.roll(notes, LANES - 2 * slots, 1) * (1 << shift)
    source_rec = lax.broadcasted_iota(jnp.int32, (sources, LANES), 0) // tiles
    receptor = jnp.where(notes < per, source_rec * per + notes, empty)
    table_ref[...] = jnp.where(lane < slots, offset, receptor)
    for load in loads:
        load.wait()


def forward_kernel(
    par_ref, foot_ref, table_ref, got_far, flux_in, scale_ref,
    out_ref, flux_ref, got_ref, sums, table_smem, sems, *, shift, slots, heights, tiles, per,
):
    load = pltpu.make_async_copy(got_far, got_ref, sems.at[1])
    load.start()
    odd = par_ref[0, 0]
    sources = foot_ref.shape[0]
    rows = flux_ref.shape[0]
    first = (rows - RAD) * odd
    groups = out_ref.shape[1]
    lane = lane_ids((sources, LANES))
    table = table_ref[...]
    copy = pltpu.make_async_copy(table_ref, table_smem, sems.at[0])
    copy.start()
    load.wait()
    for k in range(RAD):
        line = jnp.where(odd == 1, RAD - 1 - k, k)
        flux_ref[first + line] = flux_in[first + line] + scale_ref[line] * got_ref[k].astype(F32)
    copy.wait()

    def body(source, carry):
        for c, block in blocks_of(foot_ref, source, heights, slots):
            offset = table_smem[source, c]
            row = lax.shift_right_logical(offset, shift)
            begin = jnp.bitwise_and(offset, (1 << shift) - 1)
            product = flux_ref[row, pl.ds(begin, heights), :] * block
            sums[c, pl.ds(source, 1), :] = jnp.sum(product, axis=0, keepdims=True)
        return carry

    lax.fori_loop(0, sources, body, 0)
    totals = [jnp.zeros((sources, LANES), F32) for _ in range(groups)]
    for c in range(slots):
        value = jnp.sum(sums[c], axis=1, keepdims=True)
        which = table[:, 3 * slots + c : 3 * slots + c + 1]
        for q in range(groups):
            totals[q] = totals[q] + jnp.where(which == lane + q * LANES, value, 0.0)
    for q in range(groups):
        total = jnp.sum(totals[q], axis=0, keepdims=True)
        out_ref[:, q : q + 1, :] = jnp.broadcast_to(total[None], (sources, 1, LANES))


def adjoint_kernel(
    par_ref, table_vmem, seen_ref, got_ref, foot_ref, scale_ref,
    model_ref, factor_ref, field_ref, rows_even, last_ref, first_ref,
    weight_rows, table_ref, sem, *, shift, slots, heights, tiles, per,
):
    load = pltpu.make_async_copy(table_vmem, table_ref, sem)
    load.start()
    sources = foot_ref.shape[0]
    groups = got_ref.shape[1]
    rows, hours, _ = field_ref.shape
    model = jnp.sum(got_ref[:, 0:groups, :], axis=0)
    packed = LANES // per
    lane = lane_ids((1, LANES))
    own = jnp.zeros((1, LANES), F32)
    for q in range(groups):
        for k in range(packed):
            line = model[q : q + 1, :]
            line = line if k == 0 else pltpu.roll(line, LANES - k * per, 1)
            own = choose(par_ref[2:3, :] == q * packed + k, line, own)
    model_ref[...] = own
    weights = []
    for q in range(groups):
        observed, error = jnp.zeros((1, LANES), F32), jnp.ones((1, LANES), F32)
        for k in range(packed):
            source = (q * packed + k) * tiles
            line = seen_ref[source : source + 1, :]
            here = (lane >= k * per) & (lane < (k + 1) * per)
            observed = jnp.where(here, line if k == 0 else pltpu.roll(line, k * per, 1), observed)
            turn = (k * per - per) % LANES
            error = jnp.where(here, line if turn == 0 else pltpu.roll(line, turn, 1), error)
        weights.append((model[q : q + 1, :] - observed) / (error * error))
    lanes = lane_ids((sources, LANES))
    table = table_vmem[...]
    for c in range(slots):
        which = table[:, 3 * slots + c : 3 * slots + c + 1]
        found = jnp.zeros((sources, LANES), F32)
        for q in range(groups):
            found = jnp.where(which == lanes + q * LANES, weights[q], found)
        weight_rows[c] = jnp.broadcast_to(jnp.sum(found, axis=1, keepdims=True), (sources, LANES))
    field_ref[...] = jnp.zeros_like(field_ref)
    largest = jnp.abs(weights[0])
    for weight in weights[1:]:
        largest = jnp.maximum(largest, jnp.abs(weight))
    top = jnp.max(largest, keepdims=True) * (FOOT_MAX * SCALE_MAX * sources * slots)
    top = jnp.maximum(top, 1e-25)
    factor_ref[0:1, :] = jnp.broadcast_to(HALF_TOP / top, (1, LANES))
    factor_ref[1:2, :] = jnp.broadcast_to(top * (1.0 / HALF_TOP), (1, LANES))
    load.wait()

    def body(source, carry):
        for c, block in blocks_of(foot_ref, source, heights, slots):
            offset = table_ref[source, c]
            row = lax.shift_right_logical(offset, shift)
            begin = jnp.bitwise_and(offset, (1 << shift) - 1)
            weight = weight_rows[c, pl.ds(source, 1), :]
            field_ref[row, pl.ds(begin, heights), :] += block * weight
        return carry

    lax.fori_loop(0, sources, body, 0)
    for row in range(rows):
        field_ref[row] = field_ref[row] * scale_ref[row]
    rows_kernel(par_ref, None, factor_ref, field_ref, rows_even, even=True)
    write_strips(field_ref, last_ref, first_ref)


def swap_pairs(count, odd):
    pairs = []
    for i in range(1 if odd else 0, count - 1, 2):
        pairs += [(i, i + 1), (i + 1, i)]
    return pairs


def swap(axis, even, odd):
    count = lax.axis_size(axis)
    return (
        lax.ppermute(even, axis, swap_pairs(count, False)),
        lax.ppermute(odd, axis, swap_pairs(count, True)),
    )


VM = pl.BlockSpec(memory_space=pltpu.VMEM)
HB = pl.BlockSpec(memory_space=pltpu.HBM)


def call(kernel, out_shape, in_specs, scratch, name, out_specs=None, alias=None):
    return pl.pallas_call(
        kernel,
        out_shape=out_shape,
        in_specs=in_specs,
        out_specs=jax.tree.map(lambda _: VM, out_shape) if out_specs is None else out_specs,
        scratch_shapes=scratch,
        input_output_aliases={} if alias is None else alias,
        compiler_params=pltpu.CompilerParams(vmem_limit_bytes=VMEM_LIMIT),
        name=name,
    )


def far(x):
    return pltpu.with_memory_space_constraint(x, pltpu.HBM)


def array(*shape):
    return jax.ShapeDtypeStruct(shape, F32)


def per_device(
    prior_flux,
    flux_scale,
    control,
    footprint,
    slot_count,
    start_hour,
    grid_row,
    receptor_slot,
    observed,
    obs_error,
):
    hours, rows, cols = control.shape
    n_rec, n_tile = lax.axis_size("rec"), lax.axis_size("tile")
    devices = n_rec * n_tile
    slots, heights = footprint.shape[1], footprint.shape[2]
    per = observed.shape[0]
    groups = per * n_rec // LANES
    shift = (hours - 1).bit_length()
    base, own_parts, corner_parts, beyond_parts = constants(hours, rows, cols)
    base = [jnp.asarray(c) for c in base]
    own_parts = jnp.asarray(own_parts)
    corner_parts = jnp.asarray(corner_parts)
    beyond_parts = jnp.asarray(beyond_parts)
    strip = array(-(-hours // (2 * SUB)) * SUB, LANES)
    corner = array(-(-hours // (4 * SUB)) * SUB, LANES)
    block = array(RAD, hours, cols)
    field_shape = array(rows, hours, cols)
    row_scratch = pltpu.VMEM((RAD, hours, cols), F32)

    def pass_on(axis, last, first):
        count = lax.axis_size(axis)
        onward = [(i, (i + 1) % count) for i in range(count)]
        back = [(j, i) for i, j in onward]
        return lax.ppermute(last, axis, onward), lax.ppermute(first, axis, back)

    def swaps(after, field, got_strips, name):
        local = call(local_kernel, field_shape, [VM] * 5, [], name + "_local")(after, field, *base)
        corners = call(far_corner_kernel, [corner, corner], [VM] * 4, [], name + "_corners")(par, local, *got_strips)
        return local, pass_on("rec", *corners)

    def strip_sums(local, got_strips, by_hour, name):
        def kernel(*refs):
            strips_kernel(*refs, by_hour=by_hour)

        shape = array(hours, rows, cols) if by_hour else field_shape
        return call(kernel, shape, [VM] * 7, [], name)(par, local, *got_strips, *base[:2], own_parts)

    def swap_rows(even, after, factor, field, name):
        def kernel(*refs):
            rows_kernel(*refs, even=even)

        sent = call(kernel, block, [VM] * 4, [], name)(par, after, factor, field)
        return sent, lax.ppermute(sent.astype(F16), "rec", swap_pairs(n_rec, not even))

    def prepare(*refs):
        prepare_kernel(*refs, per=per)

    numbers = pltpu.VMEM((slots, devices), jnp.int32)
    lines = slots * heights + SUB
    sent = call(
        prepare,
        jax.ShapeDtypeStruct((devices, lines, cols), BF16),
        [HB] * 7,
        [
            pltpu.VMEM((devices, slots * heights, cols), BF16),
            pltpu.VMEM((devices, SUB, LANES), BF16),
            numbers, numbers, numbers, pltpu.VMEM((1, devices), jnp.int32),
            pltpu.VMEM((1, per), F32), pltpu.VMEM((1, per), F32),
            pltpu.SemaphoreType.DMA((7 + 2 * PARTS,)),
        ],
        "prepare_blocks",
        out_specs=HB,
    )(*[
        far(x)
        for x in (
            footprint.reshape(devices, slots * heights, cols),
            start_hour.T, grid_row.T, receptor_slot.T, slot_count[None], observed[None], obs_error[None],
        )
    ])
    foot = lax.all_to_all(sent, AXES, split_axis=0, concat_axis=0, tiled=True)
    def turn(*refs):
        turn_kernel(*refs, n_rec=n_rec, n_tile=n_tile)

    field, *strips, par = call(
        turn,
        [field_shape, strip, strip, jax.ShapeDtypeStruct((SUB, LANES), jnp.int32)],
        [HB, VM],
        [],
        "turn_control",
    )(sent, control)
    got_strips = pass_on("tile", *strips)
    local = call(local_kernel, field_shape, [VM] * 5, [], "control_local")(strips[0], field, *base)
    small = jax.ShapeDtypeStruct((RAD, hours, cols), BF16)
    sent_even, sent_odd = call(beyond_kernel, [small, small], [VM] * 8, [], "control_beyond")(
        par, field, *got_strips, *base, beyond_parts
    )
    got_even, got_odd = swap("rec", sent_even, sent_odd)
    local = strip_sums(local, got_strips, False, "control_strips")
    flux, scale = call(
        flux_kernel, [field_shape, field_shape], [VM] * 5, [pltpu.VMEM((hours, rows, cols), F32)], "flux_field"
    )(par, local, prior_flux, flux_scale, got_even)

    sizes = dict(shift=shift, slots=slots, heights=heights, tiles=n_tile, per=per)

    def forward(*refs):
        forward_kernel(*refs, **sizes)


    def load(*refs):
        load_kernel(*refs, empty=groups * LANES, **sizes)

    table, seen, scale_near, flux_near = call(
        load,
        [jax.ShapeDtypeStruct((devices, LANES), jnp.int32), array(devices, LANES), block, field_shape],
        [VM, VM, HB, HB],
        [pltpu.SemaphoreType.DMA((1 + rows // RAD,))],
        "load_flux",
    )(par, foot, far(scale), far(flux))
    table, got_odd = lax.optimization_barrier((table, got_odd))
    partial, _ = call(
        forward,
        [array(devices, groups, LANES), field_shape],
        [VM] * 3 + [HB] + [VM] * 2,
        [
            pltpu.VMEM((RAD, hours, cols), BF16),
            pltpu.VMEM((slots, devices, LANES), F32),
            pltpu.SMEM((devices, LANES), jnp.int32),
            pltpu.SemaphoreType.DMA((2,)),
        ],
        "block_values",
        alias={4: 1},
    )(par, foot, table, far(got_odd), flux_near, scale_near)
    everyone = lax.all_to_all(partial, AXES, split_axis=0, concat_axis=0, tiled=True)

    def adjoint(*refs):
        adjoint_kernel(*refs, **sizes)

    model, factor, field, sent_even, *strips = call(
        adjoint,
        [array(1, LANES), array(2, LANES), field_shape, block, strip, strip],
        [VM] * 6,
        [
            pltpu.VMEM((slots, devices, LANES), F32),
            pltpu.SMEM((devices, LANES), jnp.int32),
            pltpu.SemaphoreType.DMA,
        ],
        "adjoint_field",
    )(par, table, seen, everyone, foot, scale)
    got_even = lax.ppermute(sent_even.astype(F16), "rec", swap_pairs(n_rec, False))
    got_strips = pass_on("tile", *strips)
    sent_odd, got_odd = swap_rows(False, strips[0], factor, field, "gradient_odd")
    local, got_corners = swaps(sent_odd, field, got_strips, "gradient")
    local = strip_sums(local, got_strips, True, "gradient_strips")
    model_co2, gradient = call(
        finish_kernel,
        [array(1, per), array(hours, rows, cols)],
        [VM] * 12,
        [
            pltpu.VMEM((2, RAD, hours, cols), F32),
            pltpu.VMEM((2, hours, rows // 2, cols), F32),
            pltpu.VMEM((hours, rows, cols), F32),
            pltpu.VMEM((1, per), F32),
            pltpu.SemaphoreType.DMA((2 * PIECES + 1,)),
        ],
        "gradient",
        out_specs=[HB, HB],
    )(par, model, local, factor, got_even.astype(F32), got_odd.astype(F32), *got_corners, *base, corner_parts)
    return (model_co2.reshape(-1), gradient)


def solution(mesh):
    return jax.shard_map(
        per_device,
        mesh=mesh,
        in_specs=(
            P(None, "rec", "tile"),
            P(None, "rec", "tile"),
            P(None, "rec", "tile"),
            P(("rec", "tile"), None, None, None),
            P(("rec", "tile")),
            P(("rec", "tile"), None),
            P(("rec", "tile"), None),
            P(("rec", "tile"), None),
            P("rec"),
            P("rec"),
        ),
        out_specs=(P("rec"), P(None, "rec", "tile")),
        check_vma=False,
    )
```
